256 devices in a mesh: user: 32 (over y, z), hist: 8 (over x, core).
Axes of the slice: x: 4, y: 4, z: 8, core: 2. Of those that a mesh axis runs over, the one named last changes fastest.
Arguments:
- quot_ids: int32 [64, 2048], P('user', 'hist'), may hold values from 0 to 2047
- rem_ids: int32 [64, 2048], P('user', 'hist'), may hold values from 0 to 65535, as said below
- lengths: int32 [64], P('user'), may hold values from 426 to 2048, as said below
- log_decay: float32 [64, 4, 2048], P('user', None, 'hist'), may hold values from -1.1 to 0
- quot_table: bfloat16 [2048, 256], replicated, may hold values from -6 to 6
- rem_table: bfloat16 [65536, 256], P('user'), may hold values from -6 to 6
- w_query: bfloat16 [256, 256], replicated, may hold values from -0.375 to 0.375
- w_key: bfloat16 [256, 256], replicated, may hold values from -0.375 to 0.375
- w_value: bfloat16 [256, 256], replicated, may hold values from -0.375 to 0.375
- w_out: bfloat16 [256, 256], replicated, may hold values from -0.375 to 0.375
- cotangent: bfloat16 [64, 2048, 256], P('user', 'hist'), may hold values from -0.59765625 to 0.59765625
Outputs:
- output: bfloat16 [64, 2048, 256], P('user', 'hist')
- quot_grad: float32 [2048, 256], replicated
- rem_grad: float32 [65536, 256], P('user')
The draws below stay inside these ranges and needn't reach their ends.
Inputs may be any that keep to these rules, and one draw needn't show every extreme that they name: rem_ids[u, t] // 2048 names a shard of the remainder table. In each aligned block of 256 events of one user (events b * 256 to (b + 1) * 256 - 1), no shard is named by more than 16 events, and one shard, the same for all blocks, is named by exactly 16. The valid events of user u are its first lengths[u] ones.
All inputs are finite; a program needn't handle non-finite values.
Results may differ from the reference program's by a relative error of at most 0.0073.
Values may be sent and summed in bfloat16 or wider, within the bound.
No kernel may reach another device: no remote copies, remote signals or barrier semaphores. Data moves between devices by JAX's collectives and lax.ppermute only.
A program may use at most 192 MiB of HBM per device.

```python
import math
import jax
import jax.numpy as jnp
import numpy as np
from jax import lax

D = 256
HEADS = 4
HEAD = 64
QROWS = 2048
RROW_DEV = 2048
L_DEV = 256
CUSTOMER_COUNT = 64
PAST_ACTIONS = 2048
SHARDS = 32
REM = 65536
MOST = 16


def draw_rem_ids(key, part):
    base_key = jax.random.fold_in(key, 7)
    key_crowd, key_blocks, key_offsets = jax.random.split(base_key, 3)
    block_total = CUSTOMER_COUNT * (PAST_ACTIONS // L_DEV)
    crowded = jax.random.randint(key_crowd, (), 0, SHARDS)
    remaining = L_DEV - MOST
    repeats = (remaining + SHARDS - 2) // (SHARDS - 1)
    pattern = jnp.arange((SHARDS - 1) * repeats, dtype=jnp.int32) // repeats

    def one_block(block_key):
        key_order, key_mix = jax.random.split(block_key)
        others = jax.random.permutation(key_order, pattern)[:remaining]
        owners = jnp.concatenate([jnp.zeros((MOST,), jnp.int32), 1 + others])
        owners = (owners + crowded) % SHARDS
        return jax.random.permutation(key_mix, owners)
    owners = jax.vmap(one_block)(jax.random.split(key_blocks, block_total))
    offsets = jax.random.randint(key_offsets, (block_total, L_DEV), 0, RROW_DEV)
    return (owners * RROW_DEV + offsets).astype(jnp.int32).reshape(CUSTOMER_COUNT, PAST_ACTIONS)


def draw_lengths(key, part):
    base_key = jax.random.fold_in(key, 13)
    ranks = jnp.arange(CUSTOMER_COUNT, dtype=jnp.int32)
    rising = PAST_ACTIONS // 3 + 2 * PAST_ACTIONS // 3 * ranks // max(CUSTOMER_COUNT - 1, 1)
    stochastic_jitter = jax.random.randint(base_key, (CUSTOMER_COUNT,), 0, PAST_ACTIONS // 8 + 1)
    result = jnp.clip(rising - stochastic_jitter, 1, PAST_ACTIONS)
    return jnp.where(ranks == CUSTOMER_COUNT - 1, PAST_ACTIONS, result).astype(jnp.int32)


def draw_log_decay(key, part):
    base_key = jax.random.fold_in(key, 29)
    lookup_series = jax.random.split(base_key, 7)

    def head_order(one_key):
        return jax.random.permutation(one_key, HEADS)
    order = jax.vmap(head_order)(jax.random.split(lookup_series[0], CUSTOMER_COUNT))
    fast = order < HEADS // 2
    slow_rate = jnp.exp(jax.random.uniform(lookup_series[1], (CUSTOMER_COUNT, HEADS), jnp.float32, math.log(0.1), math.log(0.4))) / PAST_ACTIONS
    fast_rate = jnp.exp(jax.random.uniform(lookup_series[2], (CUSTOMER_COUNT, HEADS), jnp.float32, math.log(0.05), math.log(0.15)))
    forgetting_factors = jnp.where(fast, fast_rate, slow_rate)
    segment_scaling = jnp.exp(jax.random.uniform(lookup_series[3], (CUSTOMER_COUNT, HEADS, PAST_ACTIONS // L_DEV), jnp.float32, math.log(0.5), math.log(1.5)))
    segment_scaling = jnp.repeat(segment_scaling, L_DEV, axis=2)
    stochastic_jitter = jax.random.uniform(lookup_series[4], (CUSTOMER_COUNT, HEADS, PAST_ACTIONS), jnp.float32, 0.5, 1.5)
    spike_offset = jax.random.randint(lookup_series[5], (CUSTOMER_COUNT, 2), 0, PAST_ACTIONS)
    spike_kept = jax.random.uniform(lookup_series[6], (CUSTOMER_COUNT, 2), jnp.float32, 0.5, 0.8)
    placement_spots = jnp.arange(PAST_ACTIONS, dtype=jnp.int32)[None, :]
    spike_clusters = jnp.where(placement_spots == spike_offset[:, 0:1], jnp.log(spike_kept[:, 0:1]), 0.0)
    spike_clusters = spike_clusters + jnp.where(placement_spots == spike_offset[:, 1:2], jnp.log(spike_kept[:, 1:2]), 0.0)
    return (-forgetting_factors[..., None] * segment_scaling * stochastic_jitter + spike_clusters[:, None, :]).astype(jnp.float32)


def set_ends(entries, key, low, top_value):
    longest = entries.shape.index(max(entries.shape))
    spots = []
    for shift in (0, 1):
        where = [jax.random.randint(jax.random.fold_in(key, axis), (), 0, length) for axis, length in enumerate(entries.shape)]
        where[longest] = (where[longest] + shift) % entries.shape[longest]
        spots.append(tuple(where))
    return entries.at[spots[0]].set(low).at[spots[1]].set(top_value)


def shard_levels(rng, shape, cuts, least, top_value):
    level = 1.0
    for dim, blocks in cuts:
        draws = jax.random.uniform(jax.random.fold_in(jax.random.fold_in(rng, 6), dim), (blocks,), jnp.float32, least / len(cuts), top_value / len(cuts))
        level = level * jnp.repeat(jnp.exp(draws), shape[dim] // blocks).reshape((-1,) + (1,) * (len(shape) - 1 - dim))
    return level


def rank_bounds(number_of, skew):
    loads = [(1 << 20) // math.isqrt(rank ** skew) + 1 for rank in range(1, number_of + 1)]
    spread = 1 + sum(loads) // (1 << 30)
    return np.cumsum(np.array([max(1, weight // spread) for weight in loads]))


def ranked_ids(stream_key, shape, number_of, lean):
    grid = rank_bounds(number_of, lean)
    lot = jax.random.randint(jax.random.fold_in(stream_key, 1), shape, 0, int(grid[number_of - 1]))
    rank = jnp.searchsorted(jnp.asarray(grid, jnp.int32), lot, side="right")
    return jax.random.permutation(jax.random.fold_in(stream_key, 2), number_of)[rank].astype(jnp.int32)


def bell_draw(key, dims, deviation, limit, shards=(), kind=jnp.bfloat16):
    values = jax.random.normal(key, dims, jnp.float32) * deviation
    if len(shards) > 0:
        values = shard_levels(key, dims, shards, -0.22, 0.18) * values
    return jnp.clip(values, min=-limit, max=limit).astype(kind)


def setup_inputs(seed: int = 0) -> dict:
    key_list = jax.random.split(jax.random.key(seed), 12)
    return {
        "quot_ids": set_ends(ranked_ids(key_list[0], (CUSTOMER_COUNT, PAST_ACTIONS), QROWS, 1), jax.random.fold_in(key_list[0], 3), 0, QROWS - 1).astype(jnp.int32),
        "rem_ids": draw_rem_ids(jax.random.fold_in(key_list[11], 71), 0),
        "lengths": draw_lengths(jax.random.fold_in(key_list[11], 71), 0),
        "log_decay": draw_log_decay(jax.random.fold_in(key_list[11], 71), 0),
        "quot_table": bell_draw(key_list[4], (QROWS, D), 1.0, 6.0),
        "rem_table": bell_draw(key_list[5], (REM, D), 1.0, 6.0, ((0, 32),)),
        "w_query": bell_draw(key_list[6], (D, D), D ** -0.5, 0.375),
        "w_key": bell_draw(key_list[7], (D, D), D ** -0.5, 0.375),
        "w_value": bell_draw(key_list[8], (D, D), D ** -0.5, 0.375),
        "w_out": bell_draw(key_list[9], (D, D), D ** -0.5, 0.375),
        "cotangent": bell_draw(key_list[10], (CUSTOMER_COUNT, PAST_ACTIONS, D), 0.1, 0.59765625, ((0, 32), (1, 8))),
    }


largest_value = lax.Precision.HIGHEST

def decay_mask(cumulative):
    length = cumulative.shape[-1]
    gap = cumulative[..., :, None] - cumulative[..., None, :]
    lower_tri = jnp.arange(length)[:, None] >= jnp.arange(length)[None, :]
    return jnp.where(lower_tri, jnp.exp(jnp.minimum(gap, 0.0)), 0.0)

def reference(quot_ids, rem_ids, lengths, log_decay, quot_table, rem_table, w_query, w_key, w_value, w_out, cotangent):
    blocks = PAST_ACTIONS // L_DEV
    score_scale = 1.0 / math.sqrt(HEAD * PAST_ACTIONS)
    quot_emb = quot_table[quot_ids].reshape(-1, D)
    rem_emb = rem_table[rem_ids].reshape(-1, D)
    embedded = (quot_emb.astype(jnp.float32) * rem_emb.astype(jnp.float32)).astype(jnp.bfloat16)

    def project(matrix):
        result = jnp.dot(embedded, matrix, preferred_element_type=jnp.float32).astype(jnp.bfloat16)
        return result.reshape(CUSTOMER_COUNT, blocks, L_DEV, HEADS, HEAD).transpose(1, 0, 2, 3, 4)
    query_rows = project(w_query)
    key_rows = project(w_key)
    value_rows = project(w_value)
    cumulative = jnp.cumsum(log_decay.reshape(CUSTOMER_COUNT, HEADS, blocks, L_DEV), axis=-1).transpose(2, 0, 1, 3)

    def forward_block(carried_state, inputs):
        query_block, key_block, value_block, cum_block = inputs
        block_end = cum_block[..., -1]
        score_matrix = jnp.einsum('ulhd,umhd->uhlm', query_block.astype(jnp.float32), key_block.astype(jnp.float32), precision=largest_value)
        weight_matrix = (score_scale * score_matrix * decay_mask(cum_block)).astype(jnp.bfloat16)
        within_bounds = jnp.einsum('uhlm,umhd->ulhd', weight_matrix.astype(jnp.float32), value_block.astype(jnp.float32), precision=largest_value)
        growth = jnp.exp(cum_block).transpose(0, 2, 1)[..., None]
        carried = score_scale * jnp.einsum('ulhd,uhde->ulhe', query_block.astype(jnp.float32) * growth, carried_state, precision=largest_value)
        mixed = (within_bounds + carried).astype(jnp.bfloat16)
        falloff = jnp.exp(block_end[..., None] - cum_block).transpose(0, 2, 1)[..., None]
        local_state = jnp.einsum('ulhd,ulhe->uhde', key_block.astype(jnp.float32) * falloff, value_block.astype(jnp.float32), precision=largest_value)
        new_state = jnp.exp(block_end)[..., None, None] * carried_state + local_state
        return (new_state, (mixed, carried_state))
    zero_state = jnp.zeros((CUSTOMER_COUNT, HEADS, HEAD, HEAD), jnp.float32)
    _, (mixed, entering) = lax.scan(forward_block, zero_state, (query_rows, key_rows, value_rows, cumulative))
    flat_mixed = mixed.transpose(1, 0, 2, 3, 4).reshape(-1, D)
    output = jnp.dot(flat_mixed, w_out, preferred_element_type=jnp.float32).astype(jnp.bfloat16).reshape(CUSTOMER_COUNT, PAST_ACTIONS, D)
    position = jnp.arange(PAST_ACTIONS, dtype=jnp.int32)
    in_history = position[None, :] < lengths[:, None]
    masked_cot = jnp.where(in_history[..., None], cotangent.astype(jnp.float32), 0.0).astype(jnp.bfloat16)
    dmixed = jnp.dot(masked_cot.reshape(-1, D), w_out.T, preferred_element_type=jnp.float32).astype(jnp.bfloat16)
    dmixed = dmixed.reshape(CUSTOMER_COUNT, blocks, L_DEV, HEADS, HEAD).transpose(1, 0, 2, 3, 4)

    def backward_block(leaving, inputs):
        query_block, key_block, value_block, dmixed_block, cum_block, entering_block = inputs
        block_end = cum_block[..., -1]
        mask = decay_mask(cum_block)
        query_f = query_block.astype(jnp.float32)
        key_f = key_block.astype(jnp.float32)
        value_f = value_block.astype(jnp.float32)
        dmixed_f = dmixed_block.astype(jnp.float32)
        score_matrix = jnp.einsum('ulhd,umhd->uhlm', query_f, key_f, precision=largest_value)
        weight_matrix = (score_scale * score_matrix * mask).astype(jnp.bfloat16).astype(jnp.float32)
        dscores = jnp.einsum('ulhe,umhe->uhlm', dmixed_f, value_f, precision=largest_value)
        weight_gradient = (score_scale * dscores * mask).astype(jnp.bfloat16).astype(jnp.float32)
        growth = jnp.exp(cum_block).transpose(0, 2, 1)[..., None]
        falloff = jnp.exp(block_end[..., None] - cum_block).transpose(0, 2, 1)[..., None]
        dquery = jnp.einsum('uhlm,umhd->ulhd', weight_gradient, key_f, precision=largest_value) + score_scale * growth * jnp.einsum('uhde,ulhe->ulhd', entering_block, dmixed_f, precision=largest_value)
        dkeys = jnp.einsum('uhlm,ulhd->umhd', weight_gradient, query_f, precision=largest_value) + score_scale * falloff * jnp.einsum('uhde,umhe->umhd', leaving, value_f, precision=largest_value)
        dvalue = jnp.einsum('uhlm,ulhe->umhe', weight_matrix, dmixed_f, precision=largest_value) + score_scale * falloff * jnp.einsum('uhde,umhd->umhe', leaving, key_f, precision=largest_value)
        local_grad = jnp.einsum('ulhd,ulhe->uhde', query_f * growth, dmixed_f, precision=largest_value)
        new_leaving = jnp.exp(block_end)[..., None, None] * leaving + local_grad
        return (new_leaving, (dquery.astype(jnp.bfloat16), dkeys.astype(jnp.bfloat16), dvalue.astype(jnp.bfloat16)))
    _, (dquery, dkeys, dvalue) = lax.scan(backward_block, zero_state, (query_rows, key_rows, value_rows, dmixed, cumulative, entering), reverse=True)

    def flatten(stacked):
        return stacked.transpose(1, 0, 2, 3, 4).reshape(-1, D)
    dembedded = jnp.dot(flatten(dquery), w_query.T, preferred_element_type=jnp.float32)
    dembedded = dembedded + jnp.dot(flatten(dkeys), w_key.T, preferred_element_type=jnp.float32)
    dembedded = dembedded + jnp.dot(flatten(dvalue), w_value.T, preferred_element_type=jnp.float32)
    all_events = jnp.sum(lengths.astype(jnp.float32))
    grad_ratio = float(CUSTOMER_COUNT * PAST_ACTIONS) / all_events
    quot_grad = grad_ratio * jax.ops.segment_sum(dembedded * rem_emb.astype(jnp.float32), quot_ids.reshape(-1), num_segments=QROWS)
    rem_grad = grad_ratio * jax.ops.segment_sum(dembedded * quot_emb.astype(jnp.float32), rem_ids.reshape(-1), num_segments=REM)
    return (output, quot_grad, rem_grad)
```

```python
import math

import jax
import jax.numpy as jnp
from jax import lax
from jax.experimental import pallas as pl
from jax.experimental.pallas import tpu as pltpu
from jax.sharding import PartitionSpec as P

f32 = jnp.float32
bf16 = jnp.bfloat16
i32 = jnp.int32
EXACT = lax.Precision.HIGHEST
VM = pl.BlockSpec(memory_space=pltpu.VMEM)
SM = pl.BlockSpec(memory_space=pltpu.SMEM)

NN = (((1,), (0,)), ((), ()))
NT = (((1,), (1,)), ((), ()))
TN = (((0,), (0,)), ((), ()))


def dot(a, b, dims=NN, precision=None):
    return lax.dot_general(a, b, dims, preferred_element_type=f32, precision=precision)


def iota(shape, dim):
    return lax.broadcasted_iota(i32, shape, dim)


def where_bf16(mask, a):
    return jnp.where(mask, a, 0.0).astype(bf16)


def halves(whole):
    return (whole >> 4).astype(f32), (whole & 15).astype(f32)


def spread_column(row):
    n = row.shape[1]
    diagonal = iota((n, n), 0) == iota((n, n), 1)
    high, low = halves(row)
    ones = jnp.ones((n, 128), bf16)
    column = 16.0 * dot(where_bf16(diagonal, high), ones) + dot(where_bf16(diagonal, low), ones)
    return column.astype(i32)


def tiled_match(column, width):
    n = column.shape[0]
    lanes = iota((n, 128), 1)
    parts = [where_bf16(column == lanes + j * 128, 1.0) for j in range(width // 128)]
    return jnp.concatenate(parts, axis=1)


def call(kernel, outs, args, specs=None, scratch=(), limit=40):
    return pl.pallas_call(
        kernel,
        out_shape=tuple(jax.ShapeDtypeStruct(s, d) for s, d in outs),
        in_specs=specs if specs is not None else [VM] * len(args),
        out_specs=tuple(VM for _ in outs),
        scratch_shapes=list(scratch),
        compiler_params=pltpu.CompilerParams(vmem_limit_bytes=limit * 1024 * 1024),
    )(*args)


def request_kernel(len_ref, ids_ref, out_ref, slot_ref, *, rows_own, cap):
    users, block = ids_ref.shape
    shards, _, lanes = out_ref.shape
    shift = rows_own.bit_length() - 1
    earlier = where_bf16(iota((block, block), 0) < iota((block, block), 1), 1.0)
    place = iota((lanes, block), 0)
    total = jnp.zeros((shards, lanes), f32)
    count = jnp.int32(0)
    slot_ref[...] = jnp.zeros_like(slot_ref)
    for u in range(users):
        ids = ids_ref[u : u + 1, :]
        owner = ids >> shift
        named = iota((shards, block), 0) == owner
        named_16 = where_bf16(named, 1.0)
        before = dot(named_16, earlier)
        rank = jnp.sum(jnp.where(named, before, 0.0), axis=0, keepdims=True).astype(i32)
        high, low = halves((ids & (rows_own - 1)) + 1)
        chosen = place == rank + u * cap
        total = total + 16.0 * dot(named_16, where_bf16(chosen, high), NT)
        total = total + dot(named_16, where_bf16(chosen, low), NT)
        slot_ref[u : u + 1, :] = (owner * users + u) * cap + rank
        count = count + len_ref[u]
    wanted = jnp.where(iota((shards, lanes), 1) == users * cap, count, total.astype(i32))
    out_ref[:, 0, :] = wanted


def spread_wanted(wanted, per):
    return halves(wanted)


def answer_kernel(wanted_ref, table_ref, out_ref, hot_ref, *, per):
    shards, _, lanes = wanted_ref.shape
    slots = shards * per
    rows = table_ref.shape[0]
    wanted = jnp.where(iota((shards, lanes), 1) < per, wanted_ref[:, 0, :], 0)
    high, low = halves(wanted)
    repeat = where_bf16(iota((slots, shards), 0) // per == iota((slots, shards), 1), 1.0)
    own = iota((slots, lanes), 0) % per == iota((slots, lanes), 1)
    ones = jnp.ones((lanes, 128), bf16)
    high = dot(where_bf16(own, dot(repeat, high.astype(bf16))), ones)
    low = dot(where_bf16(own, dot(repeat, low.astype(bf16))), ones)
    column = (16.0 * high + low).astype(i32) - 1
    spot = iota((slots, 128), 1)
    for j in range(rows // 128):
        hot_ref[:, j * 128 : (j + 1) * 128] = where_bf16(column == spot + j * 128, 1.0)
    out_ref[...] = dot(hot_ref[...], table_ref[...]).astype(bf16)


def quotient_kernel(
    len_ref, at_ref, ids_ref, table_ref, cot_ref, w_out_ref, quot_ref, dmixed_ref
):
    users, block = ids_ref.shape
    rows, width = table_ref.shape
    for u in range(users):
        hot = tiled_match(spread_column(ids_ref[u : u + 1, :]), rows)
        quot_ref[u * block : (u + 1) * block, :] = dot(hot, table_ref[...]).astype(bf16)
        valid = at_ref[0] * block + iota((block, width), 0) < len_ref[u]
        masked = jnp.where(valid, cot_ref[u].astype(f32), 0.0).astype(bf16)
        dmixed_ref[u * block : (u + 1) * block, :] = dot(masked, w_out_ref[...], NT).astype(bf16)


def decays(log_decay, width):
    heads, block = log_decay.shape
    upper = jnp.where(iota((block, block), 0) <= iota((block, block), 1), 1.0, 0.0)
    lower = jnp.where(iota((block, block), 0) >= iota((block, block), 1), 1.0, 0.0)
    padded = jnp.concatenate([log_decay, jnp.zeros((8 - heads, block), f32)], axis=0)
    rows = dot(padded, upper, precision=EXACT)
    columns = dot(lower, padded, NT, precision=EXACT)
    return rows, columns


def over_heads(columns, heads, width):
    n = columns.shape[0]
    head_of = iota((n, width), 1) // (width // heads)
    wide = jnp.broadcast_to(columns[:, 0:1], (n, width))
    for h in range(1, heads):
        wide = jnp.where(head_of == h, jnp.broadcast_to(columns[:, h : h + 1], (n, width)), wide)
    return wide


def diagonal_heads(square, heads):
    width = square.shape[1]
    size = width // heads
    head_of = iota((size, width), 1) // size
    out = square[0:size, :]
    for h in range(1, heads):
        out = jnp.where(head_of == h, square[h * size : (h + 1) * size, :], out)
    return out


def block_diagonal(state, heads):
    size, width = state.shape
    head_of = iota((size, width), 1) // (width // heads)
    return jnp.concatenate([where_bf16(head_of == h, state) for h in range(heads)], axis=0)


def project_kernel(
    at_ref,
    answered_ref,
    slot_ref,
    quot_ref,
    dmixed_ref,
    decay_ref,
    wq_ref,
    wk_ref,
    wv_ref,
    rem_ref,
    q_ref,
    k_ref,
    v_ref,
    payload_ref,
):
    users, heads, block = decay_ref.shape
    slots, width = answered_ref.shape
    peers = payload_ref.shape[0]
    size = width // heads
    me = at_ref[0]
    ends = []
    for u in range(users):
        at = slice(u * block, (u + 1) * block)
        hot = tiled_match(spread_column(slot_ref[u : u + 1, :]), slots)
        rem = dot(hot, answered_ref[...]).astype(bf16)
        rem_ref[at, :] = rem
        embedded = (quot_ref[at, :].astype(f32) * rem.astype(f32)).astype(bf16)
        q = dot(embedded, wq_ref[...]).astype(bf16)
        k = dot(embedded, wk_ref[...]).astype(bf16)
        v = dot(embedded, wv_ref[...]).astype(bf16)
        q_ref[at, :] = q
        k_ref[at, :] = k
        v_ref[at, :] = v
        _, columns = decays(decay_ref[u], width)
        wide = over_heads(columns, heads, width)
        end = wide[block - 1 : block, :]
        ends.append(end)
        falling = (k.astype(f32) * jnp.exp(end - wide)).astype(bf16)
        growing = (q.astype(f32) * jnp.exp(wide)).astype(bf16)
        state = diagonal_heads(dot(falling, v, TN), heads).astype(bf16)
        grad = diagonal_heads(dot(growing, dmixed_ref[at, :], TN), heads).astype(bf16)
        for peer in range(peers):
            payload_ref[peer, u * size : (u + 1) * size, :] = jnp.where(peer > me, state, grad)
    rows = iota((16, width), 0)
    tail = jnp.zeros((16, width), f32)
    for u in range(users):
        left = ends[u]
        for part in range(3):
            piece = left.astype(bf16).astype(f32)
            left = left - piece
            tail = jnp.where(rows == part * users + u, piece, tail)
    tail = tail.astype(bf16)
    for peer in range(peers):
        payload_ref[peer, users * size :, :] = tail


def within_kernel(
    q_ref, k_ref, v_ref, dmixed_ref, decay_ref, mixed_ref, dq_ref, dk_ref, dv_ref, *, scale
):
    users, heads, block = decay_ref.shape
    width = q_ref.shape[1]
    head_of = iota((block, width), 1) // (width // heads)
    lower_tri = iota((block, block), 0) >= iota((block, block), 1)
    for u in range(users):
        at = slice(u * block, (u + 1) * block)
        q, k, v, dmixed = q_ref[at, :], k_ref[at, :], v_ref[at, :], dmixed_ref[at, :]
        rows, columns = decays(decay_ref[u], width)
        mixed = jnp.zeros((block, width), f32)
        dq = jnp.zeros((block, width), f32)
        dk = jnp.zeros((block, width), f32)
        dv = jnp.zeros((block, width), f32)
        zero = jnp.zeros((), bf16)
        for h in range(heads):
            own = head_of == h
            q_h = jnp.where(own, q, zero)
            k_h = jnp.where(own, k, zero)
            v_h = jnp.where(own, v, zero)
            d_h = jnp.where(own, dmixed, zero)
            gap = columns[:, h : h + 1] - rows[h : h + 1, :]
            mask = jnp.where(lower_tri, scale * jnp.exp(jnp.minimum(gap, 0.0)), 0.0)
            weights = (dot(q_h, k, NT) * mask).astype(bf16)
            dweights = (dot(d_h, v, NT) * mask).astype(bf16)
            mixed = mixed + dot(weights, v_h)
            dq = dq + dot(dweights, k_h)
            dk = dk + dot(dweights, q_h, TN)
            dv = dv + dot(weights, d_h, TN)
        mixed_ref[at, :] = mixed
        dq_ref[at, :] = dq
        dk_ref[at, :] = dk
        dv_ref[at, :] = dv


def gradient_kernel(
    at_ref,
    payload_ref,
    mixed_ref,
    dq_ref,
    dk_ref,
    dv_ref,
    q_ref,
    k_ref,
    v_ref,
    dmixed_ref,
    decay_ref,
    wq_ref,
    wk_ref,
    wv_ref,
    w_out_ref,
    rem_ref,
    quot_ref,
    slot_ref,
    ids_ref,
    out_ref,
    rem_send_ref,
    quot_part_ref,
    *,
    scale,
):
    users, heads, block = decay_ref.shape
    width = q_ref.shape[1]
    peers = payload_ref.shape[0]
    size = width // heads
    slots = rem_send_ref.shape[0]
    rows_all = quot_part_ref.shape[0]
    me = at_ref[0]
    rem_terms, quot_terms = [], []
    for u in range(users):
        at = slice(u * block, (u + 1) * block)
        ends = []
        for peer in range(peers):
            tail = payload_ref[peer, users * size :, :].astype(f32)
            ends.append(
                tail[u : u + 1, :]
                + tail[users + u : users + u + 1, :]
                + tail[2 * users + u : 2 * users + u + 1, :]
            )
        entering = jnp.zeros((size, width), f32)
        for peer in range(peers):
            part = payload_ref[peer, u * size : (u + 1) * size, :].astype(f32)
            linked = jnp.exp(ends[peer]) * entering + part
            entering = jnp.where(peer < me, linked, entering)
        leaving = jnp.zeros((size, width), f32)
        for peer in reversed(range(peers)):
            part = payload_ref[peer, u * size : (u + 1) * size, :].astype(f32)
            linked = jnp.exp(ends[peer]) * leaving + part
            leaving = jnp.where(peer > me, linked, leaving)
        entering = block_diagonal(entering, heads)
        leaving = block_diagonal(leaving, heads)
        q, k, v, dmixed = q_ref[at, :], k_ref[at, :], v_ref[at, :], dmixed_ref[at, :]
        _, columns = decays(decay_ref[u], width)
        wide = over_heads(columns, heads, width)
        growth = scale * jnp.exp(wide)
        falloff = scale * jnp.exp(wide[block - 1 : block, :] - wide)
        mixed = (mixed_ref[at, :] + growth * dot(q, entering)).astype(bf16)
        out_ref[u] = dot(mixed, w_out_ref[...]).astype(bf16)
        dq = (dq_ref[at, :] + growth * dot(dmixed, entering, NT)).astype(bf16)
        dk = (dk_ref[at, :] + falloff * dot(v, leaving, NT)).astype(bf16)
        dv = (dv_ref[at, :] + falloff * dot(k, leaving)).astype(bf16)
        dembedded = dot(dq, wq_ref[...], NT) + dot(dk, wk_ref[...], NT) + dot(dv, wv_ref[...], NT)
        rem_terms.append((dembedded * quot_ref[at, :].astype(f32)).astype(bf16))
        quot_terms.append((dembedded * rem_ref[at, :].astype(f32)).astype(bf16))
    rem_terms = jnp.concatenate(rem_terms, axis=0)
    quot_terms = jnp.concatenate(quot_terms, axis=0)
    slot = jnp.concatenate([slot_ref[u : u + 1, :] for u in range(users)], axis=1)
    ids = jnp.concatenate([ids_ref[u : u + 1, :] for u in range(users)], axis=1)
    spot = iota((block, users * block), 0)
    for j in range(slots // block):
        hot = where_bf16(spot + j * block == slot, 1.0)
        rem_send_ref[j * block : (j + 1) * block, :] = dot(hot, rem_terms).astype(bf16)
    for j in range(rows_all // block):
        hot = where_bf16(spot + j * block == ids, 1.0)
        quot_part_ref[j * block : (j + 1) * block, :] = dot(hot, quot_terms).astype(bf16)


def collect_kernel(wanted_ref, back_ref, out_ref, *, per):
    shards, _, lanes = wanted_ref.shape
    slots = shards * per
    rows, width = out_ref.shape
    chunk = 256
    wanted = jnp.where(iota((shards, lanes), 1) < per, wanted_ref[:, 0, :], 0)
    high, low = halves(wanted)
    tile = where_bf16(iota((lanes, slots), 1) % per == iota((lanes, slots), 0), 1.0)
    own = iota((shards, slots), 1) // per == iota((shards, slots), 0)
    high = jnp.sum(jnp.where(own, dot(high.astype(bf16), tile), 0.0), axis=0, keepdims=True)
    low = jnp.sum(jnp.where(own, dot(low.astype(bf16), tile), 0.0), axis=0, keepdims=True)
    row = (16.0 * high + low).astype(i32) - 1
    spot = iota((chunk, slots), 0)
    back = back_ref[...]
    for j in range(rows // chunk):
        hot = where_bf16(spot + j * chunk == row, 1.0)
        out_ref[j * chunk : (j + 1) * chunk, :] = dot(hot, back).astype(bf16)


def exchange(array, axis):
    return lax.all_to_all(array, axis, split_axis=0, concat_axis=0, tiled=True)


def added(parts):
    return jnp.sum(parts.astype(f32), axis=0).astype(bf16)


def body(
    quot_ids,
    rem_ids,
    lengths,
    log_decay,
    quot_table,
    rem_table,
    w_query,
    w_key,
    w_value,
    w_out,
    cotangent,
):
    users, block = quot_ids.shape
    rows_all, width = quot_table.shape
    heads = log_decay.shape[1]
    size = width // heads
    shards = lax.axis_size("user")
    peers = lax.axis_size("hist")
    rows_own = rem_table.shape[0]
    cap = 2 * block // shards
    per = users * cap
    slots = shards * per
    scale = 1.0 / math.sqrt(size * block * peers)
    at = lax.axis_index("hist").astype(i32).reshape(1)
    lanes = (per // 128 + 1) * 128

    def bound(kernel, **fixed):
        def run(*refs):
            kernel(*refs, **fixed)

        run.__name__ = kernel.__name__
        return run

    requests, slot = call(
        bound(request_kernel, rows_own=rows_own, cap=cap),
        [((shards, 1, lanes), i32), ((8, block), i32)],
        (lengths, rem_ids),
        [SM, VM],
    )
    wanted = exchange(requests, "user")
    quot_emb, dmixed = call(
        quotient_kernel,
        [((users * block, width), bf16)] * 2,
        (lengths, at, quot_ids, quot_table, cotangent, w_out),
        [SM, SM, VM, VM, VM, VM],
    )
    (found,) = call(
        bound(answer_kernel, per=per),
        [((slots, width), bf16)],
        (wanted, rem_table),
        scratch=[pltpu.VMEM((slots, rows_own), bf16)],
    )
    answered = exchange(found.reshape(shards, per, width), "user").reshape(slots, width)
    rem_emb, q, k, v, payload = call(
        project_kernel,
        [((users * block, width), bf16)] * 4 + [((peers, users * size + 16, width), bf16)],
        (at, answered, slot, quot_emb, dmixed, log_decay, w_query, w_key, w_value),
        [SM] + [VM] * 8,
    )
    states = exchange(payload, "hist")
    mixed, dq, dk, dv = call(
        bound(within_kernel, scale=scale),
        [((users * block, width), f32)] * 4,
        (q, k, v, dmixed, log_decay),
    )
    output, rem_send, quot_part = call(
        bound(gradient_kernel, scale=scale),
        [((users, block, width), bf16), ((slots, width), bf16), ((rows_all, width), bf16)],
        (
            at,
            states,
            mixed,
            dq,
            dk,
            dv,
            q,
            k,
            v,
            dmixed,
            log_decay,
            w_query,
            w_key,
            w_value,
            w_out,
            rem_emb,
            quot_emb,
            slot,
            quot_ids,
        ),
        [SM] + [VM] * 18,
    )
    rem_back = exchange(rem_send.reshape(shards, per, width), "user").reshape(slots, width)
    quot_back = exchange(quot_part.reshape(peers, rows_all // peers, width), "hist")
    quot_sum = added(quot_back)
    quot_back = exchange(quot_sum.reshape(shards, -1, width), "user")
    (rem_part,) = call(
        bound(collect_kernel, per=per), [((rows_own, width), bf16)], (wanted, rem_back)
    )
    rem_back = exchange(rem_part.reshape(peers, rows_own // peers, width), "hist")
    rem_sum = added(rem_back)
    quot_sum = added(quot_back)
    quot_sum = exchange(jnp.broadcast_to(quot_sum, (shards,) + quot_sum.shape), "user")
    both = jnp.concatenate([rem_sum, quot_sum.reshape(-1, width)], axis=0)
    both = exchange(jnp.broadcast_to(both, (peers,) + both.shape), "hist")
    all_events = jnp.sum(wanted[:, 0, per].astype(f32))
    grad_ratio = float(users * shards * block * peers) / all_events
    rem_rows = rows_own // peers
    rem_grad = grad_ratio * both[:, :rem_rows].astype(f32).reshape(rows_own, width)
    quot_grad = grad_ratio * both[:, rem_rows:].astype(f32).reshape(rows_all, width)
    return (output, quot_grad, rem_grad)


def solution(mesh):
    return jax.shard_map(
        body,
        mesh=mesh,
        in_specs=(
            P("user", "hist"),
            P("user", "hist"),
            P("user"),
            P("user", None, "hist"),
            P(),
            P("user", None),
            P(),
            P(),
            P(),
            P(),
            P("user", "hist", None),
        ),
        out_specs=(P("user", "hist", None), P(), P("user", None)),
        check_vma=False,
    )
```

```python
import functools
import math

import jax
import jax.numpy as jnp
from jax import lax
from jax.experimental import pallas as pl
from jax.experimental.pallas import tpu as pltpu
from jax.sharding import PartitionSpec as P

f32 = jnp.float32
bf16 = jnp.bfloat16
i32 = jnp.int32
EXACT = lax.Precision.HIGHEST
VM = pl.BlockSpec(memory_space=pltpu.VMEM)
SM = pl.BlockSpec(memory_space=pltpu.SMEM)

NN = (((1,), (0,)), ((), ()))
NT = (((1,), (1,)), ((), ()))
TN = (((0,), (0,)), ((), ()))


def dot(a, b, dims=NN, precision=None):
    return lax.dot_general(a, b, dims, preferred_element_type=f32, precision=precision)


def iota(shape, dim):
    return lax.broadcasted_iota(i32, shape, dim)


def where_bf16(mask, a):
    return jnp.where(mask, a, 0.0).astype(bf16)


def halves(whole):
    return (whole >> 4).astype(f32), (whole & 15).astype(f32)


def spread_column(row):
    n = row.shape[1]
    diagonal = iota((n, n), 0) == iota((n, n), 1)
    high, low = halves(row)
    ones = jnp.ones((n, 128), bf16)
    column = 16.0 * dot(where_bf16(diagonal, high), ones) + dot(where_bf16(diagonal, low), ones)
    return column.astype(i32)


def tiled_match(column, width):
    n = column.shape[0]
    lanes = iota((n, 128), 1)
    parts = [where_bf16(column == lanes + j * 128, 1.0) for j in range(width // 128)]
    return jnp.concatenate(parts, axis=1)


def call(kernel, outs, args, specs=None, scratch=(), limit=20):
    return pl.pallas_call(
        kernel,
        out_shape=tuple(jax.ShapeDtypeStruct(s, d) for s, d in outs),
        in_specs=specs if specs is not None else [VM] * len(args),
        out_specs=tuple(VM for _ in outs),
        scratch_shapes=list(scratch),
        compiler_params=pltpu.CompilerParams(vmem_limit_bytes=limit * 1024 * 1024),
    )(*args)


def request_kernel(len_ref, ids_ref, out_ref, slot_ref, *, rows_own, cap):
    users, block = ids_ref.shape
    shards, _, lanes = out_ref.shape
    shift = rows_own.bit_length() - 1
    earlier = where_bf16(iota((block, block), 0) < iota((block, block), 1), 1.0)
    place = iota((lanes, block), 0)
    total = jnp.zeros((shards, lanes), f32)
    count = jnp.int32(0)
    slot_ref[...] = jnp.zeros_like(slot_ref)
    for u in range(users):
        ids = ids_ref[u : u + 1, :]
        owner = ids >> shift
        named = iota((shards, block), 0) == owner
        named_16 = where_bf16(named, 1.0)
        before = dot(named_16, earlier)
        rank = jnp.sum(jnp.where(named, before, 0.0), axis=0, keepdims=True).astype(i32)
        high, low = halves((ids & (rows_own - 1)) + 1)
        chosen = place == rank + u * cap
        total = total + 16.0 * dot(named_16, where_bf16(chosen, high), NT)
        total = total + dot(named_16, where_bf16(chosen, low), NT)
        slot_ref[u : u + 1, :] = (owner * users + u) * cap + rank
        count = count + len_ref[u]
    wanted = jnp.where(iota((shards, lanes), 1) == users * cap, count, total.astype(i32))
    out_ref[:, 0, :] = wanted


def answer_kernel(wanted_ref, table_ref, out_ref, hot_ref, *, per):
    shards, _, lanes = wanted_ref.shape
    slots = shards * per
    rows = table_ref.shape[0]
    wanted = jnp.where(iota((shards, lanes), 1) < per, wanted_ref[:, 0, :], 0)
    high, low = halves(wanted)
    repeat = where_bf16(iota((slots, shards), 0) // per == iota((slots, shards), 1), 1.0)
    own = iota((slots, lanes), 0) % per == iota((slots, lanes), 1)
    ones = jnp.ones((lanes, 128), bf16)
    high = dot(where_bf16(own, dot(repeat, high.astype(bf16))), ones)
    low = dot(where_bf16(own, dot(repeat, low.astype(bf16))), ones)
    column = (16.0 * high + low).astype(i32) - 1
    spot = iota((slots, 128), 1)
    for j in range(rows // 128):
        hot_ref[:, j * 128 : (j + 1) * 128] = where_bf16(column == spot + j * 128, 1.0)
    out_ref[...] = dot(hot_ref[...], table_ref[...]).astype(bf16)


def quotient_kernel(
    len_ref, at_ref, ids_ref, table_ref, cot_ref, w_out_ref, quot_ref, dmixed_ref
):
    users, block = ids_ref.shape
    rows, width = table_ref.shape
    for u in range(users):
        hot = tiled_match(spread_column(ids_ref[u : u + 1, :]), rows)
        quot_ref[u * block : (u + 1) * block, :] = dot(hot, table_ref[...]).astype(bf16)
        valid = at_ref[0] * block + iota((block, width), 0) < len_ref[u]
        masked = jnp.where(valid, cot_ref[u].astype(f32), 0.0).astype(bf16)
        dmixed_ref[u * block : (u + 1) * block, :] = dot(masked, w_out_ref[...], NT).astype(bf16)


def decays(log_decay, width):
    heads, block = log_decay.shape
    upper = jnp.where(iota((block, block), 0) <= iota((block, block), 1), 1.0, 0.0)
    lower = jnp.where(iota((block, block), 0) >= iota((block, block), 1), 1.0, 0.0)
    padded = jnp.concatenate([log_decay, jnp.zeros((8 - heads, block), f32)], axis=0)
    rows = dot(padded, upper, precision=EXACT)
    columns = dot(lower, padded, NT, precision=EXACT)
    return rows, columns


def over_heads(columns, heads, width):
    n = columns.shape[0]
    head_of = iota((n, width), 1) // (width // heads)
    wide = jnp.broadcast_to(columns[:, 0:1], (n, width))
    for h in range(1, heads):
        wide = jnp.where(head_of == h, jnp.broadcast_to(columns[:, h : h + 1], (n, width)), wide)
    return wide


def diagonal_heads(square, heads):
    width = square.shape[1]
    size = width // heads
    head_of = iota((size, width), 1) // size
    out = square[0:size, :]
    for h in range(1, heads):
        out = jnp.where(head_of == h, square[h * size : (h + 1) * size, :], out)
    return out


def block_diagonal(state, heads):
    size, width = state.shape
    head_of = iota((size, width), 1) // (width // heads)
    return jnp.concatenate([where_bf16(head_of == h, state) for h in range(heads)], axis=0)


def project_kernel(
    at_ref,
    answered_ref,
    slot_ref,
    quot_ref,
    dmixed_ref,
    decay_ref,
    wq_ref,
    wk_ref,
    wv_ref,
    rem_ref,
    q_ref,
    k_ref,
    v_ref,
    payload_ref,
):
    users, heads, block = decay_ref.shape
    slots, width = answered_ref.shape
    peers = payload_ref.shape[0]
    size = width // heads
    me = at_ref[0]
    ends = []
    for u in range(users):
        at = slice(u * block, (u + 1) * block)
        hot = tiled_match(spread_column(slot_ref[u : u + 1, :]), slots)
        rem = dot(hot, answered_ref[...]).astype(bf16)
        rem_ref[at, :] = rem
        embedded = (quot_ref[at, :].astype(f32) * rem.astype(f32)).astype(bf16)
        q = dot(embedded, wq_ref[...]).astype(bf16)
        k = dot(embedded, wk_ref[...]).astype(bf16)
        v = dot(embedded, wv_ref[...]).astype(bf16)
        q_ref[at, :] = q
        k_ref[at, :] = k
        v_ref[at, :] = v
        _, columns = decays(decay_ref[u], width)
        wide = over_heads(columns, heads, width)
        end = wide[block - 1 : block, :]
        ends.append(end)
        falling = (k.astype(f32) * jnp.exp(end - wide)).astype(bf16)
        growing = (q.astype(f32) * jnp.exp(wide)).astype(bf16)
        state = diagonal_heads(dot(falling, v, TN), heads).astype(bf16)
        grad = diagonal_heads(dot(growing, dmixed_ref[at, :], TN), heads).astype(bf16)
        for peer in range(peers):
            payload_ref[peer, u * size : (u + 1) * size, :] = jnp.where(peer > me, state, grad)
    rows = iota((16, width), 0)
    tail = jnp.zeros((16, width), f32)
    for u in range(users):
        left = ends[u]
        for part in range(3):
            piece = left.astype(bf16).astype(f32)
            left = left - piece
            tail = jnp.where(rows == part * users + u, piece, tail)
    tail = tail.astype(bf16)
    for peer in range(peers):
        payload_ref[peer, users * size :, :] = tail


def within_kernel(
    q_ref, k_ref, v_ref, dmixed_ref, decay_ref, mixed_ref, dq_ref, dk_ref, dv_ref, *, scale
):
    users, heads, block = decay_ref.shape
    width = q_ref.shape[1]
    head_of = iota((block, width), 1) // (width // heads)
    lower_tri = iota((block, block), 0) >= iota((block, block), 1)
    for u in range(users):
        at = slice(u * block, (u + 1) * block)
        q, k, v, dmixed = q_ref[at, :], k_ref[at, :], v_ref[at, :], dmixed_ref[at, :]
        rows, columns = decays(decay_ref[u], width)
        mixed = jnp.zeros((block, width), f32)
        dq = jnp.zeros((block, width), f32)
        dk = jnp.zeros((block, width), f32)
        dv = jnp.zeros((block, width), f32)
        zero = jnp.zeros((), bf16)
        for h in range(heads):
            own = head_of == h
            q_h = jnp.where(own, q, zero)
            k_h = jnp.where(own, k, zero)
            v_h = jnp.where(own, v, zero)
            d_h = jnp.where(own, dmixed, zero)
            gap = columns[:, h : h + 1] - rows[h : h + 1, :]
            mask = jnp.where(lower_tri, scale * jnp.exp(jnp.minimum(gap, 0.0)), 0.0)
            weights = (dot(q_h, k, NT) * mask).astype(bf16)
            dweights = (dot(d_h, v, NT) * mask).astype(bf16)
            mixed = mixed + dot(weights, v_h)
            dq = dq + dot(dweights, k_h)
            dk = dk + dot(dweights, q_h, TN)
            dv = dv + dot(weights, d_h, TN)
        mixed_ref[at, :] = mixed
        dq_ref[at, :] = dq
        dk_ref[at, :] = dk
        dv_ref[at, :] = dv


def sum_halves(ids, terms, core, keep_ref, give_ref):
    half = keep_ref.shape[0]
    chunk = min(256, half)
    spot = iota((chunk, ids.shape[1]), 0)
    for ref, owner in ((give_ref, 1 - core), (keep_ref, core)):
        near = ids - owner * half
        for j in range(half // chunk):
            hot = where_bf16(spot + j * chunk == near, 1.0)
            ref[j * chunk : (j + 1) * chunk, :] = dot(hot, terms).astype(ref.dtype)


def gradient_kernel(
    at_ref,
    payload_ref,
    mixed_ref,
    dq_ref,
    dk_ref,
    dv_ref,
    q_ref,
    k_ref,
    v_ref,
    dmixed_ref,
    decay_ref,
    wq_ref,
    wk_ref,
    wv_ref,
    w_out_ref,
    rem_ref,
    quot_ref,
    slot_ref,
    ids_ref,
    out_ref,
    rem_send_ref,
    keep_ref,
    give_ref,
    *,
    scale,
):
    users, heads, block = decay_ref.shape
    width = q_ref.shape[1]
    peers = payload_ref.shape[0]
    size = width // heads
    slots = rem_send_ref.shape[0]
    me = at_ref[0]
    rem_terms, quot_terms = [], []
    for u in range(users):
        at = slice(u * block, (u + 1) * block)
        ends = []
        for peer in range(peers):
            tail = payload_ref[peer, users * size :, :].astype(f32)
            ends.append(
                tail[u : u + 1, :]
                + tail[users + u : users + u + 1, :]
                + tail[2 * users + u : 2 * users + u + 1, :]
            )
        entering = jnp.zeros((size, width), f32)
        for peer in range(peers):
            part = payload_ref[peer, u * size : (u + 1) * size, :].astype(f32)
            linked = jnp.exp(ends[peer]) * entering + part
            entering = jnp.where(peer < me, linked, entering)
        leaving = jnp.zeros((size, width), f32)
        for peer in reversed(range(peers)):
            part = payload_ref[peer, u * size : (u + 1) * size, :].astype(f32)
            linked = jnp.exp(ends[peer]) * leaving + part
            leaving = jnp.where(peer > me, linked, leaving)
        entering = block_diagonal(entering, heads)
        leaving = block_diagonal(leaving, heads)
        q, k, v, dmixed = q_ref[at, :], k_ref[at, :], v_ref[at, :], dmixed_ref[at, :]
        _, columns = decays(decay_ref[u], width)
        wide = over_heads(columns, heads, width)
        growth = scale * jnp.exp(wide)
        falloff = scale * jnp.exp(wide[block - 1 : block, :] - wide)
        mixed = (mixed_ref[at, :] + growth * dot(q, entering)).astype(bf16)
        out_ref[u] = dot(mixed, w_out_ref[...]).astype(bf16)
        dq = (dq_ref[at, :] + growth * dot(dmixed, entering, NT)).astype(bf16)
        dk = (dk_ref[at, :] + falloff * dot(v, leaving, NT)).astype(bf16)
        dv = (dv_ref[at, :] + falloff * dot(k, leaving)).astype(bf16)
        dembedded = dot(dq, wq_ref[...], NT) + dot(dk, wk_ref[...], NT) + dot(dv, wv_ref[...], NT)
        rem_terms.append((dembedded * quot_ref[at, :].astype(f32)).astype(bf16))
        quot_terms.append((dembedded * rem_ref[at, :].astype(f32)).astype(bf16))
    rem_terms = jnp.concatenate(rem_terms, axis=0)
    quot_terms = jnp.concatenate(quot_terms, axis=0)
    slot = jnp.concatenate([slot_ref[u : u + 1, :] for u in range(users)], axis=1)
    ids = jnp.concatenate([ids_ref[u : u + 1, :] for u in range(users)], axis=1)
    spot = iota((block, users * block), 0)
    for j in range(slots // block):
        hot = where_bf16(spot + j * block == slot, 1.0)
        rem_send_ref[j * block : (j + 1) * block, :] = dot(hot, rem_terms).astype(bf16)
    sum_halves(ids, quot_terms, me % 2, keep_ref, give_ref)


def collect_kernel(at_ref, wanted_ref, back_ref, keep_ref, give_ref, *, per):
    shards, _, lanes = wanted_ref.shape
    slots = shards * per
    wanted = jnp.where(iota((shards, lanes), 1) < per, wanted_ref[:, 0, :], 0)
    high, low = halves(wanted)
    tile = where_bf16(iota((lanes, slots), 1) % per == iota((lanes, slots), 0), 1.0)
    own = iota((shards, slots), 1) // per == iota((shards, slots), 0)
    high = jnp.sum(jnp.where(own, dot(high.astype(bf16), tile), 0.0), axis=0, keepdims=True)
    low = jnp.sum(jnp.where(own, dot(low.astype(bf16), tile), 0.0), axis=0, keepdims=True)
    row = (16.0 * high + low).astype(i32) - 1
    sum_halves(row, back_ref[...], at_ref[0] % 2, keep_ref, give_ref)


def split_kernel(at_ref, keep_ref, got_ref, *out_refs):
    chips = len(out_refs)
    rows = out_refs[0].shape[0]
    for d, out_ref in enumerate(out_refs):
        base = pl.multiple_of(lax.rem(at_ref[0] // 2 + d, chips) * rows, rows)
        both = keep_ref[pl.ds(base, rows), :] + got_ref[pl.ds(base, rows), :].astype(f32)
        out_ref[...] = both.astype(bf16)


def place_kernel(at_ref, wanted_ref, *refs, per, total):
    out_ref = refs[-1]
    chunks = refs[:-1]
    chips = len(chunks) // 2
    rows = chunks[0].shape[0]
    shards, _, lanes = wanted_ref.shape
    counted = jnp.where(iota((shards, lanes), 1) == per, wanted_ref[:, 0, :], 0)
    ratio = total / jnp.sum(counted.astype(f32), axis=(0, 1), keepdims=True)
    chip, core = at_ref[0] // 2, at_ref[0] % 2
    for other in range(2):
        half = core + other - 2 * core * other
        for d in range(chips):
            spot = half * chips + lax.rem(chip + chips - d, chips)
            base = pl.multiple_of(spot * rows, rows)
            out_ref[pl.ds(base, rows), :] = ratio * chunks[other * chips + d][...].astype(f32)


def exchange(array, axis):
    return lax.all_to_all(array, axis, split_axis=0, concat_axis=0, tiled=True)


def added(parts):
    return jnp.sum(parts.astype(f32), axis=0).astype(bf16)


def to_core(array):
    peers = lax.axis_size("hist")
    return lax.ppermute(array, "hist", [(i, i ^ 1) for i in range(peers)])


def to_chip(array, steps):
    peers = lax.axis_size("hist")
    return lax.ppermute(array, "hist", [(i, (i + 2 * steps) % peers) for i in range(peers)])


def reduced(at, keep, give):
    chips = lax.axis_size("hist") // 2
    rows = keep.shape[0] // chips
    chunks = call(
        split_kernel,
        [((rows, keep.shape[1]), bf16)] * chips,
        (at, keep, to_core(give)),
        [SM, VM, VM],
    )
    got = [to_chip(chunks[d], d) for d in range(1, chips)]
    return sum((c.astype(f32) for c in got), chunks[0].astype(f32)).astype(bf16)


def gathered(at, wanted, chunk, per, total):
    chips = lax.axis_size("hist") // 2
    mine = [chunk] + [to_chip(chunk, d) for d in range(1, chips)]
    theirs = [to_core(c) for c in mine]
    kernel = functools.partial(place_kernel, per=per, total=total)
    (out,) = call(
        kernel,
        [((2 * chips * chunk.shape[0], chunk.shape[1]), f32)],
        (at, wanted, *mine, *theirs),
        [SM] + [VM] * (1 + 2 * chips),
    )
    return out


def body(
    quot_ids,
    rem_ids,
    lengths,
    log_decay,
    quot_table,
    rem_table,
    w_query,
    w_key,
    w_value,
    w_out,
    cotangent,
):
    users, block = quot_ids.shape
    rows_all, width = quot_table.shape
    heads = log_decay.shape[1]
    size = width // heads
    shards = lax.axis_size("user")
    peers = lax.axis_size("hist")
    rows_own = rem_table.shape[0]
    cap = 2 * block // shards
    per = users * cap
    slots = shards * per
    scale = 1.0 / math.sqrt(size * block * peers)
    at = lax.axis_index("hist").astype(i32).reshape(1)
    lanes = (per // 128 + 1) * 128

    requests, slot = call(
        functools.partial(request_kernel, rows_own=rows_own, cap=cap),
        [((shards, 1, lanes), i32), ((8, block), i32)],
        (lengths, rem_ids),
        [SM, VM],
    )
    wanted = exchange(requests, "user")
    quot_emb, dmixed = call(
        quotient_kernel,
        [((users * block, width), bf16)] * 2,
        (lengths, at, quot_ids, quot_table, cotangent, w_out),
        [SM, SM, VM, VM, VM, VM],
    )
    (found,) = call(
        functools.partial(answer_kernel, per=per),
        [((slots, width), bf16)],
        (wanted, rem_table),
        scratch=[pltpu.VMEM((slots, rows_own), bf16)],
    )
    answered = exchange(found.reshape(shards, per, width), "user").reshape(slots, width)
    rem_emb, q, k, v, payload = call(
        project_kernel,
        [((users * block, width), bf16)] * 4 + [((peers, users * size + 16, width), bf16)],
        (at, answered, slot, quot_emb, dmixed, log_decay, w_query, w_key, w_value),
        [SM] + [VM] * 8,
    )
    states = exchange(payload, "hist")
    mixed, dq, dk, dv = call(
        functools.partial(within_kernel, scale=scale),
        [((users * block, width), f32)] * 4,
        (q, k, v, dmixed, log_decay),
    )
    output, rem_send, keep, give = call(
        functools.partial(gradient_kernel, scale=scale),
        [
            ((users, block, width), bf16),
            ((slots, width), bf16),
            ((rows_all // 2, width), f32),
            ((rows_all // 2, width), bf16),
        ],
        (
            at,
            states,
            mixed,
            dq,
            dk,
            dv,
            q,
            k,
            v,
            dmixed,
            log_decay,
            w_query,
            w_key,
            w_value,
            w_out,
            rem_emb,
            quot_emb,
            slot,
            quot_ids,
        ),
        [SM] + [VM] * 18,
    )
    rem_back = exchange(rem_send.reshape(shards, per, width), "user").reshape(slots, width)
    quot_sum = reduced(at, keep, give)
    quot_back = exchange(quot_sum.reshape(shards, -1, width), "user")
    keep, give = call(
        functools.partial(collect_kernel, per=per),
        [((rows_own // 2, width), f32), ((rows_own // 2, width), bf16)],
        (at, wanted, rem_back),
        [SM, VM, VM],
    )
    rem_sum = reduced(at, keep, give)
    quot_sum = added(quot_back)
    quot_sum = exchange(jnp.broadcast_to(quot_sum, (shards,) + quot_sum.shape), "user")
    total = float(users * shards * block * peers)
    rem_grad = gathered(at, wanted, rem_sum, per, total)
    quot_grad = gathered(at, wanted, quot_sum.reshape(-1, width), per, total)
    return (output, quot_grad, rem_grad)


def solution(mesh):
    return jax.shard_map(
        body,
        mesh=mesh,
        in_specs=(
            P("user", "hist"),
            P("user", "hist"),
            P("user"),
            P("user", None, "hist"),
            P(),
            P("user", None),
            P(),
            P(),
            P(),
            P(),
            P("user", "hist", None),
        ),
        out_specs=(P("user", "hist", None), P(), P("user", None)),
        check_vma=False,
    )
```

```python
import functools
import math

import jax
import jax.numpy as jnp
from jax import lax
from jax.experimental import pallas as pl
from jax.experimental.pallas import tpu as pltpu
from jax.sharding import PartitionSpec as P

f32 = jnp.float32
bf16 = jnp.bfloat16
i32 = jnp.int32
FULL = 62
MOST = 60
EXACT = lax.Precision.HIGHEST
VM = pl.BlockSpec(memory_space=pltpu.VMEM)
SM = pl.BlockSpec(memory_space=pltpu.SMEM)
HB = pl.BlockSpec(memory_space=pltpu.HBM)

NN = (((1,), (0,)), ((), ()))
NT = (((1,), (1,)), ((), ()))
TN = (((0,), (0,)), ((), ()))


def dot(a, b, dims=NN, precision=None):
    return lax.dot_general(a, b, dims, preferred_element_type=f32, precision=precision)


def iota(shape, dim):
    return lax.broadcasted_iota(i32, shape, dim)


def where_bf16(mask, a):
    return jnp.where(mask, a, 0.0).astype(bf16)


def halves(whole):
    return (whole >> 4).astype(f32), (whole & 15).astype(f32)


def spread_column(row):
    n = row.shape[1]
    diagonal = iota((n, n), 0) == iota((n, n), 1)
    high, low = halves(row)
    ones = jnp.ones((n, 128), bf16)
    column = 16.0 * dot(where_bf16(diagonal, high), ones) + dot(where_bf16(diagonal, low), ones)
    return column.astype(i32)


def tiled_match(column, width):
    n = column.shape[0]
    lanes = iota((n, 128), 1)
    parts = [where_bf16(column == lanes + j * 128, 1.0) for j in range(width // 128)]
    return jnp.concatenate(parts, axis=1)


def begin(pairs, arrived, at=0):
    copies = [
        pltpu.make_async_copy(source, target, arrived.at[at + i])
        for i, (source, target) in enumerate(pairs)
    ]
    for copy in copies:
        copy.start()
    return copies


def finish(copies):
    for copy in copies:
        copy.wait()


def dma(n):
    return pltpu.SemaphoreType.DMA((n,))


def call(kernel, outs, args, specs=None, scratch=(), out_specs=None, limit=16):
    return pl.pallas_call(
        kernel,
        out_shape=tuple(jax.ShapeDtypeStruct(s, d) for s, d in outs),
        in_specs=specs if specs is not None else [VM] * len(args),
        out_specs=tuple(out_specs if out_specs is not None else (VM for _ in outs)),
        scratch_shapes=list(scratch),
        compiler_params=pltpu.CompilerParams(vmem_limit_bytes=limit * 1024 * 1024),
    )(*args)


def request_kernel(
    len_ref, ids_hbm, out_ref, slot_ref, ids_ref, arrived, *, rows_own, cap
):
    copies = begin([(ids_hbm, ids_ref)], arrived)
    users, block = ids_ref.shape
    shards, _, lanes = out_ref.shape
    shift = rows_own.bit_length() - 1
    earlier = where_bf16(iota((block, block), 0) < iota((block, block), 1), 1.0)
    place = iota((lanes, block), 0)
    finish(copies)
    total = jnp.zeros((shards, lanes), f32)
    count = jnp.int32(0)
    slot_ref[...] = jnp.zeros_like(slot_ref)
    for u in range(users):
        ids = ids_ref[u : u + 1, :]
        owner = ids >> shift
        named = iota((shards, block), 0) == owner
        named_16 = where_bf16(named, 1.0)
        before = dot(named_16, earlier)
        rank = jnp.sum(jnp.where(named, before, 0.0), axis=0, keepdims=True).astype(i32)
        high, low = halves((ids & (rows_own - 1)) + 1)
        chosen = place == rank + u * cap
        total = total + 16.0 * dot(named_16, where_bf16(chosen, high), NT)
        total = total + dot(named_16, where_bf16(chosen, low), NT)
        slot_ref[u : u + 1, :] = (owner * users + u) * cap + rank
        count = count + len_ref[u]
    wanted = jnp.where(iota((shards, lanes), 1) == users * cap, count, total.astype(i32))
    out_ref[:, 0, :] = wanted


def answer_kernel(
    wanted_ref, table_hbm, out_hbm, hot_ref, table_ref, out_ref, arrived, *, per
):
    copies = begin([(table_hbm, table_ref)], arrived)
    shards, _, lanes = wanted_ref.shape
    slots = shards * per
    rows = table_ref.shape[0]
    wanted = jnp.where(iota((shards, lanes), 1) < per, wanted_ref[:, 0, :], 0)
    high, low = halves(wanted)
    repeat = where_bf16(iota((slots, shards), 0) // per == iota((slots, shards), 1), 1.0)
    own = iota((slots, lanes), 0) % per == iota((slots, lanes), 1)
    ones = jnp.ones((lanes, 128), bf16)
    high = dot(where_bf16(own, dot(repeat, high.astype(bf16))), ones)
    low = dot(where_bf16(own, dot(repeat, low.astype(bf16))), ones)
    column = (16.0 * high + low).astype(i32) - 1
    spot = iota((slots, 128), 1)
    for j in range(rows // 128):
        hot_ref[:, j * 128 : (j + 1) * 128] = where_bf16(column == spot + j * 128, 1.0)
    finish(copies)
    copies = []
    part = slots // 4
    for j in range(4):
        at = slice(j * part, (j + 1) * part)
        out_ref[at, :] = dot(hot_ref[at, :], table_ref[...]).astype(bf16)
        copies += begin([(out_ref.at[at, :], out_hbm.at[at, :])], arrived, 1 + j)
    finish(copies)


def quotient_kernel(
    len_ref,
    at_ref,
    ids_ref,
    table_ref,
    cot_ref,
    decay_ref,
    w_out_ref,
    quot_ref,
    dmixed_ref,
    wide_ref,
):
    users, block = ids_ref.shape
    heads = decay_ref.shape[1]
    rows, width = table_ref.shape
    for u in range(users):
        at = slice(u * block, (u + 1) * block)
        hot = tiled_match(spread_column(ids_ref[u : u + 1, :]), rows)
        quot_ref[at, :] = dot(hot, table_ref[...]).astype(bf16)
        valid = at_ref[0] * block + iota((block, width), 0) < len_ref[u]
        masked = jnp.where(valid, cot_ref[u].astype(f32), 0.0).astype(bf16)
        dmixed_ref[at, :] = dot(masked, w_out_ref[...], NT).astype(bf16)
        _, columns = decays(decay_ref[u], width)
        wide_ref[at, :] = over_heads(columns, heads, width)


def decays(log_decay, width):
    heads, block = log_decay.shape
    upper = jnp.where(iota((block, block), 0) <= iota((block, block), 1), 1.0, 0.0)
    lower = jnp.where(iota((block, block), 0) >= iota((block, block), 1), 1.0, 0.0)
    padded = jnp.concatenate([log_decay, jnp.zeros((8 - heads, block), f32)], axis=0)
    rows = dot(padded, upper, precision=EXACT)
    columns = dot(lower, padded, NT, precision=EXACT)
    return rows, columns


def over_heads(columns, heads, width):
    n = columns.shape[0]
    head_of = iota((n, width), 1) // (width // heads)
    wide = jnp.broadcast_to(columns[:, 0:1], (n, width))
    for h in range(1, heads):
        wide = jnp.where(head_of == h, jnp.broadcast_to(columns[:, h : h + 1], (n, width)), wide)
    return wide


def diagonal_heads(square, heads):
    width = square.shape[1]
    size = width // heads
    head_of = iota((size, width), 1) // size
    out = square[0:size, :]
    for h in range(1, heads):
        out = jnp.where(head_of == h, square[h * size : (h + 1) * size, :], out)
    return out


def block_diagonal(state, heads):
    size, width = state.shape
    head_of = iota((size, width), 1) // (width // heads)
    return jnp.concatenate([where_bf16(head_of == h, state) for h in range(heads)], axis=0)


def project_kernel(
    at_ref,
    slot_hbm,
    answered_ref,
    quot_hbm,
    wq_hbm,
    wk_hbm,
    wv_hbm,
    wide_hbm,
    dmixed_hbm,
    rem_hbm,
    payload_hbm,
    slot_ref,
    quot_ref,
    wq_ref,
    wk_ref,
    wv_ref,
    wide_ref,
    dmixed_ref,
    rem_ref,
    states_ref,
    arrived,
    *,
    users,
    heads,
):
    slots, width = answered_ref.shape
    block = quot_ref.shape[0] // users
    peers = payload_hbm.shape[0]
    size = width // heads
    me = at_ref[0]
    ends = []
    copies = begin(
        (
            (slot_hbm, slot_ref),
            (quot_hbm, quot_ref),
            (wq_hbm, wq_ref),
            (wk_hbm, wk_ref),
            (wv_hbm, wv_ref),
            (wide_hbm, wide_ref),
            (dmixed_hbm, dmixed_ref),
        ),
        arrived,
    )
    finish(copies[:1])
    hot = [tiled_match(spread_column(slot_ref[u : u + 1, :]), slots) for u in range(users)]
    finish(copies[1:])
    copies = []
    for u in range(users):
        at = slice(u * block, (u + 1) * block)
        rem_ref[at, :] = dot(hot[u], answered_ref[...]).astype(bf16)
        copies += begin([(rem_ref.at[at, :], rem_hbm.at[at, :])], arrived, u)
        embedded = (quot_ref[at, :].astype(f32) * rem_ref[at, :].astype(f32)).astype(bf16)
        q = dot(embedded, wq_ref[...]).astype(bf16)
        k = dot(embedded, wk_ref[...]).astype(bf16)
        v = dot(embedded, wv_ref[...]).astype(bf16)
        wide = wide_ref[at, :]
        end = wide[block - 1 : block, :]
        ends.append(end)
        falling = (k.astype(f32) * jnp.exp(end - wide)).astype(bf16)
        growing = (q.astype(f32) * jnp.exp(wide)).astype(bf16)
        state = diagonal_heads(dot(falling, v, TN), heads).astype(bf16)
        grad = diagonal_heads(dot(growing, dmixed_ref[at, :], TN), heads).astype(bf16)
        states_ref[0, u * size : (u + 1) * size, :] = state
        states_ref[1, u * size : (u + 1) * size, :] = grad
    rows = iota((16, width), 0)
    tail = jnp.zeros((16, width), f32)
    for u in range(users):
        left = ends[u]
        for part in range(3):
            piece = left.astype(bf16).astype(f32)
            left = left - piece
            tail = jnp.where(rows == part * users + u, piece, tail)
    tail = tail.astype(bf16)
    states_ref[0, users * size :, :] = tail
    states_ref[1, users * size :, :] = tail
    which = [jnp.where(peer > me, 0, 1) for peer in range(peers)]
    pairs = [(states_ref.at[which[peer]], payload_hbm.at[peer]) for peer in range(peers)]
    finish(copies + begin(pairs, arrived, users))


def within_kernel(
    quot_ref,
    rem_ref,
    dmixed_ref,
    decay_ref,
    wq_ref,
    wk_ref,
    wv_ref,
    out_hbm,
    out_ref,
    arrived,
    *,
    scale,
):
    users, heads, block = decay_ref.shape
    width = quot_ref.shape[1]
    copies = []
    head_of = iota((block, width), 1) // (width // heads)
    lower_tri = iota((block, block), 0) >= iota((block, block), 1)
    for u in range(users):
        at = slice(u * block, (u + 1) * block)
        embedded = (quot_ref[at, :].astype(f32) * rem_ref[at, :].astype(f32)).astype(bf16)
        q = dot(embedded, wq_ref[...]).astype(bf16)
        k = dot(embedded, wk_ref[...]).astype(bf16)
        v = dot(embedded, wv_ref[...]).astype(bf16)
        dmixed = dmixed_ref[at, :]
        rows, columns = decays(decay_ref[u], width)
        mixed = jnp.zeros((block, width), f32)
        dq = jnp.zeros((block, width), f32)
        dk = jnp.zeros((block, width), f32)
        dv = jnp.zeros((block, width), f32)
        zero = jnp.zeros((), bf16)
        for h in range(heads):
            own = head_of == h
            q_h = jnp.where(own, q, zero)
            k_h = jnp.where(own, k, zero)
            v_h = jnp.where(own, v, zero)
            d_h = jnp.where(own, dmixed, zero)
            gap = columns[:, h : h + 1] - rows[h : h + 1, :]
            mask = jnp.where(lower_tri, scale * jnp.exp(jnp.minimum(gap, 0.0)), 0.0)
            weights = (dot(q_h, k, NT) * mask).astype(bf16)
            dweights = (dot(d_h, v, NT) * mask).astype(bf16)
            mixed = mixed + dot(weights, v_h)
            dq = dq + dot(dweights, k_h)
            dk = dk + dot(dweights, q_h, TN)
            dv = dv + dot(weights, d_h, TN)
        for i, part in enumerate((mixed, dq, dk, dv)):
            out_ref[i, at, :] = part
        copies += begin([(out_ref.at[:, at, :], out_hbm.at[:, at, :])], arrived, u)
    finish(copies)


def sum_half(ids, terms, owner, out_ref):
    half = out_ref.shape[0]
    chunk = min(256, half)
    spot = iota((chunk, ids.shape[1]), 0)
    near = ids - owner * half
    for j in range(half // chunk):
        hot = where_bf16(spot + j * chunk == near, 1.0)
        out_ref[j * chunk : (j + 1) * chunk, :] = dot(hot, terms).astype(out_ref.dtype)


def gradient_kernel(
    at_ref,
    payload_ref,
    within_hbm,
    dmixed_hbm,
    wide_hbm,
    rem_hbm,
    quot_hbm,
    slot_hbm,
    ids_hbm,
    wq_hbm,
    wk_hbm,
    wv_hbm,
    w_out_hbm,
    out_hbm,
    rem_send_hbm,
    keep_hbm,
    give_hbm,
    within_ref,
    dmixed_ref,
    wide_ref,
    rem_ref,
    quot_ref,
    slot_ref,
    ids_ref,
    wq_ref,
    wk_ref,
    wv_ref,
    w_out_ref,
    out_ref,
    rem_send_ref,
    keep_ref,
    give_ref,
    arrived,
    *,
    scale,
    heads,
):
    users, block = ids_ref.shape
    width = quot_ref.shape[1]
    copies = begin(
        (
            (quot_hbm, quot_ref),
            (rem_hbm, rem_ref),
            (wq_hbm, wq_ref),
            (wk_hbm, wk_ref),
            (wv_hbm, wv_ref),
            (wide_hbm, wide_ref),
            (dmixed_hbm, dmixed_ref),
            (w_out_hbm, w_out_ref),
            (within_hbm, within_ref),
            (slot_hbm, slot_ref),
            (ids_hbm, ids_ref),
        ),
        arrived,
    )
    peers = payload_ref.shape[0]
    size = width // heads
    slots = rem_send_ref.shape[0]
    me = at_ref[0]
    carried = []
    for u in range(users):
        ends = []
        for peer in range(peers):
            tail = payload_ref[peer, users * size :, :].astype(f32)
            ends.append(
                tail[u : u + 1, :]
                + tail[users + u : users + u + 1, :]
                + tail[2 * users + u : 2 * users + u + 1, :]
            )
        entering = jnp.zeros((size, width), f32)
        for peer in range(peers):
            part = payload_ref[peer, u * size : (u + 1) * size, :].astype(f32)
            linked = jnp.exp(ends[peer]) * entering + part
            entering = jnp.where(peer < me, linked, entering)
        leaving = jnp.zeros((size, width), f32)
        for peer in reversed(range(peers)):
            part = payload_ref[peer, u * size : (u + 1) * size, :].astype(f32)
            linked = jnp.exp(ends[peer]) * leaving + part
            leaving = jnp.where(peer > me, linked, leaving)
        carried.append((block_diagonal(entering, heads), block_diagonal(leaving, heads)))
    finish(copies)
    copies = []
    rem_terms, quot_terms = [], []
    for u in range(users):
        at = slice(u * block, (u + 1) * block)
        entering, leaving = carried[u]
        embedded = (quot_ref[at, :].astype(f32) * rem_ref[at, :].astype(f32)).astype(bf16)
        q = dot(embedded, wq_ref[...]).astype(bf16)
        k = dot(embedded, wk_ref[...]).astype(bf16)
        v = dot(embedded, wv_ref[...]).astype(bf16)
        dmixed = dmixed_ref[at, :]
        wide = wide_ref[at, :]
        growth = scale * jnp.exp(wide)
        falloff = scale * jnp.exp(wide[block - 1 : block, :] - wide)
        mixed = (within_ref[0, at, :] + growth * dot(q, entering)).astype(bf16)
        out_ref[u] = dot(mixed, w_out_ref[...]).astype(bf16)
        copies += begin([(out_ref.at[u], out_hbm.at[u])], arrived, u)
        dq = (within_ref[1, at, :] + growth * dot(dmixed, entering, NT)).astype(bf16)
        dk = (within_ref[2, at, :] + falloff * dot(v, leaving, NT)).astype(bf16)
        dv = (within_ref[3, at, :] + falloff * dot(k, leaving)).astype(bf16)
        dembedded = dot(dq, wq_ref[...], NT) + dot(dk, wk_ref[...], NT) + dot(dv, wv_ref[...], NT)
        rem_terms.append((dembedded * quot_ref[at, :].astype(f32)).astype(bf16))
        quot_terms.append((dembedded * rem_ref[at, :].astype(f32)).astype(bf16))
    rem_terms = jnp.concatenate(rem_terms, axis=0)
    quot_terms = jnp.concatenate(quot_terms, axis=0)
    slot = jnp.concatenate([slot_ref[u : u + 1, :] for u in range(users)], axis=1)
    ids = jnp.concatenate([ids_ref[u : u + 1, :] for u in range(users)], axis=1)
    spot = iota((block, users * block), 0)
    for j in range(slots // block):
        hot = where_bf16(spot + j * block == slot, 1.0)
        rem_send_ref[j * block : (j + 1) * block, :] = dot(hot, rem_terms).astype(bf16)
    copies += begin([(rem_send_ref, rem_send_hbm)], arrived, users)
    sum_half(ids, quot_terms, 1 - me % 2, give_ref)
    copies += begin([(give_ref, give_hbm)], arrived, users + 1)
    sum_half(ids, quot_terms, me % 2, keep_ref)
    copies += begin([(keep_ref, keep_hbm)], arrived, users + 2)
    finish(copies)


def collect_kernel(at_ref, wanted_ref, back_ref, keep_ref, give_ref, *, per):
    shards, _, lanes = wanted_ref.shape
    slots = shards * per
    wanted = jnp.where(iota((shards, lanes), 1) < per, wanted_ref[:, 0, :], 0)
    high, low = halves(wanted)
    tile = where_bf16(iota((lanes, slots), 1) % per == iota((lanes, slots), 0), 1.0)
    own = iota((shards, slots), 1) // per == iota((shards, slots), 0)
    high = jnp.sum(jnp.where(own, dot(high.astype(bf16), tile), 0.0), axis=0, keepdims=True)
    low = jnp.sum(jnp.where(own, dot(low.astype(bf16), tile), 0.0), axis=0, keepdims=True)
    row = (16.0 * high + low).astype(i32) - 1
    sum_half(row, back_ref[...], 1 - at_ref[0] % 2, give_ref)
    sum_half(row, back_ref[...], at_ref[0] % 2, keep_ref)


def split_kernel(at_ref, keep_ref, got_ref, *out_refs):
    chips = len(out_refs)
    rows = out_refs[0].shape[0]
    for d, out_ref in enumerate(out_refs):
        base = pl.multiple_of(lax.rem(at_ref[0] // 2 + d, chips) * rows, rows)
        both = keep_ref[pl.ds(base, rows), :] + got_ref[pl.ds(base, rows), :].astype(f32)
        out_ref[...] = both.astype(bf16)


def cut(chunk, shards):
    rows, width = chunk.shape
    lanes = width // 128
    part = rows * lanes // shards
    return [
        chunk[i // lanes * part : (i // lanes + 1) * part, i % lanes * 128 : (i % lanes + 1) * 128]
        for i in range(shards)
    ]


def total_kernel(*refs):
    total = sum((ref[...].astype(f32) for ref in refs[1:-1]), refs[0][...].astype(f32))
    for i, tile in enumerate(cut(total, refs[-1].shape[0])):
        refs[-1][i] = tile.astype(bf16)


def repeat_kernel(tiles_ref, out_ref):
    total = jnp.sum(tiles_ref[...].astype(f32), axis=0).astype(bf16)
    for i in range(out_ref.shape[0]):
        out_ref[i] = total


def place_kernel(at_ref, wanted_ref, *refs, per, total):
    out_hbm, out_ref, arrived = refs[-3:]
    chunks = refs[:-3]
    copies = []
    chips = len(chunks) // 2
    _, rows, width = out_ref.shape
    shards, _, lanes = wanted_ref.shape
    counted = jnp.where(iota((shards, lanes), 1) == per, wanted_ref[:, 0, :], 0)
    ratio = total / jnp.sum(counted.astype(f32), axis=(0, 1), keepdims=True)
    chip, core = at_ref[0] // 2, at_ref[0] % 2
    for other in range(2):
        half = core + other - 2 * core * other
        for d in range(chips):
            spot = half * chips + lax.rem(chip + chips - d, chips)
            base = pl.multiple_of(spot * rows, rows)
            chunk = chunks[other * chips + d]
            n = other * chips + d
            if len(chunk.shape) == 2:
                out_ref[n] = ratio * chunk[...].astype(f32)
            else:
                part = chunk.shape[1]
                for i in range(shards):
                    across = i % (width // 128) * 128
                    down = i // (width // 128) * part
                    tile = ratio * chunk[i].astype(f32)
                    out_ref[n, down : down + part, across : across + 128] = tile
            copies += begin([(out_ref.at[n], out_hbm.at[pl.ds(base, rows), :])], arrived, n)
    finish(copies)


def exchange(array, axis):
    return lax.all_to_all(array, axis, split_axis=0, concat_axis=0, tiled=True)


def to_core(array):
    peers = lax.axis_size("hist")
    return lax.ppermute(array, "hist", [(i, i ^ 1) for i in range(peers)])


def to_chip(array, steps):
    peers = lax.axis_size("hist")
    return lax.ppermute(array, "hist", [(i, (i + 2 * steps) % peers) for i in range(peers)])


def reduced(at, keep, give):
    chips = lax.axis_size("hist") // 2
    rows = keep.shape[0] // chips
    chunks = call(
        split_kernel,
        [((rows, keep.shape[1]), bf16)] * chips,
        (at, keep, to_core(give)),
        [SM, VM, VM],
    )
    return [chunks[0]] + [to_chip(chunks[d], d) for d in range(1, chips)]


def everywhere(chunk):
    chips = lax.axis_size("hist") // 2
    mine = [chunk] + [to_chip(chunk, d) for d in range(1, chips)]
    return mine + [to_core(c) for c in mine]


def placed(at, wanted, chunks, rows, width, per, total):
    kernel = functools.partial(place_kernel, per=per, total=total)
    specs = [SM] + [VM] * (1 + len(chunks))
    n = len(chunks)
    scratch = [pltpu.VMEM((n, rows // n, width), f32), dma(n)]
    args = (at, wanted, *chunks)
    (out,) = call(kernel, [((rows, width), f32)], args, specs, scratch, [HB])
    return out


def body(
    quot_ids,
    rem_ids,
    lengths,
    log_decay,
    quot_table,
    rem_table,
    w_query,
    w_key,
    w_value,
    w_out,
    cotangent,
):
    users, block = quot_ids.shape
    rows_all, width = quot_table.shape
    heads = log_decay.shape[1]
    size = width // heads
    shards = lax.axis_size("user")
    peers = lax.axis_size("hist")
    rows_own = rem_table.shape[0]
    cap = 2 * block // shards
    per = users * cap
    slots = shards * per
    scale = 1.0 / math.sqrt(size * block * peers)
    at = lax.axis_index("hist").astype(i32).reshape(1)
    lanes = (per // 128 + 1) * 128

    requests, slot = call(
        functools.partial(request_kernel, rows_own=rows_own, cap=cap),
        [((shards, 1, lanes), i32), ((8, block), i32)],
        (lengths, rem_ids),
        [SM, HB],
        [pltpu.VMEM((users, block), i32), dma(1)],
        limit=FULL,
    )
    wanted = exchange(requests, "user")
    quot_emb, dmixed, wide = call(
        quotient_kernel,
        [
            ((users * block, width), bf16),
            ((users * block, width), bf16),
            ((users * block, width), f32),
        ],
        (lengths, at, quot_ids, quot_table, cotangent, log_decay, w_out),
        [SM, SM] + [VM] * 5,
        limit=FULL,
    )
    (found,) = call(
        functools.partial(answer_kernel, per=per),
        [((slots, width), bf16)],
        (wanted, rem_table),
        [VM, HB],
        [
            pltpu.VMEM((slots, rows_own), bf16),
            pltpu.VMEM((rows_own, width), bf16),
            pltpu.VMEM((slots, width), bf16),
            dma(5),
        ],
        [HB],
        FULL,
    )
    answered = exchange(found.reshape(shards, per, width), "user").reshape(slots, width)
    events = pltpu.VMEM((users * block, width), bf16)
    square = pltpu.VMEM((width, width), bf16)
    rem_emb, payload = call(
        functools.partial(project_kernel, users=users, heads=heads),
        [((users * block, width), bf16), ((peers, users * size + 16, width), bf16)],
        (at, slot, answered, quot_emb, w_query, w_key, w_value, wide, dmixed),
        [SM, HB, VM] + [HB] * 6,
        [pltpu.VMEM((8, block), i32), events]
        + [square] * 3
        + [pltpu.VMEM((users * block, width), f32), events, events]
        + [pltpu.VMEM((2, users * size + 16, width), bf16), dma(8 + users + peers)],
        [HB, HB],
        MOST,
    )
    states = exchange(payload, "hist")
    parts = (4, users * block, width)
    (within,) = call(
        functools.partial(within_kernel, scale=scale),
        [(parts, f32)],
        (quot_emb, rem_emb, dmixed, log_decay, w_query, w_key, w_value),
        scratch=[pltpu.VMEM(parts, f32), dma(users)],
        out_specs=[HB],
        limit=FULL,
    )
    output, rem_send, keep, give = call(
        functools.partial(gradient_kernel, scale=scale, heads=heads),
        [
            ((users, block, width), bf16),
            ((slots, width), bf16),
            ((rows_all // 2, width), f32),
            ((rows_all // 2, width), bf16),
        ],
        (at, states, within, dmixed, wide, rem_emb, quot_emb, slot, quot_ids)
        + (w_query, w_key, w_value, w_out),
        [SM, VM] + [HB] * 11,
        [pltpu.VMEM(parts, f32), events]
        + [pltpu.VMEM((users * block, width), f32), events, events]
        + [pltpu.VMEM((8, block), i32), pltpu.VMEM((users, block), i32)]
        + [square] * 4
        + [pltpu.VMEM((users, block, width), bf16), pltpu.VMEM((slots, width), bf16)]
        + [pltpu.VMEM((rows_all // 2, width), f32), pltpu.VMEM((rows_all // 2, width), bf16)]
        + [dma(12)],
        [HB] * 4,
        MOST,
    )
    rem_back = exchange(rem_send.reshape(shards, per, width), "user").reshape(slots, width)
    tiles = (shards, rows_all // peers * width // shards // 128, 128)
    (quot_tiles,) = call(total_kernel, [(tiles, bf16)], reduced(at, keep, give))
    rem_back, quot_tiles = lax.optimization_barrier((rem_back, quot_tiles))
    quot_back = exchange(quot_tiles, "user")
    keep, give = call(
        functools.partial(collect_kernel, per=per),
        [((rows_own // 2, width), f32), ((rows_own // 2, width), bf16)],
        (at, wanted, rem_back),
        [SM, VM, VM],
    )
    rem_sum = sum(c.astype(f32) for c in reduced(at, keep, give)).astype(bf16)
    (quot_tiles,) = call(repeat_kernel, [(tiles, bf16)], (quot_back,))
    quot_tiles, rem_sum = lax.optimization_barrier((quot_tiles, rem_sum))
    quot_tiles = exchange(quot_tiles, "user")
    rem_chunks = everywhere(rem_sum)
    quot_tiles, *rem_chunks = lax.optimization_barrier((quot_tiles, *rem_chunks))
    total = float(users * shards * block * peers)
    rem_grad = placed(at, wanted, rem_chunks, rows_own, width, per, total)
    quot_grad = placed(at, wanted, everywhere(quot_tiles), rows_all, width, per, total)
    return (output, quot_grad, rem_grad)


def solution(mesh):
    return jax.shard_map(
        body,
        mesh=mesh,
        in_specs=(
            P("user", "hist"),
            P("user", "hist"),
            P("user"),
            P("user", None, "hist"),
            P(),
            P("user", None),
            P(),
            P(),
            P(),
            P(),
            P("user", "hist", None),
        ),
        out_specs=(P("user", "hist", None), P(), P("user", None)),
        check_vma=False,
    )
```

```python
import functools
import math

import jax
import jax.numpy as jnp
from jax import lax
from jax.experimental import pallas as pl
from jax.experimental.pallas import tpu as pltpu
from jax.sharding import PartitionSpec as P

f32 = jnp.float32
bf16 = jnp.bfloat16
i32 = jnp.int32
FULL = 62
EXACT = lax.Precision.HIGHEST
VM = pl.BlockSpec(memory_space=pltpu.VMEM)
SM = pl.BlockSpec(memory_space=pltpu.SMEM)
HB = pl.BlockSpec(memory_space=pltpu.HBM)

NN = (((1,), (0,)), ((), ()))
NT = (((1,), (1,)), ((), ()))
TN = (((0,), (0,)), ((), ()))


def dot(a, b, dims=NN, precision=None):
    return lax.dot_general(a, b, dims, preferred_element_type=f32, precision=precision)


def iota(shape, dim):
    return lax.broadcasted_iota(i32, shape, dim)


def quotient(a, n):
    return a >> (n.bit_length() - 1) if n & (n - 1) == 0 else a // n


def remainder(a, n):
    return a & (n - 1) if n & (n - 1) == 0 else a % n


def where_bf16(mask, a):
    return jnp.where(mask, a, 0.0).astype(bf16)


def halves(whole):
    return (whole >> 4).astype(f32), (whole & 15).astype(f32)


def spread_column(row):
    n = row.shape[1]
    diagonal = iota((n, n), 0) == iota((n, n), 1)
    high, low = halves(row)
    ones = jnp.ones((n, 128), bf16)
    column = 16.0 * dot(where_bf16(diagonal, high), ones) + dot(where_bf16(diagonal, low), ones)
    return column.astype(i32)


def tiled_match(column, width):
    n = column.shape[0]
    lanes = iota((n, 128), 1)
    parts = [where_bf16(column == lanes + j * 128, 1.0) for j in range(width // 128)]
    return jnp.concatenate(parts, axis=1)


def begin(pairs, arrived, at=0):
    copies = [
        pltpu.make_async_copy(source, target, arrived.at[at + i])
        for i, (source, target) in enumerate(pairs)
    ]
    for copy in copies:
        copy.start()
    return copies


def finish(copies):
    for copy in copies:
        copy.wait()


def dma(n):
    return pltpu.SemaphoreType.DMA((n,))


def call(kernel, outs, args, specs=None, scratch=(), out_specs=None, limit=16):
    return pl.pallas_call(
        kernel,
        out_shape=tuple(jax.ShapeDtypeStruct(s, d) for s, d in outs),
        in_specs=specs if specs is not None else [VM] * len(args),
        out_specs=tuple(out_specs if out_specs is not None else (VM for _ in outs)),
        scratch_shapes=list(scratch),
        compiler_params=pltpu.CompilerParams(vmem_limit_bytes=limit * 1024 * 1024),
    )(*args)


def request_kernel(len_ref, ids_ref, out_ref, slot_ref, *, rows_own, cap):
    users, block = ids_ref.shape
    shards, _, lanes = out_ref.shape
    shift = rows_own.bit_length() - 1
    earlier = where_bf16(iota((block, block), 0) < iota((block, block), 1), 1.0)
    place = iota((lanes, block), 0)
    total = jnp.zeros((shards, lanes), f32)
    count = jnp.int32(0)
    slot_ref[...] = jnp.zeros_like(slot_ref)
    for u in range(users):
        ids = ids_ref[u : u + 1, :]
        owner = ids >> shift
        named = iota((shards, block), 0) == owner
        named_16 = where_bf16(named, 1.0)
        before = dot(named_16, earlier)
        rank = jnp.sum(jnp.where(named, before, 0.0), axis=0, keepdims=True).astype(i32)
        high, low = halves((ids & (rows_own - 1)) + 1)
        chosen = place == rank + u * cap
        total = total + 16.0 * dot(named_16, where_bf16(chosen, high), NT)
        total = total + dot(named_16, where_bf16(chosen, low), NT)
        slot_ref[u : u + 1, :] = (owner * users + u) * cap + rank
        count = count + len_ref[u]
    wanted = jnp.where(iota((shards, lanes), 1) == users * cap, count, total.astype(i32))
    out_ref[:, 0, :] = wanted


def answer_kernel(
    wanted_hbm, table_hbm, out_hbm, wanted_ref, table_ref, out_ref, arrived, *, per
):
    shards, _, lanes = wanted_ref.shape
    copies = begin(((wanted_hbm, wanted_ref), (table_hbm, table_ref)), arrived)
    parts = 4
    group = shards // parts
    slots = group * per
    rows = table_ref.shape[0]
    repeat = where_bf16(quotient(iota((slots, group), 0), per) == iota((slots, group), 1), 1.0)
    own = remainder(iota((slots, lanes), 0), per) == iota((slots, lanes), 1)
    ones = jnp.ones((lanes, 128), bf16)
    finish(copies[:1])
    wanted = jnp.where(iota((shards, lanes), 1) < per, wanted_ref[:, 0, :], 0)
    stores = []
    for j in range(parts):
        high, low = halves(wanted[j * group : (j + 1) * group, :])
        high = dot(where_bf16(own, dot(repeat, high.astype(bf16))), ones)
        low = dot(where_bf16(own, dot(repeat, low.astype(bf16))), ones)
        column = (16.0 * high + low).astype(i32) - 1
        hot = tiled_match(column, rows)
        if j == 0:
            finish(copies[1:])
        at = slice(j * slots, (j + 1) * slots)
        out_ref[at, :] = dot(hot, table_ref[...]).astype(bf16)
        stores += begin([(out_ref.at[at, :], out_hbm.at[at, :])], arrived, 2 + j)
    finish(stores)


def quotient_kernel(
    len_ref,
    at_ref,
    ids_ref,
    table_ref,
    cot_ref,
    decay_ref,
    w_out_ref,
    quot_ref,
    dmixed_ref,
    wide_ref,
):
    users, block = ids_ref.shape
    heads = decay_ref.shape[1]
    rows, width = table_ref.shape
    for u in range(users):
        at = slice(u * block, (u + 1) * block)
        hot = tiled_match(spread_column(ids_ref[u : u + 1, :]), rows)
        quot_ref[at, :] = dot(hot, table_ref[...]).astype(bf16)
        valid = at_ref[0] * block + iota((block, width), 0) < len_ref[u]
        masked = jnp.where(valid, cot_ref[u].astype(f32), 0.0).astype(bf16)
        dmixed_ref[at, :] = dot(masked, w_out_ref[...], NT).astype(bf16)
        _, columns = decays(decay_ref[u], width)
        wide_ref[at, :] = over_heads(columns, heads, width)


def decays(log_decay, width):
    heads, block = log_decay.shape
    upper = jnp.where(iota((block, block), 0) <= iota((block, block), 1), 1.0, 0.0)
    lower = jnp.where(iota((block, block), 0) >= iota((block, block), 1), 1.0, 0.0)
    padded = jnp.concatenate([log_decay, jnp.zeros((8 - heads, block), f32)], axis=0)
    rows = dot(padded, upper, precision=EXACT)
    columns = dot(lower, padded, NT, precision=EXACT)
    return rows, columns


def over_heads(columns, heads, width):
    n = columns.shape[0]
    head_of = quotient(iota((n, width), 1), width // heads)
    wide = jnp.broadcast_to(columns[:, 0:1], (n, width))
    for h in range(1, heads):
        wide = jnp.where(head_of == h, jnp.broadcast_to(columns[:, h : h + 1], (n, width)), wide)
    return wide


def diagonal_heads(square, heads):
    width = square.shape[1]
    size = width // heads
    head_of = quotient(iota((size, width), 1), size)
    out = square[0:size, :]
    for h in range(1, heads):
        out = jnp.where(head_of == h, square[h * size : (h + 1) * size, :], out)
    return out


def block_diagonal(state, heads):
    size, width = state.shape
    head_of = quotient(iota((size, width), 1), width // heads)
    return jnp.concatenate([where_bf16(head_of == h, state) for h in range(heads)], axis=0)


def project_kernel(
    at_ref,
    slot_hbm,
    answered_hbm,
    quot_hbm,
    wq_hbm,
    wk_hbm,
    wv_hbm,
    wide_hbm,
    dmixed_hbm,
    rem_hbm,
    payload_hbm,
    slot_ref,
    answered_ref,
    quot_ref,
    wq_ref,
    wk_ref,
    wv_ref,
    wide_ref,
    dmixed_ref,
    rem_ref,
    states_ref,
    arrived,
    *,
    users,
    heads,
):
    slots, width = answered_ref.shape
    block = quot_ref.shape[0] // users
    peers = payload_hbm.shape[0]
    size = width // heads
    me = at_ref[0]
    ends = []
    copies = begin(
        (
            (slot_hbm, slot_ref),
            (answered_hbm, answered_ref),
            (quot_hbm, quot_ref),
            (wq_hbm, wq_ref),
            (wk_hbm, wk_ref),
            (wv_hbm, wv_ref),
            (wide_hbm, wide_ref),
            (dmixed_hbm, dmixed_ref),
        ),
        arrived,
    )
    finish(copies[:1])
    hot = [tiled_match(spread_column(slot_ref[u : u + 1, :]), slots) for u in range(users)]
    finish(copies[1:6])
    waits, copies = copies[6:], []
    for u in range(users):
        at = slice(u * block, (u + 1) * block)
        rem_ref[at, :] = dot(hot[u], answered_ref[...]).astype(bf16)
        copies += begin([(rem_ref.at[at, :], rem_hbm.at[at, :])], arrived, 8 + u)
        embedded = (quot_ref[at, :].astype(f32) * rem_ref[at, :].astype(f32)).astype(bf16)
        q = dot(embedded, wq_ref[...]).astype(bf16)
        k = dot(embedded, wk_ref[...]).astype(bf16)
        v = dot(embedded, wv_ref[...]).astype(bf16)
        if u == 0:
            finish(waits)
        wide = wide_ref[at, :]
        end = wide[block - 1 : block, :]
        ends.append(end)
        falling = (k.astype(f32) * jnp.exp(end - wide)).astype(bf16)
        growing = (q.astype(f32) * jnp.exp(wide)).astype(bf16)
        state = diagonal_heads(dot(falling, v, TN), heads).astype(bf16)
        grad = diagonal_heads(dot(growing, dmixed_ref[at, :], TN), heads).astype(bf16)
        states_ref[0, u * size : (u + 1) * size, :] = state
        states_ref[1, u * size : (u + 1) * size, :] = grad
    rows = iota((16, width), 0)
    tail = jnp.zeros((16, width), f32)
    for u in range(users):
        left = ends[u]
        for part in range(3):
            piece = left.astype(bf16).astype(f32)
            left = left - piece
            tail = jnp.where(rows == part * users + u, piece, tail)
    tail = tail.astype(bf16)
    states_ref[0, users * size :, :] = tail
    states_ref[1, users * size :, :] = tail
    which = [jnp.where(peer > me, 0, 1) for peer in range(peers)]
    pairs = [(states_ref.at[which[peer]], payload_hbm.at[peer]) for peer in range(peers)]
    finish(copies + begin(pairs, arrived, 8 + users))


def within_kernel(
    quot_ref,
    rem_ref,
    dmixed_ref,
    decay_ref,
    wq_ref,
    wk_ref,
    wv_ref,
    out_hbm,
    out_ref,
    arrived,
    *,
    scale,
):
    users, heads, block = decay_ref.shape
    width = quot_ref.shape[1]
    copies = []
    head_of = quotient(iota((block, width), 1), width // heads)
    lower_tri = iota((block, block), 0) >= iota((block, block), 1)
    for u in range(users):
        at = slice(u * block, (u + 1) * block)
        embedded = (quot_ref[at, :].astype(f32) * rem_ref[at, :].astype(f32)).astype(bf16)
        q = dot(embedded, wq_ref[...]).astype(bf16)
        k = dot(embedded, wk_ref[...]).astype(bf16)
        v = dot(embedded, wv_ref[...]).astype(bf16)
        dmixed = dmixed_ref[at, :]
        rows, columns = decays(decay_ref[u], width)
        mixed = jnp.zeros((block, width), f32)
        dq = jnp.zeros((block, width), f32)
        dk = jnp.zeros((block, width), f32)
        dv = jnp.zeros((block, width), f32)
        zero = jnp.zeros((), bf16)
        for h in range(heads):
            own = head_of == h
            q_h = jnp.where(own, q, zero)
            k_h = jnp.where(own, k, zero)
            v_h = jnp.where(own, v, zero)
            d_h = jnp.where(own, dmixed, zero)
            gap = columns[:, h : h + 1] - rows[h : h + 1, :]
            mask = jnp.where(lower_tri, scale * jnp.exp(jnp.minimum(gap, 0.0)), 0.0)
            weights = (dot(q_h, k, NT) * mask).astype(bf16)
            dweights = (dot(d_h, v, NT) * mask).astype(bf16)
            mixed = mixed + dot(weights, v_h)
            dq = dq + dot(dweights, k_h)
            dk = dk + dot(dweights, q_h, TN)
            dv = dv + dot(weights, d_h, TN)
        for i, part in enumerate((mixed, dq, dk, dv)):
            out_ref[i, at, :] = part
        copies += begin([(out_ref.at[:, at, :], out_hbm.at[:, at, :])], arrived, u)
    finish(copies)


def sum_half(ids, terms, owner, out_ref):
    half = out_ref.shape[0]
    chunk = min(256, half)
    spot = iota((chunk, ids.shape[1]), 0)
    near = ids - owner * half
    for j in range(half // chunk):
        hot = where_bf16(spot + j * chunk == near, 1.0)
        out_ref[j * chunk : (j + 1) * chunk, :] = dot(hot, terms).astype(out_ref.dtype)


def gradient_kernel(
    at_ref,
    payload_hbm,
    within_hbm,
    dmixed_hbm,
    wide_hbm,
    rem_hbm,
    quot_hbm,
    slot_hbm,
    ids_hbm,
    wq_hbm,
    wk_hbm,
    wv_hbm,
    w_out_hbm,
    out_hbm,
    rem_send_hbm,
    keep_hbm,
    give_hbm,
    payload_ref,
    within_ref,
    dmixed_ref,
    wide_ref,
    rem_ref,
    quot_ref,
    slot_ref,
    ids_ref,
    wq_ref,
    wk_ref,
    wv_ref,
    w_out_ref,
    out_ref,
    rem_send_ref,
    keep_ref,
    give_ref,
    arrived,
    *,
    scale,
    heads,
):
    users, block = ids_ref.shape
    width = quot_ref.shape[1]
    copies = begin(
        (
            (payload_hbm, payload_ref),
            (quot_hbm, quot_ref),
            (rem_hbm, rem_ref),
            (wq_hbm, wq_ref),
            (wk_hbm, wk_ref),
            (wv_hbm, wv_ref),
            (wide_hbm, wide_ref),
            (dmixed_hbm, dmixed_ref),
            (w_out_hbm, w_out_ref),
            (slot_hbm, slot_ref),
            (ids_hbm, ids_ref),
        ),
        arrived,
    )
    waits = []
    for u in range(users):
        at = slice(u * block, (u + 1) * block)
        waits += begin([(within_hbm.at[:, at, :], within_ref.at[:, at, :])], arrived, 11 + u)
    finish(copies[:1])
    peers = payload_ref.shape[0]
    size = width // heads
    slots = rem_send_ref.shape[0]
    me = at_ref[0]
    carried = []
    for u in range(users):
        ends = []
        for peer in range(peers):
            tail = payload_ref[peer, users * size :, :].astype(f32)
            ends.append(
                tail[u : u + 1, :]
                + tail[users + u : users + u + 1, :]
                + tail[2 * users + u : 2 * users + u + 1, :]
            )
        entering = jnp.zeros((size, width), f32)
        for peer in range(peers):
            part = payload_ref[peer, u * size : (u + 1) * size, :].astype(f32)
            linked = jnp.exp(ends[peer]) * entering + part
            entering = jnp.where(peer < me, linked, entering)
        leaving = jnp.zeros((size, width), f32)
        for peer in reversed(range(peers)):
            part = payload_ref[peer, u * size : (u + 1) * size, :].astype(f32)
            linked = jnp.exp(ends[peer]) * leaving + part
            leaving = jnp.where(peer > me, linked, leaving)
        carried.append((block_diagonal(entering, heads), block_diagonal(leaving, heads)))
    finish(copies[1:])
    copies = []
    rem_terms, quot_terms = [], []
    for u in range(users):
        at = slice(u * block, (u + 1) * block)
        entering, leaving = carried[u]
        embedded = (quot_ref[at, :].astype(f32) * rem_ref[at, :].astype(f32)).astype(bf16)
        q = dot(embedded, wq_ref[...]).astype(bf16)
        k = dot(embedded, wk_ref[...]).astype(bf16)
        v = dot(embedded, wv_ref[...]).astype(bf16)
        dmixed = dmixed_ref[at, :]
        wide = wide_ref[at, :]
        finish(waits[u : u + 1])
        growth = scale * jnp.exp(wide)
        falloff = scale * jnp.exp(wide[block - 1 : block, :] - wide)
        mixed = (within_ref[0, at, :] + growth * dot(q, entering)).astype(bf16)
        out_ref[u] = dot(mixed, w_out_ref[...]).astype(bf16)
        copies += begin([(out_ref.at[u], out_hbm.at[u])], arrived, 11 + users + u)
        dq = (within_ref[1, at, :] + growth * dot(dmixed, entering, NT)).astype(bf16)
        dk = (within_ref[2, at, :] + falloff * dot(v, leaving, NT)).astype(bf16)
        dv = (within_ref[3, at, :] + falloff * dot(k, leaving)).astype(bf16)
        dembedded = dot(dq, wq_ref[...], NT) + dot(dk, wk_ref[...], NT) + dot(dv, wv_ref[...], NT)
        rem_terms.append((dembedded * quot_ref[at, :].astype(f32)).astype(bf16))
        quot_terms.append((dembedded * rem_ref[at, :].astype(f32)).astype(bf16))
    rem_terms = jnp.concatenate(rem_terms, axis=0)
    quot_terms = jnp.concatenate(quot_terms, axis=0)
    slot = jnp.concatenate([slot_ref[u : u + 1, :] for u in range(users)], axis=1)
    ids = jnp.concatenate([ids_ref[u : u + 1, :] for u in range(users)], axis=1)
    spot = iota((block, users * block), 0)
    n = 11 + 2 * users
    for j in range(slots // block):
        hot = where_bf16(spot + j * block == slot, 1.0)
        at = slice(j * block, (j + 1) * block)
        rem_send_ref[at, :] = dot(hot, rem_terms).astype(bf16)
        copies += begin([(rem_send_ref.at[at, :], rem_send_hbm.at[at, :])], arrived, n + j)
    n += slots // block
    for ref, hbm, owner in ((give_ref, give_hbm, 1 - me % 2), (keep_ref, keep_hbm, me % 2)):
        half = ref.shape[0]
        near = ids - owner * half
        for j in range(half // block):
            hot = where_bf16(spot + j * block == near, 1.0)
            at = slice(j * block, (j + 1) * block)
            ref[at, :] = dot(hot, quot_terms).astype(bf16)
            copies += begin([(ref.at[at, :], hbm.at[at, :])], arrived, n)
            n += 1
    finish(copies)


def collect_kernel(at_ref, wanted_ref, back_ref, keep_ref, give_ref, *, per):
    shards, _, lanes = wanted_ref.shape
    slots = shards * per
    wanted = jnp.where(iota((shards, lanes), 1) < per, wanted_ref[:, 0, :], 0)
    high, low = halves(wanted)
    tile = where_bf16(remainder(iota((lanes, slots), 1), per) == iota((lanes, slots), 0), 1.0)
    own = quotient(iota((shards, slots), 1), per) == iota((shards, slots), 0)
    high = jnp.sum(jnp.where(own, dot(high.astype(bf16), tile), 0.0), axis=0, keepdims=True)
    low = jnp.sum(jnp.where(own, dot(low.astype(bf16), tile), 0.0), axis=0, keepdims=True)
    row = (16.0 * high + low).astype(i32) - 1
    sum_half(row, back_ref[...], 1 - at_ref[0] % 2, give_ref)
    sum_half(row, back_ref[...], at_ref[0] % 2, keep_ref)


def split_kernel(at_ref, keep_ref, got_ref, *out_refs):
    chips = len(out_refs)
    rows = out_refs[0].shape[0]
    for d, out_ref in enumerate(out_refs):
        base = pl.multiple_of(lax.rem(at_ref[0] // 2 + d, chips) * rows, rows)
        both = keep_ref[pl.ds(base, rows), :].astype(f32) + got_ref[pl.ds(base, rows), :].astype(f32)
        out_ref[...] = both.astype(bf16)


def cut(chunk, shards):
    rows, width = chunk.shape
    lanes = width // 128
    part = rows * lanes // shards
    return [
        chunk[i // lanes * part : (i // lanes + 1) * part, i % lanes * 128 : (i % lanes + 1) * 128]
        for i in range(shards)
    ]


def total_kernel(*refs):
    total = sum((ref[...].astype(f32) for ref in refs[1:-1]), refs[0][...].astype(f32))
    for i, tile in enumerate(cut(total, refs[-1].shape[0])):
        refs[-1][i] = tile.astype(bf16)


def repeat_kernel(tiles_ref, out_ref):
    total = jnp.sum(tiles_ref[...].astype(f32), axis=0).astype(bf16)
    for i in range(out_ref.shape[0]):
        out_ref[i] = total


def place_kernel(at_ref, wanted_ref, *refs, per, total):
    out_hbm, out_ref, arrived = refs[-3:]
    chunks = refs[:-3]
    copies = []
    chips = len(chunks) // 2
    _, rows, width = out_ref.shape
    shards, _, lanes = wanted_ref.shape
    counted = jnp.where(iota((shards, lanes), 1) == per, wanted_ref[:, 0, :], 0)
    ratio = total / jnp.sum(counted.astype(f32), axis=(0, 1), keepdims=True)
    chip, core = at_ref[0] // 2, at_ref[0] % 2
    for other in range(2):
        half = core + other - 2 * core * other
        for d in range(chips):
            spot = half * chips + lax.rem(chip + chips - d, chips)
            base = pl.multiple_of(spot * rows, rows)
            chunk = chunks[other * chips + d]
            n = other * chips + d
            if len(chunk.shape) == 2:
                out_ref[n] = ratio * chunk[...].astype(f32)
            else:
                part = chunk.shape[1]
                for i in range(shards):
                    across = i % (width // 128) * 128
                    down = i // (width // 128) * part
                    tile = ratio * chunk[i].astype(f32)
                    out_ref[n, down : down + part, across : across + 128] = tile
            copies += begin([(out_ref.at[n], out_hbm.at[pl.ds(base, rows), :])], arrived, n)
    finish(copies)


def exchange(array, axis):
    return lax.all_to_all(array, axis, split_axis=0, concat_axis=0, tiled=True)


def to_core(array):
    peers = lax.axis_size("hist")
    return lax.ppermute(array, "hist", [(i, i ^ 1) for i in range(peers)])


def to_chip(array, steps):
    peers = lax.axis_size("hist")
    return lax.ppermute(array, "hist", [(i, (i + 2 * steps) % peers) for i in range(peers)])


def split(at, keep, give):
    chips = lax.axis_size("hist") // 2
    outs = [((keep.shape[0] // chips, keep.shape[1]), bf16)] * chips
    return call(split_kernel, outs, (at, keep, to_core(give)), [SM, VM, VM])


def shared(chunks):
    return [chunks[0]] + [to_chip(chunks[d], d) for d in range(1, len(chunks))]


def along_chips(chunk):
    chips = lax.axis_size("hist") // 2
    return [chunk] + [to_chip(chunk, d) for d in range(1, chips)]


def placed(at, wanted, chunks, rows, width, per, total):
    kernel = functools.partial(place_kernel, per=per, total=total)
    specs = [SM] + [VM] * (1 + len(chunks))
    n = len(chunks)
    scratch = [pltpu.VMEM((n, rows // n, width), f32), dma(n)]
    args = (at, wanted, *chunks)
    (out,) = call(kernel, [((rows, width), f32)], args, specs, scratch, [HB])
    return out


def body(
    quot_ids,
    rem_ids,
    lengths,
    log_decay,
    quot_table,
    rem_table,
    w_query,
    w_key,
    w_value,
    w_out,
    cotangent,
):
    users, block = quot_ids.shape
    rows_all, width = quot_table.shape
    heads = log_decay.shape[1]
    size = width // heads
    shards = lax.axis_size("user")
    peers = lax.axis_size("hist")
    rows_own = rem_table.shape[0]
    cap = 2 * block // shards
    per = users * cap
    slots = shards * per
    scale = 1.0 / math.sqrt(size * block * peers)
    at = lax.axis_index("hist").astype(i32).reshape(1)
    lanes = (per // 128 + 1) * 128

    requests, slot = call(
        functools.partial(request_kernel, rows_own=rows_own, cap=cap),
        [((shards, 1, lanes), i32), ((8, block), i32)],
        (lengths, rem_ids),
        [SM, VM],
        limit=FULL,
    )
    wanted = exchange(requests, "user")
    quot_emb, dmixed, wide = call(
        quotient_kernel,
        [
            ((users * block, width), bf16),
            ((users * block, width), bf16),
            ((users * block, width), f32),
        ],
        (lengths, at, quot_ids, quot_table, cotangent, log_decay, w_out),
        [SM, SM] + [VM] * 5,
        limit=FULL,
    )
    (found,) = call(
        functools.partial(answer_kernel, per=per),
        [((slots, width), bf16)],
        (wanted, rem_table),
        [HB, HB],
        [
            pltpu.VMEM((shards, 1, lanes), i32),
            pltpu.VMEM((rows_own, width), bf16),
            pltpu.VMEM((slots, width), bf16),
            dma(6),
        ],
        [HB],
        FULL,
    )
    answered = exchange(found.reshape(shards, per, width), "user").reshape(slots, width)
    events = pltpu.VMEM((users * block, width), bf16)
    square = pltpu.VMEM((width, width), bf16)
    rem_emb, payload = call(
        functools.partial(project_kernel, users=users, heads=heads),
        [((users * block, width), bf16), ((peers, users * size + 16, width), bf16)],
        (at, slot, answered, quot_emb, w_query, w_key, w_value, wide, dmixed),
        [SM] + [HB] * 8,
        [pltpu.VMEM((8, block), i32), pltpu.VMEM((slots, width), bf16), events]
        + [square] * 3
        + [pltpu.VMEM((users * block, width), f32), events, events]
        + [pltpu.VMEM((2, users * size + 16, width), bf16), dma(8 + users + peers)],
        [HB, HB],
        FULL,
    )
    states = exchange(payload, "hist")
    parts = (4, users * block, width)
    (within,) = call(
        functools.partial(within_kernel, scale=scale),
        [(parts, f32)],
        (quot_emb, rem_emb, dmixed, log_decay, w_query, w_key, w_value),
        scratch=[pltpu.VMEM(parts, f32), dma(users)],
        out_specs=[HB],
        limit=FULL,
    )
    output, rem_send, keep, give = call(
        functools.partial(gradient_kernel, scale=scale, heads=heads),
        [
            ((users, block, width), bf16),
            ((slots, width), bf16),
            ((rows_all // 2, width), bf16),
            ((rows_all // 2, width), bf16),
        ],
        (at, states, within, dmixed, wide, rem_emb, quot_emb, slot, quot_ids)
        + (w_query, w_key, w_value, w_out),
        [SM] + [HB] * 12,
        [pltpu.VMEM(payload.shape, bf16), pltpu.VMEM(parts, f32), events]
        + [pltpu.VMEM((users * block, width), f32), events, events]
        + [pltpu.VMEM((8, block), i32), pltpu.VMEM((users, block), i32)]
        + [square] * 4
        + [pltpu.VMEM((users, block, width), bf16), pltpu.VMEM((slots, width), bf16)]
        + [pltpu.VMEM((rows_all // 2, width), bf16)] * 2
        + [dma(11 + 2 * users + (slots + rows_all) // block)],
        [HB] * 4,
        FULL,
    )
    rem_back = exchange(rem_send.reshape(shards, per, width), "user").reshape(slots, width)
    tiles = (shards, rows_all // peers * width // shards // 128, 128)
    (quot_tiles,) = call(total_kernel, [(tiles, bf16)], shared(split(at, keep, give)))
    rem_back, quot_tiles = lax.optimization_barrier((rem_back, quot_tiles))
    quot_back = exchange(quot_tiles, "user")
    keep, give = call(
        functools.partial(collect_kernel, per=per),
        [((rows_own // 2, width), f32), ((rows_own // 2, width), bf16)],
        (at, wanted, rem_back),
        [SM, VM, VM],
    )
    chunks = split(at, keep, give)
    (quot_tiles,) = call(repeat_kernel, [(tiles, bf16)], (quot_back,))
    quot_tiles, *_ = lax.optimization_barrier((quot_tiles, *chunks))
    quot_tiles = exchange(quot_tiles, "user")
    rem_sum = sum(c.astype(f32) for c in shared(chunks)).astype(bf16)
    rem_mine = along_chips(rem_sum)
    quot_tiles, *rem_mine = lax.optimization_barrier((quot_tiles, *rem_mine))
    total = float(users * shards * block * peers)
    rem_chunks = rem_mine + [to_core(c) for c in rem_mine]
    rem_grad = placed(at, wanted, rem_chunks, rows_own, width, per, total)
    quot_mine = along_chips(quot_tiles)
    quot_chunks = quot_mine + [to_core(c) for c in quot_mine]
    quot_grad = placed(at, wanted, quot_chunks, rows_all, width, per, total)
    return (output, quot_grad, rem_grad)


def solution(mesh):
    return jax.shard_map(
        body,
        mesh=mesh,
        in_specs=(
            P("user", "hist"),
            P("user", "hist"),
            P("user"),
            P("user", None, "hist"),
            P(),
            P("user", None),
            P(),
            P(),
            P(),
            P(),
            P("user", "hist", None),
        ),
        out_specs=(P("user", "hist", None), P(), P("user", None)),
        check_vma=False,
    )
```

```python
import functools
import math

import jax
import jax.numpy as jnp
from jax import lax
from jax.experimental import pallas as pl
from jax.experimental.pallas import tpu as pltpu
from jax.sharding import PartitionSpec as P

f32 = jnp.float32
bf16 = jnp.bfloat16
i32 = jnp.int32
FULL = 62
MOST = 24
EXACT = lax.Precision.HIGHEST
VM = pl.BlockSpec(memory_space=pltpu.VMEM)
SM = pl.BlockSpec(memory_space=pltpu.SMEM)
HB = pl.BlockSpec(memory_space=pltpu.HBM)

NN = (((1,), (0,)), ((), ()))
NT = (((1,), (1,)), ((), ()))
TN = (((0,), (0,)), ((), ()))


def dot(a, b, dims=NN, precision=None):
    return lax.dot_general(a, b, dims, preferred_element_type=f32, precision=precision)


def iota(shape, dim):
    return lax.broadcasted_iota(i32, shape, dim)


def quotient(a, n):
    return a >> (n.bit_length() - 1) if n & (n - 1) == 0 else a // n


def remainder(a, n):
    return a & (n - 1) if n & (n - 1) == 0 else a % n


def where_bf16(mask, a):
    return jnp.where(mask, a, 0.0).astype(bf16)


def halves(whole):
    return (whole >> 4).astype(f32), (whole & 15).astype(f32)


def spread_column(row):
    n = row.shape[1]
    diagonal = iota((n, n), 0) == iota((n, n), 1)
    high, low = halves(row)
    ones = jnp.ones((n, 128), bf16)
    column = 16.0 * dot(where_bf16(diagonal, high), ones) + dot(where_bf16(diagonal, low), ones)
    return column.astype(i32)


def tiled_match(column, width):
    n = column.shape[0]
    lanes = iota((n, 128), 1)
    parts = [where_bf16(column == lanes + j * 128, 1.0) for j in range(width // 128)]
    return jnp.concatenate(parts, axis=1)


def begin(pairs, arrived, at=0):
    copies = [
        pltpu.make_async_copy(source, target, arrived.at[at + i])
        for i, (source, target) in enumerate(pairs)
    ]
    for copy in copies:
        copy.start()
    return copies


def finish(copies):
    for copy in copies:
        copy.wait()


def dma(n):
    return pltpu.SemaphoreType.DMA((n,))


def call(kernel, outs, args, specs=None, scratch=(), out_specs=None, limit=16):
    out_specs = out_specs if out_specs is not None else [VM] * len(outs)
    shapes = [
        pltpu.HBM(s, d) if spec is HB else jax.ShapeDtypeStruct(s, d)
        for (s, d), spec in zip(outs, out_specs, strict=True)
    ]
    specs = specs if specs is not None else [VM] * len(args)
    args = [
        pltpu.with_memory_space_constraint(a, pltpu.HBM) if spec is HB else a
        for a, spec in zip(args, specs, strict=True)
    ]
    return pl.pallas_call(
        kernel,
        out_shape=tuple(shapes),
        in_specs=specs,
        out_specs=tuple(out_specs),
        scratch_shapes=list(scratch),
        compiler_params=pltpu.CompilerParams(vmem_limit_bytes=limit * 1024 * 1024),
    )(*args)


def request_kernel(
    len_ref, ids_ref, out_ref, slot_hbm, slot_ref, arrived, *, rows_own, cap
):
    users, block = ids_ref.shape
    shards, _, lanes = out_ref.shape
    shift = rows_own.bit_length() - 1
    earlier = where_bf16(iota((block, block), 0) < iota((block, block), 1), 1.0)
    place = iota((lanes, block), 0)
    total = jnp.zeros((shards, lanes), f32)
    count = jnp.int32(0)
    slot_ref[...] = jnp.zeros_like(slot_ref)
    for u in range(users):
        ids = ids_ref[u : u + 1, :]
        owner = ids >> shift
        named = iota((shards, block), 0) == owner
        named_16 = where_bf16(named, 1.0)
        before = dot(named_16, earlier)
        rank = jnp.sum(jnp.where(named, before, 0.0), axis=0, keepdims=True).astype(i32)
        high, low = halves((ids & (rows_own - 1)) + 1)
        chosen = place == rank + u * cap
        total = total + 16.0 * dot(named_16, where_bf16(chosen, high), NT)
        total = total + dot(named_16, where_bf16(chosen, low), NT)
        slot_ref[u : u + 1, :] = (owner * users + u) * cap + rank
        count = count + len_ref[u]
    copies = begin([(slot_ref, slot_hbm)], arrived)
    wanted = jnp.where(iota((shards, lanes), 1) == users * cap, count, total.astype(i32))
    out_ref[:, 0, :] = wanted
    finish(copies)


def answer_kernel(
    wanted_hbm, table_hbm, out_hbm, wanted_ref, table_ref, out_ref, arrived, *, per
):
    shards, _, lanes = wanted_ref.shape
    copies = begin(((wanted_hbm, wanted_ref), (table_hbm, table_ref)), arrived)
    parts = 4
    group = shards // parts
    slots = group * per
    rows = table_ref.shape[0]
    repeat = where_bf16(quotient(iota((slots, group), 0), per) == iota((slots, group), 1), 1.0)
    own = remainder(iota((slots, lanes), 0), per) == iota((slots, lanes), 1)
    ones = jnp.ones((lanes, 128), bf16)
    finish(copies[:1])
    wanted = jnp.where(iota((shards, lanes), 1) < per, wanted_ref[:, 0, :], 0)
    stores = []
    for j in range(parts):
        high, low = halves(wanted[j * group : (j + 1) * group, :])
        high = dot(where_bf16(own, dot(repeat, high.astype(bf16))), ones)
        low = dot(where_bf16(own, dot(repeat, low.astype(bf16))), ones)
        column = (16.0 * high + low).astype(i32) - 1
        hot = tiled_match(column, rows)
        if j == 0:
            finish(copies[1:])
        at = slice(j * slots, (j + 1) * slots)
        out_ref[at, :] = dot(hot, table_ref[...]).astype(bf16)
        stores += begin([(out_ref.at[at, :], out_hbm.at[at, :])], arrived, 2 + j)
    finish(stores)


def quotient_kernel(
    len_ref,
    at_ref,
    ids_ref,
    table_ref,
    cot_ref,
    decay_ref,
    w_out_ref,
    quot_hbm,
    dmixed_hbm,
    wide_hbm,
    quot_ref,
    dmixed_ref,
    wide_ref,
    arrived,
):
    users, block = ids_ref.shape
    heads = decay_ref.shape[1]
    rows, width = table_ref.shape
    for u in range(users):
        at = slice(u * block, (u + 1) * block)
        hot = tiled_match(spread_column(ids_ref[u : u + 1, :]), rows)
        quot_ref[at, :] = dot(hot, table_ref[...]).astype(bf16)
        valid = at_ref[0] * block + iota((block, width), 0) < len_ref[u]
        masked = jnp.where(valid, cot_ref[u].astype(f32), 0.0).astype(bf16)
        dmixed_ref[at, :] = dot(masked, w_out_ref[...], NT).astype(bf16)
        _, columns = decays(decay_ref[u], width)
        wide_ref[at, :] = over_heads(columns, heads, width)
    pairs = ((quot_ref, quot_hbm), (dmixed_ref, dmixed_hbm), (wide_ref, wide_hbm))
    finish(begin(pairs, arrived))


def decays(log_decay, width):
    heads, block = log_decay.shape
    upper = jnp.where(iota((block, block), 0) <= iota((block, block), 1), 1.0, 0.0)
    lower = jnp.where(iota((block, block), 0) >= iota((block, block), 1), 1.0, 0.0)
    padded = jnp.concatenate([log_decay, jnp.zeros((8 - heads, block), f32)], axis=0)
    rows = dot(padded, upper, precision=EXACT)
    columns = dot(lower, padded, NT, precision=EXACT)
    return rows, columns


def over_heads(columns, heads, width):
    n = columns.shape[0]
    head_of = quotient(iota((n, width), 1), width // heads)
    wide = jnp.broadcast_to(columns[:, 0:1], (n, width))
    for h in range(1, heads):
        wide = jnp.where(head_of == h, jnp.broadcast_to(columns[:, h : h + 1], (n, width)), wide)
    return wide


def diagonal_heads(square, heads):
    width = square.shape[1]
    size = width // heads
    head_of = quotient(iota((size, width), 1), size)
    out = square[0:size, :]
    for h in range(1, heads):
        out = jnp.where(head_of == h, square[h * size : (h + 1) * size, :], out)
    return out


def block_diagonal(state, heads):
    size, width = state.shape
    head_of = quotient(iota((size, width), 1), width // heads)
    return jnp.concatenate([where_bf16(head_of == h, state) for h in range(heads)], axis=0)


def project_kernel(
    at_ref,
    slot_hbm,
    answered_ref,
    quot_hbm,
    wq_hbm,
    wk_hbm,
    wv_hbm,
    wide_hbm,
    dmixed_hbm,
    rem_hbm,
    payload_hbm,
    slot_ref,
    quot_ref,
    wq_ref,
    wk_ref,
    wv_ref,
    wide_ref,
    dmixed_ref,
    rem_ref,
    states_ref,
    arrived,
    *,
    users,
    heads,
):
    slots, width = answered_ref.shape
    block = quot_ref.shape[0] // users
    peers = payload_hbm.shape[0]
    size = width // heads
    me = at_ref[0]
    ends = []
    copies = begin(
        (
            (slot_hbm, slot_ref),
            (quot_hbm, quot_ref),
            (wq_hbm, wq_ref),
            (wk_hbm, wk_ref),
            (wv_hbm, wv_ref),
            (wide_hbm, wide_ref),
            (dmixed_hbm, dmixed_ref),
        ),
        arrived,
    )
    finish(copies[:1])
    hot = [tiled_match(spread_column(slot_ref[u : u + 1, :]), slots) for u in range(users)]
    finish(copies[1:5])
    waits, copies = copies[5:], []
    for u in range(users):
        at = slice(u * block, (u + 1) * block)
        rem_ref[at, :] = dot(hot[u], answered_ref[...]).astype(bf16)
        copies += begin([(rem_ref.at[at, :], rem_hbm.at[at, :])], arrived, 8 + u)
        embedded = (quot_ref[at, :].astype(f32) * rem_ref[at, :].astype(f32)).astype(bf16)
        q = dot(embedded, wq_ref[...]).astype(bf16)
        k = dot(embedded, wk_ref[...]).astype(bf16)
        v = dot(embedded, wv_ref[...]).astype(bf16)
        if u == 0:
            finish(waits)
        wide = wide_ref[at, :]
        end = wide[block - 1 : block, :]
        ends.append(end)
        falling = (k.astype(f32) * jnp.exp(end - wide)).astype(bf16)
        growing = (q.astype(f32) * jnp.exp(wide)).astype(bf16)
        state = diagonal_heads(dot(falling, v, TN), heads).astype(bf16)
        grad = diagonal_heads(dot(growing, dmixed_ref[at, :], TN), heads).astype(bf16)
        states_ref[0, u * size : (u + 1) * size, :] = state
        states_ref[1, u * size : (u + 1) * size, :] = grad
    rows = iota((16, width), 0)
    tail = jnp.zeros((16, width), f32)
    for u in range(users):
        left = ends[u]
        for part in range(3):
            piece = left.astype(bf16).astype(f32)
            left = left - piece
            tail = jnp.where(rows == part * users + u, piece, tail)
    tail = tail.astype(bf16)
    states_ref[0, users * size :, :] = tail
    states_ref[1, users * size :, :] = tail
    which = [jnp.where(peer > me, 0, 1) for peer in range(peers)]
    pairs = [(states_ref.at[which[peer]], payload_hbm.at[peer]) for peer in range(peers)]
    finish(copies + begin(pairs, arrived, 8 + users))


def within_kernel(
    quot_ref,
    rem_ref,
    dmixed_ref,
    decay_ref,
    wq_ref,
    wk_ref,
    wv_ref,
    out_hbm,
    out_ref,
    arrived,
    *,
    scale,
):
    users, heads, block = decay_ref.shape
    width = quot_ref.shape[1]
    copies = []
    head_of = quotient(iota((block, width), 1), width // heads)
    lower_tri = iota((block, block), 0) >= iota((block, block), 1)
    for u in range(users):
        at = slice(u * block, (u + 1) * block)
        embedded = (quot_ref[at, :].astype(f32) * rem_ref[at, :].astype(f32)).astype(bf16)
        q = dot(embedded, wq_ref[...]).astype(bf16)
        k = dot(embedded, wk_ref[...]).astype(bf16)
        v = dot(embedded, wv_ref[...]).astype(bf16)
        dmixed = dmixed_ref[at, :]
        rows, columns = decays(decay_ref[u], width)
        mixed = jnp.zeros((block, width), f32)
        dq = jnp.zeros((block, width), f32)
        dk = jnp.zeros((block, width), f32)
        dv = jnp.zeros((block, width), f32)
        zero = jnp.zeros((), bf16)
        for h in range(heads):
            own = head_of == h
            q_h = jnp.where(own, q, zero)
            k_h = jnp.where(own, k, zero)
            v_h = jnp.where(own, v, zero)
            d_h = jnp.where(own, dmixed, zero)
            gap = columns[:, h : h + 1] - rows[h : h + 1, :]
            mask = jnp.where(lower_tri, scale * jnp.exp(jnp.minimum(gap, 0.0)), 0.0)
            weights = (dot(q_h, k, NT) * mask).astype(bf16)
            dweights = (dot(d_h, v, NT) * mask).astype(bf16)
            mixed = mixed + dot(weights, v_h)
            dq = dq + dot(dweights, k_h)
            dk = dk + dot(dweights, q_h, TN)
            dv = dv + dot(weights, d_h, TN)
        for i, part in enumerate((mixed, dq, dk, dv)):
            out_ref[i, at, :] = part
        copies += begin([(out_ref.at[:, at, :], out_hbm.at[:, at, :])], arrived, u)
    finish(copies)


def sum_half(ids, terms, owner, out_ref):
    half = out_ref.shape[0]
    chunk = min(256, half)
    spot = iota((chunk, ids.shape[1]), 0)
    near = ids - owner * half
    for j in range(half // chunk):
        hot = where_bf16(spot + j * chunk == near, 1.0)
        out_ref[j * chunk : (j + 1) * chunk, :] = dot(hot, terms).astype(out_ref.dtype)


def gradient_kernel(
    at_ref,
    payload_ref,
    within_hbm,
    dmixed_hbm,
    wide_hbm,
    rem_hbm,
    quot_hbm,
    slot_hbm,
    ids_hbm,
    wq_hbm,
    wk_hbm,
    wv_hbm,
    w_out_hbm,
    out_hbm,
    rem_send_hbm,
    keep_hbm,
    give_hbm,
    within_ref,
    dmixed_ref,
    wide_ref,
    rem_ref,
    quot_ref,
    slot_ref,
    ids_ref,
    wq_ref,
    wk_ref,
    wv_ref,
    w_out_ref,
    out_ref,
    rem_send_ref,
    keep_ref,
    give_ref,
    arrived,
    *,
    scale,
    heads,
):
    users, block = ids_ref.shape
    width = quot_ref.shape[1]
    copies = begin(
        (
            (quot_hbm, quot_ref),
            (rem_hbm, rem_ref),
            (wq_hbm, wq_ref),
            (wk_hbm, wk_ref),
            (wv_hbm, wv_ref),
            (wide_hbm, wide_ref),
            (dmixed_hbm, dmixed_ref),
            (w_out_hbm, w_out_ref),
            (slot_hbm, slot_ref),
            (ids_hbm, ids_ref),
        ),
        arrived,
    )
    waits = []
    for u in range(users):
        at = slice(u * block, (u + 1) * block)
        waits += begin([(within_hbm.at[:, at, :], within_ref.at[:, at, :])], arrived, 11 + u)
    peers = payload_ref.shape[0]
    size = width // heads
    slots = rem_send_ref.shape[0]
    me = at_ref[0]
    carried = []
    for u in range(users):
        ends = []
        for peer in range(peers):
            tail = payload_ref[peer, users * size :, :].astype(f32)
            ends.append(
                tail[u : u + 1, :]
                + tail[users + u : users + u + 1, :]
                + tail[2 * users + u : 2 * users + u + 1, :]
            )
        entering = jnp.zeros((size, width), f32)
        for peer in range(peers):
            part = payload_ref[peer, u * size : (u + 1) * size, :].astype(f32)
            linked = jnp.exp(ends[peer]) * entering + part
            entering = jnp.where(peer < me, linked, entering)
        leaving = jnp.zeros((size, width), f32)
        for peer in reversed(range(peers)):
            part = payload_ref[peer, u * size : (u + 1) * size, :].astype(f32)
            linked = jnp.exp(ends[peer]) * leaving + part
            leaving = jnp.where(peer > me, linked, leaving)
        carried.append((block_diagonal(entering, heads), block_diagonal(leaving, heads)))
    finish(copies)
    copies = []
    rem_terms, quot_terms = [], []
    for u in range(users):
        at = slice(u * block, (u + 1) * block)
        entering, leaving = carried[u]
        embedded = (quot_ref[at, :].astype(f32) * rem_ref[at, :].astype(f32)).astype(bf16)
        q = dot(embedded, wq_ref[...]).astype(bf16)
        k = dot(embedded, wk_ref[...]).astype(bf16)
        v = dot(embedded, wv_ref[...]).astype(bf16)
        dmixed = dmixed_ref[at, :]
        wide = wide_ref[at, :]
        finish(waits[u : u + 1])
        growth = scale * jnp.exp(wide)
        falloff = scale * jnp.exp(wide[block - 1 : block, :] - wide)
        mixed = (within_ref[0, at, :] + growth * dot(q, entering)).astype(bf16)
        out_ref[u] = dot(mixed, w_out_ref[...]).astype(bf16)
        copies += begin([(out_ref.at[u], out_hbm.at[u])], arrived, 11 + users + u)
        dq = (within_ref[1, at, :] + growth * dot(dmixed, entering, NT)).astype(bf16)
        dk = (within_ref[2, at, :] + falloff * dot(v, leaving, NT)).astype(bf16)
        dv = (within_ref[3, at, :] + falloff * dot(k, leaving)).astype(bf16)
        dembedded = dot(dq, wq_ref[...], NT) + dot(dk, wk_ref[...], NT) + dot(dv, wv_ref[...], NT)
        rem_terms.append((dembedded * quot_ref[at, :].astype(f32)).astype(bf16))
        quot_terms.append((dembedded * rem_ref[at, :].astype(f32)).astype(bf16))
    rem_terms = jnp.concatenate(rem_terms, axis=0)
    quot_terms = jnp.concatenate(quot_terms, axis=0)
    slot = jnp.concatenate([slot_ref[u : u + 1, :] for u in range(users)], axis=1)
    ids = jnp.concatenate([ids_ref[u : u + 1, :] for u in range(users)], axis=1)
    spot = iota((block, users * block), 0)
    n = 11 + 2 * users
    for j in range(slots // block):
        hot = where_bf16(spot + j * block == slot, 1.0)
        at = slice(j * block, (j + 1) * block)
        rem_send_ref[at, :] = dot(hot, rem_terms).astype(bf16)
        copies += begin([(rem_send_ref.at[at, :], rem_send_hbm.at[at, :])], arrived, n + j)
    n += slots // block
    for ref, hbm, owner in ((give_ref, give_hbm, 1 - me % 2), (keep_ref, keep_hbm, me % 2)):
        half = ref.shape[0]
        near = ids - owner * half
        for j in range(half // block):
            hot = where_bf16(spot + j * block == near, 1.0)
            at = slice(j * block, (j + 1) * block)
            ref[at, :] = dot(hot, quot_terms).astype(bf16)
            copies += begin([(ref.at[at, :], hbm.at[at, :])], arrived, n)
            n += 1
    finish(copies)


def collect_kernel(at_ref, wanted_ref, back_ref, keep_ref, give_ref, *, per):
    shards, _, lanes = wanted_ref.shape
    slots = shards * per
    wanted = jnp.where(iota((shards, lanes), 1) < per, wanted_ref[:, 0, :], 0)
    high, low = halves(wanted)
    tile = where_bf16(remainder(iota((lanes, slots), 1), per) == iota((lanes, slots), 0), 1.0)
    own = quotient(iota((shards, slots), 1), per) == iota((shards, slots), 0)
    high = jnp.sum(jnp.where(own, dot(high.astype(bf16), tile), 0.0), axis=0, keepdims=True)
    low = jnp.sum(jnp.where(own, dot(low.astype(bf16), tile), 0.0), axis=0, keepdims=True)
    row = (16.0 * high + low).astype(i32) - 1
    sum_half(row, back_ref[...], 1 - at_ref[0] % 2, give_ref)
    sum_half(row, back_ref[...], at_ref[0] % 2, keep_ref)


def split_kernel(at_ref, keep_ref, got_ref, *refs, chips):
    out_refs = refs[:chips]
    rows = out_refs[0].shape[0]
    bases = [
        pl.multiple_of(lax.rem(at_ref[0] // 2 + d, chips) * rows, rows) for d in range(chips)
    ]
    copies = []
    if len(refs) > chips:
        near_ref, arrived = refs[chips:]
        copies = begin([(keep_ref.at[pl.ds(b, rows), :], near_ref.at[d]) for d, b in enumerate(bases)], arrived)
    for d, out_ref in enumerate(out_refs):
        finish(copies[d : d + 1])
        kept = near_ref[d] if copies else keep_ref[pl.ds(bases[d], rows), :]
        both = kept.astype(f32) + got_ref[pl.ds(bases[d], rows), :].astype(f32)
        out_ref[...] = both.astype(bf16)


def cut(chunk, shards):
    rows, width = chunk.shape
    lanes = width // 128
    part = rows * lanes // shards
    return [
        chunk[i // lanes * part : (i // lanes + 1) * part, i % lanes * 128 : (i % lanes + 1) * 128]
        for i in range(shards)
    ]


def total_kernel(*refs):
    total = sum((ref[...].astype(f32) for ref in refs[1:-1]), refs[0][...].astype(f32))
    for i, tile in enumerate(cut(total, refs[-1].shape[0])):
        refs[-1][i] = tile.astype(bf16)


def repeat_kernel(tiles_ref, out_ref):
    total = jnp.sum(tiles_ref[...].astype(f32), axis=0).astype(bf16)
    for i in range(out_ref.shape[0]):
        out_ref[i] = total


def place_kernel(at_ref, wanted_ref, *refs, per, total):
    out_hbm, out_ref, arrived = refs[-3:]
    chunks = refs[:-3]
    copies = []
    chips = len(chunks) // 2
    _, rows, width = out_ref.shape
    shards, _, lanes = wanted_ref.shape
    counted = jnp.where(iota((shards, lanes), 1) == per, wanted_ref[:, 0, :], 0)
    ratio = total / jnp.sum(counted.astype(f32), axis=(0, 1), keepdims=True)
    chip, core = at_ref[0] // 2, at_ref[0] % 2
    for other in range(2):
        half = core + other - 2 * core * other
        for d in range(chips):
            spot = half * chips + lax.rem(chip + chips - d, chips)
            base = pl.multiple_of(spot * rows, rows)
            chunk = chunks[other * chips + d]
            n = other * chips + d
            if len(chunk.shape) == 2:
                out_ref[n] = ratio * chunk[...].astype(f32)
            else:
                part = chunk.shape[1]
                for i in range(shards):
                    across = i % (width // 128) * 128
                    down = i // (width // 128) * part
                    tile = ratio * chunk[i].astype(f32)
                    out_ref[n, down : down + part, across : across + 128] = tile
            copies += begin([(out_ref.at[n], out_hbm.at[pl.ds(base, rows), :])], arrived, n)
    finish(copies)


def exchange(array, axis):
    return lax.all_to_all(array, axis, split_axis=0, concat_axis=0, tiled=True)


def to_core(array):
    peers = lax.axis_size("hist")
    return lax.ppermute(array, "hist", [(i, i ^ 1) for i in range(peers)])


def to_chip(array, steps):
    peers = lax.axis_size("hist")
    return lax.ppermute(array, "hist", [(i, (i + 2 * steps) % peers) for i in range(peers)])


def split(at, keep, give, spec=VM):
    chips = lax.axis_size("hist") // 2
    rows, width = keep.shape[0] // chips, keep.shape[1]
    kernel = functools.partial(split_kernel, chips=chips)
    scratch = [pltpu.VMEM((chips, rows, width), keep.dtype), dma(chips)] if spec is HB else []
    args = (at, keep, to_core(give))
    return call(kernel, [((rows, width), bf16)] * chips, args, [SM, spec, VM], scratch)


def shared(chunks):
    return [chunks[0]] + [to_chip(chunks[d], d) for d in range(1, len(chunks))]


def along_chips(chunk):
    chips = lax.axis_size("hist") // 2
    return [chunk] + [to_chip(chunk, d) for d in range(1, chips)]


def placed(at, wanted, chunks, rows, width, per, total):
    kernel = functools.partial(place_kernel, per=per, total=total)
    specs = [SM] + [VM] * (1 + len(chunks))
    n = len(chunks)
    scratch = [pltpu.VMEM((n, rows // n, width), f32), dma(n)]
    args = (at, wanted, *chunks)
    (out,) = call(kernel, [((rows, width), f32)], args, specs, scratch, [HB])
    return out


def body(
    quot_ids,
    rem_ids,
    lengths,
    log_decay,
    quot_table,
    rem_table,
    w_query,
    w_key,
    w_value,
    w_out,
    cotangent,
):
    users, block = quot_ids.shape
    rows_all, width = quot_table.shape
    heads = log_decay.shape[1]
    size = width // heads
    shards = lax.axis_size("user")
    peers = lax.axis_size("hist")
    rows_own = rem_table.shape[0]
    cap = 2 * block // shards
    per = users * cap
    slots = shards * per
    scale = 1.0 / math.sqrt(size * block * peers)
    at = lax.axis_index("hist").astype(i32).reshape(1)
    lanes = (per // 128 + 1) * 128

    events = pltpu.VMEM((users * block, width), bf16)
    square = pltpu.VMEM((width, width), bf16)
    requests, slot = call(
        functools.partial(request_kernel, rows_own=rows_own, cap=cap),
        [((shards, 1, lanes), i32), ((8, block), i32)],
        (lengths, rem_ids),
        [SM, VM],
        [pltpu.VMEM((8, block), i32), dma(1)],
        [VM, HB],
        FULL,
    )
    wanted = exchange(requests, "user")
    quot_emb, dmixed, wide = call(
        quotient_kernel,
        [
            ((users * block, width), bf16),
            ((users * block, width), bf16),
            ((users * block, width), f32),
        ],
        (lengths, at, quot_ids, quot_table, cotangent, log_decay, w_out),
        [SM, SM] + [VM] * 5,
        [events, events, pltpu.VMEM((users * block, width), f32), dma(3)],
        [HB] * 3,
        FULL,
    )
    (found,) = call(
        functools.partial(answer_kernel, per=per),
        [((slots, width), bf16)],
        (wanted, rem_table),
        [HB, HB],
        [
            pltpu.VMEM((shards, 1, lanes), i32),
            pltpu.VMEM((rows_own, width), bf16),
            pltpu.VMEM((slots, width), bf16),
            dma(6),
        ],
        [HB],
        FULL,
    )
    answered = exchange(found.reshape(shards, per, width), "user").reshape(slots, width)
    rem_emb, payload = call(
        functools.partial(project_kernel, users=users, heads=heads),
        [((users * block, width), bf16), ((peers, users * size + 16, width), bf16)],
        (at, slot, answered, quot_emb, w_query, w_key, w_value, wide, dmixed),
        [SM, HB, VM] + [HB] * 6,
        [pltpu.VMEM((8, block), i32), events]
        + [square] * 3
        + [pltpu.VMEM((users * block, width), f32), events, events]
        + [pltpu.VMEM((2, users * size + 16, width), bf16), dma(8 + users + peers)],
        [HB, HB],
        MOST,
    )
    states = exchange(payload, "hist")
    parts = (4, users * block, width)
    (within,) = call(
        functools.partial(within_kernel, scale=scale),
        [(parts, f32)],
        (quot_emb, rem_emb, dmixed, log_decay, w_query, w_key, w_value),
        scratch=[pltpu.VMEM(parts, f32), dma(users)],
        out_specs=[HB],
        limit=FULL,
    )
    output, rem_send, keep, give = call(
        functools.partial(gradient_kernel, scale=scale, heads=heads),
        [
            ((users, block, width), bf16),
            ((slots, width), bf16),
            ((rows_all // 2, width), bf16),
            ((rows_all // 2, width), bf16),
        ],
        (at, states, within, dmixed, wide, rem_emb, quot_emb, slot, quot_ids)
        + (w_query, w_key, w_value, w_out),
        [SM, VM] + [HB] * 11,
        [pltpu.VMEM(parts, f32), events]
        + [pltpu.VMEM((users * block, width), f32), events, events]
        + [pltpu.VMEM((8, block), i32), pltpu.VMEM((users, block), i32)]
        + [square] * 4
        + [pltpu.VMEM((users, block, width), bf16), pltpu.VMEM((slots, width), bf16)]
        + [pltpu.VMEM((rows_all // 2, width), bf16)] * 2
        + [dma(11 + 2 * users + (slots + rows_all) // block)],
        [HB] * 4,
        MOST,
    )
    rem_back = exchange(rem_send.reshape(shards, per, width), "user").reshape(slots, width)
    tiles = (shards, rows_all // peers * width // shards // 128, 128)
    (quot_tiles,) = call(total_kernel, [(tiles, bf16)], shared(split(at, keep, give, HB)))
    rem_back, quot_tiles = lax.optimization_barrier((rem_back, quot_tiles))
    quot_back = exchange(quot_tiles, "user")
    keep, give = call(
        functools.partial(collect_kernel, per=per),
        [((rows_own // 2, width), f32), ((rows_own // 2, width), bf16)],
        (at, wanted, rem_back),
        [SM, VM, VM],
    )
    chunks = split(at, keep, give)
    (quot_tiles,) = call(repeat_kernel, [(tiles, bf16)], (quot_back,))
    quot_tiles, *_ = lax.optimization_barrier((quot_tiles, *chunks))
    quot_tiles = exchange(quot_tiles, "user")
    rem_sum = sum(c.astype(f32) for c in shared(chunks)).astype(bf16)
    rem_mine = along_chips(rem_sum)
    quot_tiles, _ = lax.optimization_barrier((quot_tiles, rem_sum))
    total = float(users * shards * block * peers)
    rem_chunks = rem_mine + [to_core(c) for c in rem_mine]
    rem_grad = placed(at, wanted, rem_chunks, rows_own, width, per, total)
    quot_mine = along_chips(quot_tiles)
    quot_chunks = quot_mine + [to_core(c) for c in quot_mine]
    quot_grad = placed(at, wanted, quot_chunks, rows_all, width, per, total)
    return (output, quot_grad, rem_grad)


def solution(mesh):
    return jax.shard_map(
        body,
        mesh=mesh,
        in_specs=(
            P("user", "hist"),
            P("user", "hist"),
            P("user"),
            P("user", None, "hist"),
            P(),
            P("user", None),
            P(),
            P(),
            P(),
            P(),
            P("user", "hist", None),
        ),
        out_specs=(P("user", "hist", None), P(), P("user", None)),
        check_vma=False,
    )
```

```python
import functools
import math

import jax
import jax.numpy as jnp
from jax import lax
from jax.experimental import pallas as pl
from jax.experimental.pallas import tpu as pltpu
from jax.sharding import PartitionSpec as P

f32 = jnp.float32
bf16 = jnp.bfloat16
i32 = jnp.int32
FULL = 62
MOST = 24
EXACT = lax.Precision.HIGHEST
VM = pl.BlockSpec(memory_space=pltpu.VMEM)
SM = pl.BlockSpec(memory_space=pltpu.SMEM)
HB = pl.BlockSpec(memory_space=pltpu.HBM)

NN = (((1,), (0,)), ((), ()))
NT = (((1,), (1,)), ((), ()))
TN = (((0,), (0,)), ((), ()))


def dot(a, b, dims=NN, precision=None):
    return lax.dot_general(a, b, dims, preferred_element_type=f32, precision=precision)


def iota(shape, dim):
    return lax.broadcasted_iota(i32, shape, dim)


def quotient(a, n):
    return a >> (n.bit_length() - 1) if n & (n - 1) == 0 else a // n


def remainder(a, n):
    return a & (n - 1) if n & (n - 1) == 0 else a % n


def where_bf16(mask, a):
    return jnp.where(mask, a, 0.0).astype(bf16)


def halves(whole):
    return (whole >> 4).astype(f32), (whole & 15).astype(f32)


def spread_column(row):
    n = row.shape[1]
    diagonal = iota((n, n), 0) == iota((n, n), 1)
    high, low = halves(row)
    ones = jnp.ones((n, 128), bf16)
    column = 16.0 * dot(where_bf16(diagonal, high), ones) + dot(where_bf16(diagonal, low), ones)
    return column.astype(i32)


def tiled_match(column, width):
    near = where_bf16(iota(column.shape, 1) == (column & 127), 1.0)
    tile = (column >> 7).astype(f32).astype(bf16)
    zero = jnp.zeros_like(near)
    parts = [jnp.where(tile == jnp.asarray(j, bf16), near, zero) for j in range(width // 128)]
    return jnp.concatenate(parts, axis=1)


def stacked_match(row, chunk, count):
    row = jnp.broadcast_to(row, (chunk, row.shape[1]))
    near = where_bf16(iota(row.shape, 0) == (row & (chunk - 1)), 1.0)
    part = (row >> (chunk.bit_length() - 1)).astype(f32).astype(bf16)
    zero = jnp.zeros_like(near)
    return [jnp.where(part == jnp.asarray(j, bf16), near, zero) for j in range(count)]


def begin(pairs, arrived, at=0):
    copies = [
        pltpu.make_async_copy(source, target, arrived.at[at + i])
        for i, (source, target) in enumerate(pairs)
    ]
    for copy in copies:
        copy.start()
    return copies


def finish(copies):
    for copy in copies:
        copy.wait()


def dma(n):
    return pltpu.SemaphoreType.DMA((n,))


def in_hbm(array):
    return pltpu.with_memory_space_constraint(array, pltpu.HBM)


def call(kernel, outs, args, specs=None, scratch=(), out_specs=None, limit=16, aliases={}):
    out_specs = out_specs if out_specs is not None else [VM] * len(outs)
    shapes = [
        pltpu.HBM(s, d) if spec is HB else jax.ShapeDtypeStruct(s, d)
        for (s, d), spec in zip(outs, out_specs, strict=True)
    ]
    specs = specs if specs is not None else [VM] * len(args)
    args = [
        in_hbm(a) if spec is HB else a
        for a, spec in zip(args, specs, strict=True)
    ]
    return pl.pallas_call(
        kernel,
        out_shape=tuple(shapes),
        in_specs=specs,
        out_specs=tuple(out_specs),
        input_output_aliases=aliases,
        scratch_shapes=list(scratch),
        compiler_params=pltpu.CompilerParams(vmem_limit_bytes=limit * 1024 * 1024),
    )(*args)


def request_kernel(
    len_ref, ids_ref, out_ref, slot_hbm, slot_ref, arrived, *, rows_own, cap
):
    users, block = ids_ref.shape
    shards, _, lanes = out_ref.shape
    shift = rows_own.bit_length() - 1
    earlier = where_bf16(iota((block, block), 0) < iota((block, block), 1), 1.0)
    place = iota((lanes, block), 0)
    total = jnp.zeros((shards, lanes), f32)
    count = jnp.int32(0)
    slot_ref[...] = jnp.zeros_like(slot_ref)
    for u in range(users):
        ids = ids_ref[u : u + 1, :]
        owner = ids >> shift
        named = iota((shards, block), 0) == owner
        named_16 = where_bf16(named, 1.0)
        before = dot(named_16, earlier)
        rank = jnp.sum(jnp.where(named, before, 0.0), axis=0, keepdims=True).astype(i32)
        high, low = halves((ids & (rows_own - 1)) + 1)
        chosen = place == rank + u * cap
        total = total + 16.0 * dot(named_16, where_bf16(chosen, high), NT)
        total = total + dot(named_16, where_bf16(chosen, low), NT)
        slot_ref[u : u + 1, :] = (owner * users + u) * cap + rank
        count = count + len_ref[u]
    copies = begin([(slot_ref, slot_hbm)], arrived)
    wanted = jnp.where(iota((shards, lanes), 1) == users * cap, count, total.astype(i32))
    out_ref[:, 0, :] = wanted
    finish(copies)


def answer_kernel(
    wanted_ref, table_hbm, out_hbm, table_ref, out_ref, arrived, *, per
):
    shards, _, lanes = wanted_ref.shape
    copies = begin([(table_hbm, table_ref)], arrived)
    parts = 4
    group = shards // parts
    slots = group * per
    rows = table_ref.shape[0]
    repeat = where_bf16(quotient(iota((slots, group), 0), per) == iota((slots, group), 1), 1.0)
    own = remainder(iota((slots, lanes), 0), per) == iota((slots, lanes), 1)
    ones = jnp.ones((lanes, 128), bf16)
    wanted = jnp.where(iota((shards, lanes), 1) < per, wanted_ref[:, 0, :], 0)
    stores = []
    for j in range(parts):
        high, low = halves(wanted[j * group : (j + 1) * group, :])
        high = dot(where_bf16(own, dot(repeat, high.astype(bf16))), ones)
        low = dot(where_bf16(own, dot(repeat, low.astype(bf16))), ones)
        column = (16.0 * high + low).astype(i32) - 1
        hot = tiled_match(column, rows)
        if j == 0:
            finish(copies)
        at = slice(j * slots, (j + 1) * slots)
        out_ref[at, :] = dot(hot, table_ref[...]).astype(bf16)
        stores += begin([(out_ref.at[at, :], out_hbm.at[at, :])], arrived, 1 + j)
    finish(stores)


def quotient_kernel(
    len_ref,
    at_ref,
    ids_ref,
    table_ref,
    cot_ref,
    decay_ref,
    w_out_ref,
    quot_hbm,
    dmixed_hbm,
    wide_hbm,
    quot_ref,
    dmixed_ref,
    wide_ref,
    arrived,
):
    users, block = ids_ref.shape
    heads = decay_ref.shape[1]
    rows, width = table_ref.shape
    for u in range(users):
        at = slice(u * block, (u + 1) * block)
        hot = tiled_match(spread_column(ids_ref[u : u + 1, :]), rows)
        quot_ref[at, :] = dot(hot, table_ref[...]).astype(bf16)
        valid = at_ref[0] * block + iota((block, width), 0) < len_ref[u]
        masked = jnp.where(valid, cot_ref[u].astype(f32), 0.0).astype(bf16)
        dmixed_ref[at, :] = dot(masked, w_out_ref[...], NT).astype(bf16)
        _, columns = decays(decay_ref[u], width)
        wide_ref[at, :] = over_heads(columns, heads, width)
    pairs = ((quot_ref, quot_hbm), (dmixed_ref, dmixed_hbm), (wide_ref, wide_hbm))
    finish(begin(pairs, arrived))


def decays(log_decay, width):
    heads, block = log_decay.shape
    upper = jnp.where(iota((block, block), 0) <= iota((block, block), 1), 1.0, 0.0)
    lower = jnp.where(iota((block, block), 0) >= iota((block, block), 1), 1.0, 0.0)
    padded = jnp.concatenate([log_decay, jnp.zeros((8 - heads, block), f32)], axis=0)
    rows = dot(padded, upper, precision=EXACT)
    columns = dot(lower, padded, NT, precision=EXACT)
    return rows, columns


def over_heads(columns, heads, width):
    n = columns.shape[0]
    head_of = quotient(iota((n, width), 1), width // heads)
    wide = jnp.broadcast_to(columns[:, 0:1], (n, width))
    for h in range(1, heads):
        wide = jnp.where(head_of == h, jnp.broadcast_to(columns[:, h : h + 1], (n, width)), wide)
    return wide


def diagonal_heads(square, heads):
    width = square.shape[1]
    size = width // heads
    head_of = quotient(iota((size, width), 1), size)
    out = square[0:size, :]
    for h in range(1, heads):
        out = jnp.where(head_of == h, square[h * size : (h + 1) * size, :], out)
    return out


def block_diagonal(state, heads):
    size, width = state.shape
    head_of = quotient(iota((size, width), 1), width // heads)
    return jnp.concatenate([where_bf16(head_of == h, state) for h in range(heads)], axis=0)


def project_kernel(
    at_ref,
    slot_hbm,
    answered_ref,
    quot_hbm,
    wq_hbm,
    wk_hbm,
    wv_hbm,
    wide_hbm,
    dmixed_hbm,
    rem_hbm,
    payload_hbm,
    slot_ref,
    quot_ref,
    wq_ref,
    wk_ref,
    wv_ref,
    wide_ref,
    dmixed_ref,
    rem_ref,
    states_ref,
    arrived,
    *,
    users,
    heads,
):
    slots, width = answered_ref.shape
    block = quot_ref.shape[0] // users
    peers = payload_hbm.shape[0]
    size = width // heads
    me = at_ref[0]
    ends = []
    copies = begin(
        (
            (slot_hbm, slot_ref),
            (quot_hbm, quot_ref),
            (wq_hbm, wq_ref),
            (wk_hbm, wk_ref),
            (wv_hbm, wv_ref),
            (wide_hbm, wide_ref),
            (dmixed_hbm, dmixed_ref),
        ),
        arrived,
    )
    finish(copies[:1])
    hot = [tiled_match(spread_column(slot_ref[u : u + 1, :]), slots) for u in range(users)]
    finish(copies[1:5])
    waits, copies = copies[5:], []
    for u in range(users):
        at = slice(u * block, (u + 1) * block)
        rem_ref[at, :] = dot(hot[u], answered_ref[...]).astype(bf16)
        copies += begin([(rem_ref.at[at, :], rem_hbm.at[at, :])], arrived, 8 + u)
        embedded = (quot_ref[at, :].astype(f32) * rem_ref[at, :].astype(f32)).astype(bf16)
        q = dot(embedded, wq_ref[...]).astype(bf16)
        k = dot(embedded, wk_ref[...]).astype(bf16)
        v = dot(embedded, wv_ref[...]).astype(bf16)
        if u == 0:
            finish(waits)
        wide = wide_ref[at, :]
        end = wide[block - 1 : block, :]
        ends.append(end)
        falling = (k.astype(f32) * jnp.exp(end - wide)).astype(bf16)
        growing = (q.astype(f32) * jnp.exp(wide)).astype(bf16)
        state = diagonal_heads(dot(falling, v, TN), heads).astype(bf16)
        grad = diagonal_heads(dot(growing, dmixed_ref[at, :], TN), heads).astype(bf16)
        states_ref[0, u * size : (u + 1) * size, :] = state
        states_ref[1, u * size : (u + 1) * size, :] = grad
    rows = iota((16, width), 0)
    tail = jnp.zeros((16, width), f32)
    for u in range(users):
        left = ends[u]
        for part in range(3):
            piece = left.astype(bf16).astype(f32)
            left = left - piece
            tail = jnp.where(rows == part * users + u, piece, tail)
    tail = tail.astype(bf16)
    states_ref[0, users * size :, :] = tail
    states_ref[1, users * size :, :] = tail
    which = [jnp.where(peer > me, 0, 1) for peer in range(peers)]
    pairs = [(states_ref.at[which[peer]], payload_hbm.at[peer]) for peer in range(peers)]
    finish(copies + begin(pairs, arrived, 8 + users))


def within_kernel(
    quot_ref,
    rem_ref,
    dmixed_ref,
    decay_ref,
    wq_ref,
    wk_ref,
    wv_ref,
    out_hbm,
    out_ref,
    arrived,
    *,
    scale,
):
    users, heads, block = decay_ref.shape
    width = quot_ref.shape[1]
    copies = []
    head_of = quotient(iota((block, width), 1), width // heads)
    lower_tri = iota((block, block), 0) >= iota((block, block), 1)
    for u in range(users):
        at = slice(u * block, (u + 1) * block)
        embedded = (quot_ref[at, :].astype(f32) * rem_ref[at, :].astype(f32)).astype(bf16)
        q = dot(embedded, wq_ref[...]).astype(bf16)
        k = dot(embedded, wk_ref[...]).astype(bf16)
        v = dot(embedded, wv_ref[...]).astype(bf16)
        dmixed = dmixed_ref[at, :]
        rows, columns = decays(decay_ref[u], width)
        mixed = jnp.zeros((block, width), f32)
        dq = jnp.zeros((block, width), f32)
        dk = jnp.zeros((block, width), f32)
        dv = jnp.zeros((block, width), f32)
        zero = jnp.zeros((), bf16)
        for h in range(heads):
            own = head_of == h
            q_h = jnp.where(own, q, zero)
            k_h = jnp.where(own, k, zero)
            v_h = jnp.where(own, v, zero)
            d_h = jnp.where(own, dmixed, zero)
            gap = columns[:, h : h + 1] - rows[h : h + 1, :]
            mask = jnp.where(lower_tri, scale * jnp.exp(jnp.minimum(gap, 0.0)), 0.0)
            weights = (dot(q_h, k, NT) * mask).astype(bf16)
            dweights = (dot(d_h, v, NT) * mask).astype(bf16)
            mixed = mixed + dot(weights, v_h)
            dq = dq + dot(dweights, k_h)
            dk = dk + dot(dweights, q_h, TN)
            dv = dv + dot(weights, d_h, TN)
        for i, part in enumerate((mixed, dq, dk, dv)):
            out_ref[i, at, :] = part
        copies += begin([(out_ref.at[:, at, :], out_hbm.at[:, at, :])], arrived, u)
    finish(copies)


def sum_half(ids, terms, owner, out_ref):
    half = out_ref.shape[0]
    chunk = min(256, half)
    for j, hot in enumerate(stacked_match(ids - owner * half, chunk, half // chunk)):
        out_ref[j * chunk : (j + 1) * chunk, :] = dot(hot, terms).astype(out_ref.dtype)


def gradient_kernel(
    at_ref,
    payload_ref,
    within_hbm,
    dmixed_hbm,
    wide_hbm,
    rem_hbm,
    quot_hbm,
    slot_hbm,
    ids_hbm,
    wq_hbm,
    wk_hbm,
    wv_hbm,
    w_out_hbm,
    out_hbm,
    rem_send_hbm,
    keep_hbm,
    give_hbm,
    within_ref,
    dmixed_ref,
    wide_ref,
    rem_ref,
    quot_ref,
    slot_ref,
    ids_ref,
    wq_ref,
    wk_ref,
    wv_ref,
    w_out_ref,
    out_ref,
    rem_send_ref,
    keep_ref,
    give_ref,
    arrived,
    *,
    scale,
    heads,
):
    users, block = ids_ref.shape
    width = quot_ref.shape[1]
    copies = begin(
        (
            (quot_hbm, quot_ref),
            (rem_hbm, rem_ref),
            (wq_hbm, wq_ref),
            (wk_hbm, wk_ref),
            (wv_hbm, wv_ref),
            (wide_hbm, wide_ref),
            (dmixed_hbm, dmixed_ref),
            (w_out_hbm, w_out_ref),
            (slot_hbm, slot_ref),
            (ids_hbm, ids_ref),
        ),
        arrived,
    )
    waits = []
    for u in range(users):
        at = slice(u * block, (u + 1) * block)
        waits += begin([(within_hbm.at[:, at, :], within_ref.at[:, at, :])], arrived, 11 + u)
    peers = payload_ref.shape[0]
    size = width // heads
    slots = rem_send_ref.shape[0]
    me = at_ref[0]
    carried = []
    for u in range(users):
        ends = []
        for peer in range(peers):
            tail = payload_ref[peer, users * size :, :].astype(f32)
            ends.append(
                tail[u : u + 1, :]
                + tail[users + u : users + u + 1, :]
                + tail[2 * users + u : 2 * users + u + 1, :]
            )
        entering = jnp.zeros((size, width), f32)
        for peer in range(peers):
            part = payload_ref[peer, u * size : (u + 1) * size, :].astype(f32)
            linked = jnp.exp(ends[peer]) * entering + part
            entering = jnp.where(peer < me, linked, entering)
        leaving = jnp.zeros((size, width), f32)
        for peer in reversed(range(peers)):
            part = payload_ref[peer, u * size : (u + 1) * size, :].astype(f32)
            linked = jnp.exp(ends[peer]) * leaving + part
            leaving = jnp.where(peer > me, linked, leaving)
        carried.append((block_diagonal(entering, heads), block_diagonal(leaving, heads)))
    finish(copies)
    copies = []
    rem_terms, quot_terms = [], []
    for u in range(users):
        at = slice(u * block, (u + 1) * block)
        entering, leaving = carried[u]
        embedded = (quot_ref[at, :].astype(f32) * rem_ref[at, :].astype(f32)).astype(bf16)
        q = dot(embedded, wq_ref[...]).astype(bf16)
        k = dot(embedded, wk_ref[...]).astype(bf16)
        v = dot(embedded, wv_ref[...]).astype(bf16)
        dmixed = dmixed_ref[at, :]
        wide = wide_ref[at, :]
        finish(waits[u : u + 1])
        growth = scale * jnp.exp(wide)
        falloff = scale * jnp.exp(wide[block - 1 : block, :] - wide)
        mixed = (within_ref[0, at, :] + growth * dot(q, entering)).astype(bf16)
        out_ref[u] = dot(mixed, w_out_ref[...]).astype(bf16)
        copies += begin([(out_ref.at[u], out_hbm.at[u])], arrived, 11 + users + u)
        dq = (within_ref[1, at, :] + growth * dot(dmixed, entering, NT)).astype(bf16)
        dk = (within_ref[2, at, :] + falloff * dot(v, leaving, NT)).astype(bf16)
        dv = (within_ref[3, at, :] + falloff * dot(k, leaving)).astype(bf16)
        dembedded = dot(dq, wq_ref[...], NT) + dot(dk, wk_ref[...], NT) + dot(dv, wv_ref[...], NT)
        rem_terms.append((dembedded * quot_ref[at, :].astype(f32)).astype(bf16))
        quot_terms.append((dembedded * rem_ref[at, :].astype(f32)).astype(bf16))
    rem_terms = jnp.concatenate(rem_terms, axis=0)
    quot_terms = jnp.concatenate(quot_terms, axis=0)
    slot = jnp.concatenate([slot_ref[u : u + 1, :] for u in range(users)], axis=1)
    ids = jnp.concatenate([ids_ref[u : u + 1, :] for u in range(users)], axis=1)
    n = 11 + 2 * users
    for j, hot in enumerate(stacked_match(slot, block, slots // block)):
        at = slice(j * block, (j + 1) * block)
        rem_send_ref[at, :] = dot(hot, rem_terms).astype(bf16)
        copies += begin([(rem_send_ref.at[at, :], rem_send_hbm.at[at, :])], arrived, n + j)
    n += slots // block
    for ref, hbm, owner in ((give_ref, give_hbm, 1 - me % 2), (keep_ref, keep_hbm, me % 2)):
        half = ref.shape[0]
        for j, hot in enumerate(stacked_match(ids - owner * half, block, half // block)):
            at = slice(j * block, (j + 1) * block)
            ref[at, :] = dot(hot, quot_terms).astype(bf16)
            copies += begin([(ref.at[at, :], hbm.at[at, :])], arrived, n)
            n += 1
    finish(copies)


def collect_kernel(at_ref, wanted_ref, back_ref, keep_ref, give_ref, *, per):
    shards, _, lanes = wanted_ref.shape
    slots = shards * per
    wanted = jnp.where(iota((shards, lanes), 1) < per, wanted_ref[:, 0, :], 0)
    high, low = halves(wanted)
    tile = where_bf16(remainder(iota((lanes, slots), 1), per) == iota((lanes, slots), 0), 1.0)
    own = quotient(iota((shards, slots), 1), per) == iota((shards, slots), 0)
    high = jnp.sum(jnp.where(own, dot(high.astype(bf16), tile), 0.0), axis=0, keepdims=True)
    low = jnp.sum(jnp.where(own, dot(low.astype(bf16), tile), 0.0), axis=0, keepdims=True)
    row = (16.0 * high + low).astype(i32) - 1
    sum_half(row, back_ref[...], 1 - at_ref[0] % 2, give_ref)
    sum_half(row, back_ref[...], at_ref[0] % 2, keep_ref)


def split_kernel(at_ref, keep_ref, got_ref, *refs, chips):
    out_refs = refs[:chips]
    rows = out_refs[0].shape[0]
    bases = [
        pl.multiple_of(lax.rem(at_ref[0] // 2 + d, chips) * rows, rows) for d in range(chips)
    ]
    copies = []
    if len(refs) > chips:
        near_ref, arrived = refs[chips:]
        copies = begin([(keep_ref.at[pl.ds(b, rows), :], near_ref.at[d]) for d, b in enumerate(bases)], arrived)
    for d, out_ref in enumerate(out_refs):
        finish(copies[d : d + 1])
        kept = near_ref[d] if copies else keep_ref[pl.ds(bases[d], rows), :]
        both = kept.astype(f32) + got_ref[pl.ds(bases[d], rows), :].astype(f32)
        out_ref[...] = both.astype(bf16)


def cut(chunk, shards):
    rows, width = chunk.shape
    lanes = width // 128
    part = rows * lanes // shards
    return [
        chunk[i // lanes * part : (i // lanes + 1) * part, i % lanes * 128 : (i % lanes + 1) * 128]
        for i in range(shards)
    ]


def total_kernel(*refs):
    total = sum((ref[...].astype(f32) for ref in refs[1:-1]), refs[0][...].astype(f32))
    for i, tile in enumerate(cut(total, refs[-1].shape[0])):
        refs[-1][i] = tile.astype(bf16)


def repeat_kernel(tiles_ref, out_ref):
    total = jnp.sum(tiles_ref[...].astype(f32), axis=0).astype(bf16)
    for i in range(out_ref.shape[0]):
        out_ref[i] = total


def place_kernel(at_ref, wanted_ref, *refs, chips, per, total, other):
    out_hbm, out_ref, arrived = refs[-3:]
    chunks = refs[:chips]
    copies = []
    _, rows, width = out_ref.shape
    shards, _, lanes = wanted_ref.shape
    counted = jnp.where(iota((shards, lanes), 1) == per, wanted_ref[:, 0, :], 0)
    ratio = total / jnp.sum(counted.astype(f32), axis=(0, 1), keepdims=True)
    chip, core = at_ref[0] // 2, at_ref[0] % 2
    half = core + other - 2 * core * other
    for d, chunk in enumerate(chunks):
        spot = half * chips + lax.rem(chip + chips - d, chips)
        base = pl.multiple_of(spot * rows, rows)
        if len(chunk.shape) == 2:
            out_ref[d] = ratio * chunk[...].astype(f32)
        else:
            part = chunk.shape[1]
            for i in range(shards):
                across = i % (width // 128) * 128
                down = i // (width // 128) * part
                tile = ratio * chunk[i].astype(f32)
                out_ref[d, down : down + part, across : across + 128] = tile
        copies += begin([(out_ref.at[d], out_hbm.at[pl.ds(base, rows), :])], arrived, d)
    finish(copies)


def exchange(array, axis):
    return lax.all_to_all(array, axis, split_axis=0, concat_axis=0, tiled=True)


def to_core(array):
    peers = lax.axis_size("hist")
    return lax.ppermute(array, "hist", [(i, i ^ 1) for i in range(peers)])


def to_chip(array, steps):
    peers = lax.axis_size("hist")
    return lax.ppermute(array, "hist", [(i, (i + 2 * steps) % peers) for i in range(peers)])


def split(at, keep, give, spec=VM):
    chips = lax.axis_size("hist") // 2
    rows, width = keep.shape[0] // chips, keep.shape[1]
    kernel = functools.partial(split_kernel, chips=chips)
    scratch = [pltpu.VMEM((chips, rows, width), keep.dtype), dma(chips)] if spec is HB else []
    args = (at, keep, to_core(give))
    return call(kernel, [((rows, width), bf16)] * chips, args, [SM, spec, VM], scratch)


def shared(chunks):
    return [chunks[0]] + [to_chip(chunks[d], d) for d in range(1, len(chunks))]


def along_chips(chunk):
    chips = lax.axis_size("hist") // 2
    return [chunk] + [to_chip(chunk, d) for d in range(1, chips)]


def place(at, wanted, chunks, rows, width, per, total, out=None):
    chips = len(chunks)
    scratch = [pltpu.VMEM((chips, rows // (2 * chips), width), f32), dma(chips)]
    other = 0 if out is None else 1
    kernel = functools.partial(place_kernel, chips=chips, per=per, total=total, other=other)
    args, specs, aliases = (at, wanted, *chunks), [SM] + [VM] * (1 + chips), {}
    if other:
        args, specs, aliases = args + (out,), specs + [HB], {len(args): 0}
    (out,) = call(kernel, [((rows, width), f32)], args, specs, scratch, [HB], aliases=aliases)
    return out


def body(
    quot_ids,
    rem_ids,
    lengths,
    log_decay,
    quot_table,
    rem_table,
    w_query,
    w_key,
    w_value,
    w_out,
    cotangent,
):
    users, block = quot_ids.shape
    rows_all, width = quot_table.shape
    heads = log_decay.shape[1]
    size = width // heads
    shards = lax.axis_size("user")
    peers = lax.axis_size("hist")
    rows_own = rem_table.shape[0]
    cap = 2 * block // shards
    per = users * cap
    slots = shards * per
    scale = 1.0 / math.sqrt(size * block * peers)
    at = lax.axis_index("hist").astype(i32).reshape(1)
    lanes = (per // 128 + 1) * 128

    events = pltpu.VMEM((users * block, width), bf16)
    square = pltpu.VMEM((width, width), bf16)
    requests, slot = call(
        functools.partial(request_kernel, rows_own=rows_own, cap=cap),
        [((shards, 1, lanes), i32), ((8, block), i32)],
        (in_hbm(lengths), in_hbm(rem_ids)),
        [SM, VM],
        [pltpu.VMEM((8, block), i32), dma(1)],
        [VM, HB],
        MOST,
    )
    wanted = exchange(requests, "user")
    quot_emb, dmixed, wide = call(
        quotient_kernel,
        [
            ((users * block, width), bf16),
            ((users * block, width), bf16),
            ((users * block, width), f32),
        ],
        (lengths, at, quot_ids, quot_table, cotangent, log_decay, w_out),
        [SM, SM] + [VM] * 5,
        [events, events, pltpu.VMEM((users * block, width), f32), dma(3)],
        [HB] * 3,
        FULL,
    )
    (found,) = call(
        functools.partial(answer_kernel, per=per),
        [((slots, width), bf16)],
        (wanted, rem_table),
        [VM, HB],
        [
            pltpu.VMEM((rows_own, width), bf16),
            pltpu.VMEM((slots, width), bf16),
            dma(5),
        ],
        [HB],
        MOST,
    )
    answered = exchange(found.reshape(shards, per, width), "user").reshape(slots, width)
    rem_emb, payload = call(
        functools.partial(project_kernel, users=users, heads=heads),
        [((users * block, width), bf16), ((peers, users * size + 16, width), bf16)],
        (at, slot, answered, quot_emb, w_query, w_key, w_value, wide, dmixed),
        [SM, HB, VM] + [HB] * 6,
        [pltpu.VMEM((8, block), i32), events]
        + [square] * 3
        + [pltpu.VMEM((users * block, width), f32), events, events]
        + [pltpu.VMEM((2, users * size + 16, width), bf16), dma(8 + users + peers)],
        [HB, HB],
        MOST,
    )
    states = exchange(payload, "hist")
    parts = (4, users * block, width)
    (within,) = call(
        functools.partial(within_kernel, scale=scale),
        [(parts, f32)],
        (quot_emb, rem_emb, dmixed, log_decay, w_query, w_key, w_value),
        scratch=[pltpu.VMEM(parts, f32), dma(users)],
        out_specs=[HB],
        limit=FULL,
    )
    output, rem_send, keep, give = call(
        functools.partial(gradient_kernel, scale=scale, heads=heads),
        [
            ((users, block, width), bf16),
            ((slots, width), bf16),
            ((rows_all // 2, width), bf16),
            ((rows_all // 2, width), bf16),
        ],
        (at, states, within, dmixed, wide, rem_emb, quot_emb, slot, quot_ids)
        + (w_query, w_key, w_value, w_out),
        [SM, VM] + [HB] * 11,
        [pltpu.VMEM(parts, f32), events]
        + [pltpu.VMEM((users * block, width), f32), events, events]
        + [pltpu.VMEM((8, block), i32), pltpu.VMEM((users, block), i32)]
        + [square] * 4
        + [pltpu.VMEM((users, block, width), bf16), pltpu.VMEM((slots, width), bf16)]
        + [pltpu.VMEM((rows_all // 2, width), bf16)] * 2
        + [dma(11 + 2 * users + (slots + rows_all) // block)],
        [HB] * 4,
        MOST,
    )
    rem_back = exchange(rem_send.reshape(shards, per, width), "user").reshape(slots, width)
    tiles = (shards, rows_all // peers * width // shards // 128, 128)
    (quot_tiles,) = call(total_kernel, [(tiles, bf16)], shared(split(at, keep, give, HB)))
    rem_back, quot_tiles = lax.optimization_barrier((rem_back, quot_tiles))
    quot_back = exchange(quot_tiles, "user")
    keep, give = call(
        functools.partial(collect_kernel, per=per),
        [((rows_own // 2, width), f32), ((rows_own // 2, width), bf16)],
        (at, wanted, rem_back),
        [SM, VM, VM],
    )
    chunks = split(at, keep, give)
    (quot_tiles,) = call(repeat_kernel, [(tiles, bf16)], (quot_back,))
    quot_tiles, *_ = lax.optimization_barrier((quot_tiles, *chunks))
    quot_tiles = exchange(quot_tiles, "user")
    rem_sum = sum(c.astype(f32) for c in shared(chunks)).astype(bf16)
    rem_mine = along_chips(rem_sum)
    quot_tiles, _ = lax.optimization_barrier((quot_tiles, rem_sum))
    total = float(users * shards * block * peers)
    rem_grad = place(at, wanted, rem_mine, rows_own, width, per, total)
    quot_mine = along_chips(quot_tiles)
    rem_theirs = [to_core(c) for c in rem_mine]
    *quot_mine, rem_grad = lax.optimization_barrier((*quot_mine, rem_grad))
    rem_grad = place(at, wanted, rem_theirs, rows_own, width, per, total, rem_grad)
    quot_theirs = [to_core(c) for c in quot_mine]
    quot_grad = place(at, wanted, quot_mine, rows_all, width, per, total)
    quot_grad = place(at, wanted, quot_theirs, rows_all, width, per, total, quot_grad)
    return (output, quot_grad, rem_grad)


def solution(mesh):
    return jax.shard_map(
        body,
        mesh=mesh,
        in_specs=(
            P("user", "hist"),
            P("user", "hist"),
            P("user"),
            P("user", None, "hist"),
            P(),
            P("user", None),
            P(),
            P(),
            P(),
            P(),
            P("user", "hist", None),
        ),
        out_specs=(P("user", "hist", None), P(), P("user", None)),
        check_vma=False,
    )
```

```python
import functools
import math

import jax
import jax.numpy as jnp
from jax import lax
from jax.experimental import pallas as pl
from jax.experimental.pallas import tpu as pltpu
from jax.sharding import PartitionSpec as P

f32 = jnp.float32
bf16 = jnp.bfloat16
i32 = jnp.int32
FULL = 62
MOST = 24
EXACT = lax.Precision.HIGHEST
VM = pl.BlockSpec(memory_space=pltpu.VMEM)
SM = pl.BlockSpec(memory_space=pltpu.SMEM)
HB = pl.BlockSpec(memory_space=pltpu.HBM)
IN_VM = pl.BlockSpec(memory_space=pltpu.VMEM)

NN = (((1,), (0,)), ((), ()))
NT = (((1,), (1,)), ((), ()))
TN = (((0,), (0,)), ((), ()))


def dot(a, b, dims=NN, precision=None):
    return lax.dot_general(a, b, dims, preferred_element_type=f32, precision=precision)


def iota(shape, dim):
    return lax.broadcasted_iota(i32, shape, dim)


def quotient(a, n):
    return a >> (n.bit_length() - 1) if n & (n - 1) == 0 else a // n


def remainder(a, n):
    return a & (n - 1) if n & (n - 1) == 0 else a % n


def where_bf16(mask, a):
    return jnp.where(mask, a, 0.0).astype(bf16)


def halves(whole):
    return (whole >> 4).astype(f32), (whole & 15).astype(f32)


def spread_column(row):
    n = row.shape[1]
    diagonal = iota((n, n), 0) == iota((n, n), 1)
    high, low = halves(row)
    ones = jnp.ones((n, 128), bf16)
    column = 16.0 * dot(where_bf16(diagonal, high), ones) + dot(where_bf16(diagonal, low), ones)
    return column.astype(i32)


def tiled_match(column, width):
    near = where_bf16(iota(column.shape, 1) == (column & 127), 1.0)
    tile = (column >> 7).astype(f32).astype(bf16)
    zero = jnp.zeros_like(near)
    parts = [jnp.where(tile == jnp.asarray(j, bf16), near, zero) for j in range(width // 128)]
    return jnp.concatenate(parts, axis=1)


def stacked_match(row, chunk, count):
    row = jnp.broadcast_to(row, (chunk, row.shape[1]))
    near = where_bf16(iota(row.shape, 0) == (row & (chunk - 1)), 1.0)
    part = (row >> (chunk.bit_length() - 1)).astype(f32).astype(bf16)
    zero = jnp.zeros_like(near)
    return [jnp.where(part == jnp.asarray(j, bf16), near, zero) for j in range(count)]


def begin(pairs, arrived, at=0):
    copies = [
        pltpu.make_async_copy(source, target, arrived.at[at + i])
        for i, (source, target) in enumerate(pairs)
    ]
    for copy in copies:
        copy.start()
    return copies


def finish(copies):
    for copy in copies:
        copy.wait()


def dma(n):
    return pltpu.SemaphoreType.DMA((n,))


def held(spec):
    return pltpu.HBM if spec is HB else pltpu.VMEM if spec is IN_VM else None


def in_hbm(array):
    return pltpu.with_memory_space_constraint(array, pltpu.HBM)


def call(kernel, outs, args, specs=None, scratch=(), out_specs=None, limit=16, aliases={}):
    out_specs = out_specs if out_specs is not None else [VM] * len(outs)
    shapes = [
        held(spec)(s, d) if held(spec) else jax.ShapeDtypeStruct(s, d)
        for (s, d), spec in zip(outs, out_specs, strict=True)
    ]
    specs = specs if specs is not None else [VM] * len(args)
    args = [
        pltpu.with_memory_space_constraint(a, held(spec)) if held(spec) else a
        for a, spec in zip(args, specs, strict=True)
    ]
    return pl.pallas_call(
        kernel,
        out_shape=tuple(shapes),
        in_specs=specs,
        out_specs=tuple(out_specs),
        input_output_aliases=aliases,
        scratch_shapes=list(scratch),
        compiler_params=pltpu.CompilerParams(vmem_limit_bytes=limit * 1024 * 1024),
    )(*args)


def request_kernel(
    len_ref, ids_ref, table_hbm, out_ref, slot_hbm, table_ref, slot_ref, arrived, *, rows_own, cap
):
    tables = begin([(table_hbm, table_ref)], arrived, 1)
    users, block = ids_ref.shape
    shards, _, lanes = out_ref.shape
    shift = rows_own.bit_length() - 1
    earlier = where_bf16(iota((block, block), 0) < iota((block, block), 1), 1.0)
    place = iota((lanes, block), 0)
    total = jnp.zeros((shards, lanes), f32)
    count = jnp.int32(0)
    slot_ref[...] = jnp.zeros_like(slot_ref)
    for u in range(users):
        ids = ids_ref[u : u + 1, :]
        owner = ids >> shift
        named = iota((shards, block), 0) == owner
        named_16 = where_bf16(named, 1.0)
        before = dot(named_16, earlier)
        rank = jnp.sum(jnp.where(named, before, 0.0), axis=0, keepdims=True).astype(i32)
        high, low = halves((ids & (rows_own - 1)) + 1)
        chosen = place == rank + u * cap
        total = total + 16.0 * dot(named_16, where_bf16(chosen, high), NT)
        total = total + dot(named_16, where_bf16(chosen, low), NT)
        slot_ref[u : u + 1, :] = (owner * users + u) * cap + rank
        count = count + len_ref[u]
    copies = begin([(slot_ref, slot_hbm)], arrived)
    wanted = jnp.where(iota((shards, lanes), 1) == users * cap, count, total.astype(i32))
    out_ref[:, 0, :] = wanted
    finish(copies + tables)


def answer_kernel(
    wanted_ref, table_ref, out_hbm, out_ref, arrived, *, per
):
    shards, _, lanes = wanted_ref.shape
    parts = 4
    group = shards // parts
    slots = group * per
    rows = table_ref.shape[0]
    repeat = where_bf16(quotient(iota((slots, group), 0), per) == iota((slots, group), 1), 1.0)
    own = remainder(iota((slots, lanes), 0), per) == iota((slots, lanes), 1)
    ones = jnp.ones((lanes, 128), bf16)
    wanted = jnp.where(iota((shards, lanes), 1) < per, wanted_ref[:, 0, :], 0)
    stores = []
    for j in range(parts):
        high, low = halves(wanted[j * group : (j + 1) * group, :])
        high = dot(where_bf16(own, dot(repeat, high.astype(bf16))), ones)
        low = dot(where_bf16(own, dot(repeat, low.astype(bf16))), ones)
        column = (16.0 * high + low).astype(i32) - 1
        hot = tiled_match(column, rows)
        at = slice(j * slots, (j + 1) * slots)
        out_ref[at, :] = dot(hot, table_ref[...]).astype(bf16)
        stores += begin([(out_ref.at[at, :], out_hbm.at[at, :])], arrived, j)
    finish(stores)


def quotient_kernel(
    len_ref,
    at_ref,
    ids_ref,
    table_ref,
    cot_ref,
    decay_ref,
    w_out_ref,
    quot_ref,
    dmixed_ref,
    wide_ref,
):
    users, block = ids_ref.shape
    heads = decay_ref.shape[1]
    rows, width = table_ref.shape
    for u in range(users):
        at = slice(u * block, (u + 1) * block)
        hot = tiled_match(spread_column(ids_ref[u : u + 1, :]), rows)
        quot_ref[at, :] = dot(hot, table_ref[...]).astype(bf16)
        valid = at_ref[0] * block + iota((block, width), 0) < len_ref[u]
        masked = jnp.where(valid, cot_ref[u].astype(f32), 0.0).astype(bf16)
        dmixed_ref[at, :] = dot(masked, w_out_ref[...], NT).astype(bf16)
        _, columns = decays(decay_ref[u], width)
        wide_ref[at, :] = over_heads(columns, heads, width)


def decays(log_decay, width):
    heads, block = log_decay.shape
    upper = jnp.where(iota((block, block), 0) <= iota((block, block), 1), 1.0, 0.0)
    lower = jnp.where(iota((block, block), 0) >= iota((block, block), 1), 1.0, 0.0)
    padded = jnp.concatenate([log_decay, jnp.zeros((8 - heads, block), f32)], axis=0)
    rows = dot(padded, upper, precision=EXACT)
    columns = dot(lower, padded, NT, precision=EXACT)
    return rows, columns


def over_heads(columns, heads, width):
    n = columns.shape[0]
    head_of = quotient(iota((n, width), 1), width // heads)
    wide = jnp.broadcast_to(columns[:, 0:1], (n, width))
    for h in range(1, heads):
        wide = jnp.where(head_of == h, jnp.broadcast_to(columns[:, h : h + 1], (n, width)), wide)
    return wide


def diagonal_heads(square, heads):
    width = square.shape[1]
    size = width // heads
    head_of = quotient(iota((size, width), 1), size)
    out = square[0:size, :]
    for h in range(1, heads):
        out = jnp.where(head_of == h, square[h * size : (h + 1) * size, :], out)
    return out


def block_diagonal(state, heads):
    size, width = state.shape
    head_of = quotient(iota((size, width), 1), width // heads)
    return jnp.concatenate([where_bf16(head_of == h, state) for h in range(heads)], axis=0)


def project_kernel(
    at_ref,
    slot_hbm,
    answered_ref,
    quot_ref,
    wq_hbm,
    wk_hbm,
    wv_hbm,
    wide_ref,
    dmixed_ref,
    rem_ref,
    payload_hbm,
    slot_ref,
    wq_ref,
    wk_ref,
    wv_ref,
    states_ref,
    arrived,
    *,
    users,
    heads,
):
    slots, width = answered_ref.shape
    block = quot_ref.shape[0] // users
    peers = payload_hbm.shape[0]
    size = width // heads
    me = at_ref[0]
    ends = []
    copies = begin(
        (
            (slot_hbm, slot_ref),
            (wq_hbm, wq_ref),
            (wk_hbm, wk_ref),
            (wv_hbm, wv_ref),
        ),
        arrived,
    )
    finish(copies[:1])
    hot = [tiled_match(spread_column(slot_ref[u : u + 1, :]), slots) for u in range(users)]
    finish(copies[1:])
    for u in range(users):
        at = slice(u * block, (u + 1) * block)
        rem_ref[at, :] = dot(hot[u], answered_ref[...]).astype(bf16)
        embedded = (quot_ref[at, :].astype(f32) * rem_ref[at, :].astype(f32)).astype(bf16)
        q = dot(embedded, wq_ref[...]).astype(bf16)
        k = dot(embedded, wk_ref[...]).astype(bf16)
        v = dot(embedded, wv_ref[...]).astype(bf16)
        wide = wide_ref[at, :]
        end = wide[block - 1 : block, :]
        ends.append(end)
        falling = (k.astype(f32) * jnp.exp(end - wide)).astype(bf16)
        growing = (q.astype(f32) * jnp.exp(wide)).astype(bf16)
        state = diagonal_heads(dot(falling, v, TN), heads).astype(bf16)
        grad = diagonal_heads(dot(growing, dmixed_ref[at, :], TN), heads).astype(bf16)
        states_ref[0, u * size : (u + 1) * size, :] = state
        states_ref[1, u * size : (u + 1) * size, :] = grad
    rows = iota((16, width), 0)
    tail = jnp.zeros((16, width), f32)
    for u in range(users):
        left = ends[u]
        for part in range(3):
            piece = left.astype(bf16).astype(f32)
            left = left - piece
            tail = jnp.where(rows == part * users + u, piece, tail)
    tail = tail.astype(bf16)
    states_ref[0, users * size :, :] = tail
    states_ref[1, users * size :, :] = tail
    which = [jnp.where(peer > me, 0, 1) for peer in range(peers)]
    pairs = [(states_ref.at[which[peer]], payload_hbm.at[peer]) for peer in range(peers)]
    finish(begin(pairs, arrived, 4))


def within_kernel(
    quot_ref,
    rem_ref,
    dmixed_ref,
    decay_ref,
    wq_ref,
    wk_ref,
    wv_ref,
    out_hbm,
    out_ref,
    arrived,
    *,
    scale,
):
    users, heads, block = decay_ref.shape
    width = quot_ref.shape[1]
    copies = []
    head_of = quotient(iota((block, width), 1), width // heads)
    lower_tri = iota((block, block), 0) >= iota((block, block), 1)
    for u in range(users):
        at = slice(u * block, (u + 1) * block)
        embedded = (quot_ref[at, :].astype(f32) * rem_ref[at, :].astype(f32)).astype(bf16)
        q = dot(embedded, wq_ref[...]).astype(bf16)
        k = dot(embedded, wk_ref[...]).astype(bf16)
        v = dot(embedded, wv_ref[...]).astype(bf16)
        dmixed = dmixed_ref[at, :]
        rows, columns = decays(decay_ref[u], width)
        mixed = jnp.zeros((block, width), f32)
        dq = jnp.zeros((block, width), f32)
        dk = jnp.zeros((block, width), f32)
        dv = jnp.zeros((block, width), f32)
        zero = jnp.zeros((), bf16)
        for h in range(heads):
            own = head_of == h
            q_h = jnp.where(own, q, zero)
            k_h = jnp.where(own, k, zero)
            v_h = jnp.where(own, v, zero)
            d_h = jnp.where(own, dmixed, zero)
            gap = columns[:, h : h + 1] - rows[h : h + 1, :]
            mask = jnp.where(lower_tri, scale * jnp.exp(jnp.minimum(gap, 0.0)), 0.0)
            weights = (dot(q_h, k, NT) * mask).astype(bf16)
            dweights = (dot(d_h, v, NT) * mask).astype(bf16)
            mixed = mixed + dot(weights, v_h)
            dq = dq + dot(dweights, k_h)
            dk = dk + dot(dweights, q_h, TN)
            dv = dv + dot(weights, d_h, TN)
        for i, part in enumerate((mixed, dq, dk, dv)):
            out_ref[i, at, :] = part
        copies += begin([(out_ref.at[:, at, :], out_hbm.at[:, at, :])], arrived, u)
    finish(copies)


def sum_half(ids, terms, owner, out_ref):
    half = out_ref.shape[0]
    chunk = min(256, half)
    for j, hot in enumerate(stacked_match(ids - owner * half, chunk, half // chunk)):
        out_ref[j * chunk : (j + 1) * chunk, :] = dot(hot, terms).astype(out_ref.dtype)


def gradient_kernel(
    at_ref,
    payload_ref,
    within_hbm,
    dmixed_ref,
    wide_ref,
    rem_ref,
    quot_ref,
    slot_hbm,
    ids_hbm,
    wq_hbm,
    wk_hbm,
    wv_hbm,
    w_out_hbm,
    out_hbm,
    rem_send_hbm,
    keep_ref,
    give_ref,
    within_ref,
    slot_ref,
    ids_ref,
    wq_ref,
    wk_ref,
    wv_ref,
    w_out_ref,
    out_ref,
    rem_send_ref,
    arrived,
    *,
    scale,
    heads,
):
    users, block = ids_ref.shape
    width = quot_ref.shape[1]
    copies = begin(
        (
            (wq_hbm, wq_ref),
            (wk_hbm, wk_ref),
            (wv_hbm, wv_ref),
            (w_out_hbm, w_out_ref),
            (slot_hbm, slot_ref),
            (ids_hbm, ids_ref),
        ),
        arrived,
    )
    waits = []
    for u in range(users):
        at = slice(u * block, (u + 1) * block)
        waits += begin([(within_hbm.at[:, at, :], within_ref.at[:, at, :])], arrived, 6 + u)
    peers = payload_ref.shape[0]
    size = width // heads
    slots = rem_send_ref.shape[0]
    me = at_ref[0]
    carried = []
    for u in range(users):
        ends = []
        for peer in range(peers):
            tail = payload_ref[peer, users * size :, :].astype(f32)
            ends.append(
                tail[u : u + 1, :]
                + tail[users + u : users + u + 1, :]
                + tail[2 * users + u : 2 * users + u + 1, :]
            )
        entering = jnp.zeros((size, width), f32)
        for peer in range(peers):
            part = payload_ref[peer, u * size : (u + 1) * size, :].astype(f32)
            linked = jnp.exp(ends[peer]) * entering + part
            entering = jnp.where(peer < me, linked, entering)
        leaving = jnp.zeros((size, width), f32)
        for peer in reversed(range(peers)):
            part = payload_ref[peer, u * size : (u + 1) * size, :].astype(f32)
            linked = jnp.exp(ends[peer]) * leaving + part
            leaving = jnp.where(peer > me, linked, leaving)
        carried.append((block_diagonal(entering, heads), block_diagonal(leaving, heads)))
    finish(copies)
    copies = []
    rem_terms, quot_terms = [], []
    for u in range(users):
        at = slice(u * block, (u + 1) * block)
        entering, leaving = carried[u]
        embedded = (quot_ref[at, :].astype(f32) * rem_ref[at, :].astype(f32)).astype(bf16)
        q = dot(embedded, wq_ref[...]).astype(bf16)
        k = dot(embedded, wk_ref[...]).astype(bf16)
        v = dot(embedded, wv_ref[...]).astype(bf16)
        dmixed = dmixed_ref[at, :]
        wide = wide_ref[at, :]
        finish(waits[u : u + 1])
        growth = scale * jnp.exp(wide)
        falloff = scale * jnp.exp(wide[block - 1 : block, :] - wide)
        mixed = (within_ref[0, at, :] + growth * dot(q, entering)).astype(bf16)
        out_ref[u] = dot(mixed, w_out_ref[...]).astype(bf16)
        copies += begin([(out_ref.at[u], out_hbm.at[u])], arrived, 6 + users + u)
        dq = (within_ref[1, at, :] + growth * dot(dmixed, entering, NT)).astype(bf16)
        dk = (within_ref[2, at, :] + falloff * dot(v, leaving, NT)).astype(bf16)
        dv = (within_ref[3, at, :] + falloff * dot(k, leaving)).astype(bf16)
        dembedded = dot(dq, wq_ref[...], NT) + dot(dk, wk_ref[...], NT) + dot(dv, wv_ref[...], NT)
        rem_terms.append((dembedded * quot_ref[at, :].astype(f32)).astype(bf16))
        quot_terms.append((dembedded * rem_ref[at, :].astype(f32)).astype(bf16))
    rem_terms = jnp.concatenate(rem_terms, axis=0)
    quot_terms = jnp.concatenate(quot_terms, axis=0)
    slot = jnp.concatenate([slot_ref[u : u + 1, :] for u in range(users)], axis=1)
    ids = jnp.concatenate([ids_ref[u : u + 1, :] for u in range(users)], axis=1)
    n = 6 + 2 * users
    for j, hot in enumerate(stacked_match(slot, block, slots // block)):
        at = slice(j * block, (j + 1) * block)
        rem_send_ref[at, :] = dot(hot, rem_terms).astype(bf16)
        copies += begin([(rem_send_ref.at[at, :], rem_send_hbm.at[at, :])], arrived, n + j)
    for ref, owner in ((give_ref, 1 - me % 2), (keep_ref, me % 2)):
        sum_half(ids, quot_terms, owner, ref)
    finish(copies)


def collect_kernel(at_ref, wanted_ref, back_ref, out_ref, *, per, other):
    shards, _, lanes = wanted_ref.shape
    slots = shards * per
    wanted = jnp.where(iota((shards, lanes), 1) < per, wanted_ref[:, 0, :], 0)
    high, low = halves(wanted)
    tile = where_bf16(remainder(iota((lanes, slots), 1), per) == iota((lanes, slots), 0), 1.0)
    own = quotient(iota((shards, slots), 1), per) == iota((shards, slots), 0)
    high = jnp.sum(jnp.where(own, dot(high.astype(bf16), tile), 0.0), axis=0, keepdims=True)
    low = jnp.sum(jnp.where(own, dot(low.astype(bf16), tile), 0.0), axis=0, keepdims=True)
    row = (16.0 * high + low).astype(i32) - 1
    core = at_ref[0] % 2
    sum_half(row, back_ref[...], 1 - core if other else core, out_ref)


def split_kernel(at_ref, keep_ref, got_ref, *out_refs):
    chips = len(out_refs)
    rows = out_refs[0].shape[0]
    bases = [
        pl.multiple_of(lax.rem(at_ref[0] // 2 + d, chips) * rows, rows) for d in range(chips)
    ]
    for base, out_ref in zip(bases, out_refs, strict=True):
        at = pl.ds(base, rows)
        out_ref[...] = (keep_ref[at, :].astype(f32) + got_ref[at, :].astype(f32)).astype(bf16)


def cut(chunk, shards):
    rows, width = chunk.shape
    lanes = width // 128
    part = rows * lanes // shards
    return [
        chunk[i // lanes * part : (i // lanes + 1) * part, i % lanes * 128 : (i % lanes + 1) * 128]
        for i in range(shards)
    ]


def total_kernel(*refs):
    total = sum((ref[...].astype(f32) for ref in refs[1:-1]), refs[0][...].astype(f32))
    for i, tile in enumerate(cut(total, refs[-1].shape[0])):
        refs[-1][i] = tile.astype(bf16)


def repeat_kernel(tiles_ref, out_ref):
    total = jnp.sum(tiles_ref[...].astype(f32), axis=0).astype(bf16)
    for i in range(out_ref.shape[0]):
        out_ref[i] = total


def place_kernel(at_ref, wanted_ref, *refs, chips, per, total, other):
    out_hbm, out_ref, arrived = refs[-3:]
    chunks = refs[:chips]
    copies = []
    _, rows, width = out_ref.shape
    shards, _, lanes = wanted_ref.shape
    counted = jnp.where(iota((shards, lanes), 1) == per, wanted_ref[:, 0, :], 0)
    ratio = total / jnp.sum(counted.astype(f32), axis=(0, 1), keepdims=True)
    chip, core = at_ref[0] // 2, at_ref[0] % 2
    half = core + other - 2 * core * other
    for d, chunk in enumerate(chunks):
        spot = half * chips + lax.rem(chip + chips - d, chips)
        base = pl.multiple_of(spot * rows, rows)
        if len(chunk.shape) == 2:
            out_ref[d] = ratio * chunk[...].astype(f32)
        else:
            part = chunk.shape[1]
            for i in range(shards):
                across = i % (width // 128) * 128
                down = i // (width // 128) * part
                tile = ratio * chunk[i].astype(f32)
                out_ref[d, down : down + part, across : across + 128] = tile
        copies += begin([(out_ref.at[d], out_hbm.at[pl.ds(base, rows), :])], arrived, d)
    finish(copies)


def exchange(array, axis):
    return lax.all_to_all(array, axis, split_axis=0, concat_axis=0, tiled=True)


def to_core(array):
    peers = lax.axis_size("hist")
    return lax.ppermute(array, "hist", [(i, i ^ 1) for i in range(peers)])


def to_chip(array, steps):
    peers = lax.axis_size("hist")
    return lax.ppermute(array, "hist", [(i, (i + 2 * steps) % peers) for i in range(peers)])


def split(at, keep, give, spec=VM):
    chips = lax.axis_size("hist") // 2
    outs = [((keep.shape[0] // chips, keep.shape[1]), bf16)] * chips
    return call(split_kernel, outs, (at, keep, to_core(give)), [SM, spec, VM])


def shared(chunks):
    return [chunks[0]] + [to_chip(chunks[d], d) for d in range(1, len(chunks))]


def along_chips(chunk):
    chips = lax.axis_size("hist") // 2
    return [chunk] + [to_chip(chunk, d) for d in range(1, chips)]


def place(at, wanted, chunks, rows, width, per, total, out=None):
    chips = len(chunks)
    scratch = [pltpu.VMEM((chips, rows // (2 * chips), width), f32), dma(chips)]
    other = 0 if out is None else 1
    kernel = functools.partial(place_kernel, chips=chips, per=per, total=total, other=other)
    args, specs, aliases = (at, wanted, *chunks), [SM] + [VM] * (1 + chips), {}
    if other:
        args, specs, aliases = args + (out,), specs + [HB], {len(args): 0}
    (out,) = call(kernel, [((rows, width), f32)], args, specs, scratch, [HB], aliases=aliases)
    return out


def body(
    quot_ids,
    rem_ids,
    lengths,
    log_decay,
    quot_table,
    rem_table,
    w_query,
    w_key,
    w_value,
    w_out,
    cotangent,
):
    users, block = quot_ids.shape
    rows_all, width = quot_table.shape
    heads = log_decay.shape[1]
    size = width // heads
    shards = lax.axis_size("user")
    peers = lax.axis_size("hist")
    rows_own = rem_table.shape[0]
    cap = 2 * block // shards
    per = users * cap
    slots = shards * per
    scale = 1.0 / math.sqrt(size * block * peers)
    at = lax.axis_index("hist").astype(i32).reshape(1)
    lanes = (per // 128 + 1) * 128

    square = pltpu.VMEM((width, width), bf16)
    requests, slot, table = call(
        functools.partial(request_kernel, rows_own=rows_own, cap=cap),
        [((shards, 1, lanes), i32), ((8, block), i32), (rem_table.shape, bf16)],
        (in_hbm(lengths), in_hbm(rem_ids), rem_table),
        [SM, VM, HB],
        [pltpu.VMEM((8, block), i32), dma(2)],
        [VM, HB, IN_VM],
        MOST,
    )
    wanted = exchange(requests, "user")
    quot_emb, dmixed, wide = call(
        quotient_kernel,
        [
            ((users * block, width), bf16),
            ((users * block, width), bf16),
            ((users * block, width), f32),
        ],
        (lengths, at)
        + tuple(in_hbm(a) for a in (quot_ids, quot_table, cotangent, log_decay, w_out)),
        [SM, SM] + [VM] * 5,
        (),
        [IN_VM] * 3,
        MOST,
    )
    (found,) = call(
        functools.partial(answer_kernel, per=per),
        [((slots, width), bf16)],
        (wanted, table),
        [VM, IN_VM],
        [pltpu.VMEM((slots, width), bf16), dma(4)],
        [HB],
        MOST,
    )
    answered = exchange(found.reshape(shards, per, width), "user").reshape(slots, width)
    rem_emb, payload = call(
        functools.partial(project_kernel, users=users, heads=heads),
        [((users * block, width), bf16), ((peers, users * size + 16, width), bf16)],
        (at, slot, answered, quot_emb, w_query, w_key, w_value, wide, dmixed),
        [SM, HB, VM, IN_VM, HB, HB, HB, IN_VM, IN_VM],
        [pltpu.VMEM((8, block), i32)]
        + [square] * 3
        + [pltpu.VMEM((2, users * size + 16, width), bf16), dma(4 + peers)],
        [IN_VM, HB],
        MOST,
    )
    states = exchange(payload, "hist")
    parts = (4, users * block, width)
    (within,) = call(
        functools.partial(within_kernel, scale=scale),
        [(parts, f32)],
        (quot_emb, rem_emb, dmixed)
        + tuple(in_hbm(a) for a in (log_decay, w_query, w_key, w_value)),
        [IN_VM] * 3 + [VM] * 4,
        [pltpu.VMEM(parts, f32), dma(users)],
        [HB],
        MOST,
    )
    output, rem_send, keep, give = call(
        functools.partial(gradient_kernel, scale=scale, heads=heads),
        [
            ((users, block, width), bf16),
            ((slots, width), bf16),
            ((rows_all // 2, width), f32),
            ((rows_all // 2, width), bf16),
        ],
        (at, states, within, dmixed, wide, rem_emb, quot_emb, slot, quot_ids)
        + (w_query, w_key, w_value, w_out),
        [SM, VM, HB] + [IN_VM] * 4 + [HB] * 6,
        [pltpu.VMEM(parts, f32)]
        + [pltpu.VMEM((8, block), i32), pltpu.VMEM((users, block), i32)]
        + [square] * 4
        + [pltpu.VMEM((users, block, width), bf16), pltpu.VMEM((slots, width), bf16)]
        + [dma(6 + 2 * users + slots // block)],
        [HB, HB, IN_VM, IN_VM],
        MOST,
    )
    rem_back = exchange(rem_send.reshape(shards, per, width), "user").reshape(slots, width)
    tiles = (shards, rows_all // peers * width // shards // 128, 128)
    (quot_tiles,) = call(total_kernel, [(tiles, bf16)], shared(split(at, keep, give, IN_VM)))
    rem_back, quot_tiles = lax.optimization_barrier((rem_back, quot_tiles))
    quot_back = exchange(quot_tiles, "user")
    keep, give = (
        call(
            functools.partial(collect_kernel, per=per, other=other),
            [((rows_own // 2, width), bf16 if other else f32)],
            (at, wanted, rem_back),
            [SM, VM, VM],
        )[0]
        for other in (False, True)
    )
    chunks = split(at, keep, give)
    (quot_tiles,) = call(repeat_kernel, [(tiles, bf16)], (quot_back,))
    quot_tiles, *_ = lax.optimization_barrier((quot_tiles, *chunks))
    quot_tiles = exchange(quot_tiles, "user")
    rem_sum = sum(c.astype(f32) for c in shared(chunks)).astype(bf16)
    rem_mine = along_chips(rem_sum)
    quot_tiles, _ = lax.optimization_barrier((quot_tiles, rem_sum))
    total = float(users * shards * block * peers)
    rem_grad = place(at, wanted, rem_mine, rows_own, width, per, total)
    quot_mine = along_chips(quot_tiles)
    rem_theirs = [to_core(c) for c in rem_mine]
    *quot_mine, rem_grad = lax.optimization_barrier((*quot_mine, rem_grad))
    rem_grad = place(at, wanted, rem_theirs, rows_own, width, per, total, rem_grad)
    quot_theirs = [to_core(c) for c in quot_mine]
    quot_grad = place(at, wanted, quot_mine, rows_all, width, per, total)
    quot_grad = place(at, wanted, quot_theirs, rows_all, width, per, total, quot_grad)
    return (output, quot_grad, rem_grad)


def solution(mesh):
    return jax.shard_map(
        body,
        mesh=mesh,
        in_specs=(
            P("user", "hist"),
            P("user", "hist"),
            P("user"),
            P("user", None, "hist"),
            P(),
            P("user", None),
            P(),
            P(),
            P(),
            P(),
            P("user", "hist", None),
        ),
        out_specs=(P("user", "hist", None), P(), P("user", None)),
        check_vma=False,
    )
```

```python
import functools
import math

import jax
import jax.numpy as jnp
from jax import lax
from jax.experimental import pallas as pl
from jax.experimental.pallas import tpu as pltpu
from jax.sharding import PartitionSpec as P

f32 = jnp.float32
bf16 = jnp.bfloat16
i32 = jnp.int32
FULL = 62
MOST = 24
EXACT = lax.Precision.HIGHEST
VM = pl.BlockSpec(memory_space=pltpu.VMEM)
SM = pl.BlockSpec(memory_space=pltpu.SMEM)
HB = pl.BlockSpec(memory_space=pltpu.HBM)
IN_VM = pl.BlockSpec(memory_space=pltpu.VMEM)

NN = (((1,), (0,)), ((), ()))
NT = (((1,), (1,)), ((), ()))
TN = (((0,), (0,)), ((), ()))


def dot(a, b, dims=NN, precision=None):
    return lax.dot_general(a, b, dims, preferred_element_type=f32, precision=precision)


def iota(shape, dim):
    return lax.broadcasted_iota(i32, shape, dim)


def quotient(a, n):
    return a >> (n.bit_length() - 1) if n & (n - 1) == 0 else a // n


def remainder(a, n):
    return a & (n - 1) if n & (n - 1) == 0 else a % n


def where_bf16(mask, a):
    return jnp.where(mask, a, 0.0).astype(bf16)


def halves(whole):
    return (whole >> 4).astype(f32), (whole & 15).astype(f32)


def spread_column(row):
    n = row.shape[1]
    diagonal = iota((n, n), 0) == iota((n, n), 1)
    high, low = halves(row)
    ones = jnp.ones((n, 128), bf16)
    column = 16.0 * dot(where_bf16(diagonal, high), ones) + dot(where_bf16(diagonal, low), ones)
    return column.astype(i32)


def tiled_match(column, width):
    near = where_bf16(iota(column.shape, 1) == (column & 127), 1.0)
    tile = (column >> 7).astype(f32).astype(bf16)
    zero = jnp.zeros_like(near)
    parts = [jnp.where(tile == jnp.asarray(j, bf16), near, zero) for j in range(width // 128)]
    return jnp.concatenate(parts, axis=1)


def stacked_match(row, chunk, count):
    row = jnp.broadcast_to(row, (chunk, row.shape[1]))
    near = where_bf16(iota(row.shape, 0) == (row & (chunk - 1)), 1.0)
    part = (row >> (chunk.bit_length() - 1)).astype(f32).astype(bf16)
    zero = jnp.zeros_like(near)
    return [jnp.where(part == jnp.asarray(j, bf16), near, zero) for j in range(count)]


def begin(pairs, arrived, at=0):
    copies = [
        pltpu.make_async_copy(source, target, arrived.at[at + i])
        for i, (source, target) in enumerate(pairs)
    ]
    for copy in copies:
        copy.start()
    return copies


def finish(copies):
    for copy in copies:
        copy.wait()


def dma(n):
    return pltpu.SemaphoreType.DMA((n,))


def held(spec):
    return pltpu.HBM if spec is HB else pltpu.VMEM if spec is IN_VM else None


def in_hbm(array):
    return pltpu.with_memory_space_constraint(array, pltpu.HBM)


def call(kernel, outs, args, specs=None, scratch=(), out_specs=None, limit=16, aliases={}):
    out_specs = out_specs if out_specs is not None else [VM] * len(outs)
    shapes = [
        held(spec)(s, d) if held(spec) else jax.ShapeDtypeStruct(s, d)
        for (s, d), spec in zip(outs, out_specs, strict=True)
    ]
    specs = specs if specs is not None else [VM] * len(args)
    args = [
        pltpu.with_memory_space_constraint(a, held(spec)) if held(spec) else a
        for a, spec in zip(args, specs, strict=True)
    ]
    return pl.pallas_call(
        kernel,
        out_shape=tuple(shapes),
        in_specs=specs,
        out_specs=tuple(out_specs),
        input_output_aliases=aliases,
        scratch_shapes=list(scratch),
        compiler_params=pltpu.CompilerParams(vmem_limit_bytes=limit * 1024 * 1024),
    )(*args)


def request_kernel(
    len_ref, ids_hbm, table_hbm, out_ref, slot_ref, table_ref, ids_ref, arrived, *, rows_own, cap
):
    copies = begin(((ids_hbm, ids_ref), (table_hbm, table_ref)), arrived)
    users, block = ids_ref.shape
    shards, _, lanes = out_ref.shape
    shift = rows_own.bit_length() - 1
    earlier = where_bf16(iota((block, block), 0) < iota((block, block), 1), 1.0)
    place = iota((lanes, block), 0)
    finish(copies[:1])
    total = jnp.zeros((shards, lanes), f32)
    count = jnp.int32(0)
    slot_ref[...] = jnp.zeros_like(slot_ref)
    for u in range(users):
        ids = ids_ref[u : u + 1, :]
        owner = ids >> shift
        named = iota((shards, block), 0) == owner
        named_16 = where_bf16(named, 1.0)
        before = dot(named_16, earlier)
        rank = jnp.sum(jnp.where(named, before, 0.0), axis=0, keepdims=True).astype(i32)
        high, low = halves((ids & (rows_own - 1)) + 1)
        chosen = place == rank + u * cap
        total = total + 16.0 * dot(named_16, where_bf16(chosen, high), NT)
        total = total + dot(named_16, where_bf16(chosen, low), NT)
        slot_ref[u : u + 1, :] = (owner * users + u) * cap + rank
        count = count + len_ref[u]
    wanted = jnp.where(iota((shards, lanes), 1) == users * cap, count, total.astype(i32))
    out_ref[:, 0, :] = wanted
    finish(copies[1:])


def answer_kernel(
    wanted_ref, table_ref, out_hbm, out_ref, arrived, *, per
):
    shards, _, lanes = wanted_ref.shape
    parts = 4
    group = shards // parts
    slots = group * per
    rows = table_ref.shape[0]
    repeat = where_bf16(quotient(iota((slots, group), 0), per) == iota((slots, group), 1), 1.0)
    own = remainder(iota((slots, lanes), 0), per) == iota((slots, lanes), 1)
    ones = jnp.ones((lanes, 128), bf16)
    wanted = jnp.where(iota((shards, lanes), 1) < per, wanted_ref[:, 0, :], 0)
    stores = []
    for j in range(parts):
        high, low = halves(wanted[j * group : (j + 1) * group, :])
        high = dot(where_bf16(own, dot(repeat, high.astype(bf16))), ones)
        low = dot(where_bf16(own, dot(repeat, low.astype(bf16))), ones)
        column = (16.0 * high + low).astype(i32) - 1
        hot = tiled_match(column, rows)
        at = slice(j * slots, (j + 1) * slots)
        out_ref[at, :] = dot(hot, table_ref[...]).astype(bf16)
        stores += begin([(out_ref.at[at, :], out_hbm.at[at, :])], arrived, j)
    finish(stores)


def quotient_kernel(
    len_ref,
    at_ref,
    ids_ref,
    table_ref,
    cot_ref,
    decay_ref,
    w_out_ref,
    quot_ref,
    dmixed_ref,
    wide_ref,
):
    users, block = ids_ref.shape
    heads = decay_ref.shape[1]
    rows, width = table_ref.shape
    for u in range(users):
        at = slice(u * block, (u + 1) * block)
        hot = tiled_match(spread_column(ids_ref[u : u + 1, :]), rows)
        quot_ref[at, :] = dot(hot, table_ref[...]).astype(bf16)
        valid = at_ref[0] * block + iota((block, width), 0) < len_ref[u]
        masked = jnp.where(valid, cot_ref[u].astype(f32), 0.0).astype(bf16)
        dmixed_ref[at, :] = dot(masked, w_out_ref[...], NT).astype(bf16)
        _, columns = decays(decay_ref[u], width)
        wide_ref[at, :] = over_heads(columns, heads, width)


def decays(log_decay, width):
    heads, block = log_decay.shape
    upper = jnp.where(iota((block, block), 0) <= iota((block, block), 1), 1.0, 0.0)
    lower = jnp.where(iota((block, block), 0) >= iota((block, block), 1), 1.0, 0.0)
    padded = jnp.concatenate([log_decay, jnp.zeros((8 - heads, block), f32)], axis=0)
    rows = dot(padded, upper, precision=EXACT)
    columns = dot(lower, padded, NT, precision=EXACT)
    return rows, columns


def over_heads(columns, heads, width):
    n = columns.shape[0]
    head_of = quotient(iota((n, width), 1), width // heads)
    wide = jnp.broadcast_to(columns[:, 0:1], (n, width))
    for h in range(1, heads):
        wide = jnp.where(head_of == h, jnp.broadcast_to(columns[:, h : h + 1], (n, width)), wide)
    return wide


def diagonal_heads(square, heads):
    width = square.shape[1]
    size = width // heads
    head_of = quotient(iota((size, width), 1), size)
    out = square[0:size, :]
    for h in range(1, heads):
        out = jnp.where(head_of == h, square[h * size : (h + 1) * size, :], out)
    return out


def block_diagonal(state, heads):
    size, width = state.shape
    head_of = quotient(iota((size, width), 1), width // heads)
    return jnp.concatenate([where_bf16(head_of == h, state) for h in range(heads)], axis=0)


def project_kernel(
    at_ref,
    slot_ref,
    answered_ref,
    quot_ref,
    wq_hbm,
    wk_hbm,
    wv_hbm,
    wide_ref,
    dmixed_ref,
    rem_ref,
    payload_hbm,
    wq_ref,
    wk_ref,
    wv_ref,
    states_ref,
    arrived,
    *,
    users,
    heads,
):
    slots, width = answered_ref.shape
    block = quot_ref.shape[0] // users
    peers = payload_hbm.shape[0]
    size = width // heads
    me = at_ref[0]
    ends = []
    copies = begin(
        (
            (wq_hbm, wq_ref),
            (wk_hbm, wk_ref),
            (wv_hbm, wv_ref),
        ),
        arrived,
    )
    hot = [tiled_match(spread_column(slot_ref[u : u + 1, :]), slots) for u in range(users)]
    for u in range(users):
        at = slice(u * block, (u + 1) * block)
        rem_ref[at, :] = dot(hot[u], answered_ref[...]).astype(bf16)
    finish(copies)
    for u in range(users):
        at = slice(u * block, (u + 1) * block)
        embedded = (quot_ref[at, :].astype(f32) * rem_ref[at, :].astype(f32)).astype(bf16)
        q = dot(embedded, wq_ref[...]).astype(bf16)
        k = dot(embedded, wk_ref[...]).astype(bf16)
        v = dot(embedded, wv_ref[...]).astype(bf16)
        wide = wide_ref[at, :]
        end = wide[block - 1 : block, :]
        ends.append(end)
        falling = (k.astype(f32) * jnp.exp(end - wide)).astype(bf16)
        growing = (q.astype(f32) * jnp.exp(wide)).astype(bf16)
        state = diagonal_heads(dot(falling, v, TN), heads).astype(bf16)
        grad = diagonal_heads(dot(growing, dmixed_ref[at, :], TN), heads).astype(bf16)
        states_ref[0, u * size : (u + 1) * size, :] = state
        states_ref[1, u * size : (u + 1) * size, :] = grad
    rows = iota((16, width), 0)
    tail = jnp.zeros((16, width), f32)
    for u in range(users):
        left = ends[u]
        for part in range(3):
            piece = left.astype(bf16).astype(f32)
            left = left - piece
            tail = jnp.where(rows == part * users + u, piece, tail)
    tail = tail.astype(bf16)
    states_ref[0, users * size :, :] = tail
    states_ref[1, users * size :, :] = tail
    which = [jnp.where(peer > me, 0, 1) for peer in range(peers)]
    pairs = [(states_ref.at[which[peer]], payload_hbm.at[peer]) for peer in range(peers)]
    finish(begin(pairs, arrived, 3))


def within_kernel(
    quot_ref,
    rem_ref,
    dmixed_ref,
    decay_ref,
    wq_ref,
    wk_ref,
    wv_ref,
    near_ref,
    far_hbm,
    far_ref,
    arrived,
    *,
    scale,
):
    users, heads, block = decay_ref.shape
    width = quot_ref.shape[1]
    copies = []
    head_of = quotient(iota((block, width), 1), width // heads)
    lower_tri = iota((block, block), 0) >= iota((block, block), 1)
    for u in range(users):
        at = slice(u * block, (u + 1) * block)
        embedded = (quot_ref[at, :].astype(f32) * rem_ref[at, :].astype(f32)).astype(bf16)
        q = dot(embedded, wq_ref[...]).astype(bf16)
        k = dot(embedded, wk_ref[...]).astype(bf16)
        v = dot(embedded, wv_ref[...]).astype(bf16)
        dmixed = dmixed_ref[at, :]
        rows, columns = decays(decay_ref[u], width)
        mixed = jnp.zeros((block, width), f32)
        dq = jnp.zeros((block, width), f32)
        dk = jnp.zeros((block, width), f32)
        dv = jnp.zeros((block, width), f32)
        zero = jnp.zeros((), bf16)
        for h in range(heads):
            own = head_of == h
            q_h = jnp.where(own, q, zero)
            k_h = jnp.where(own, k, zero)
            v_h = jnp.where(own, v, zero)
            d_h = jnp.where(own, dmixed, zero)
            gap = columns[:, h : h + 1] - rows[h : h + 1, :]
            mask = jnp.where(lower_tri, scale * jnp.exp(jnp.minimum(gap, 0.0)), 0.0)
            weights = (dot(q_h, k, NT) * mask).astype(bf16)
            dweights = (dot(d_h, v, NT) * mask).astype(bf16)
            mixed = mixed + dot(weights, v_h)
            dq = dq + dot(dweights, k_h)
            dk = dk + dot(dweights, q_h, TN)
            dv = dv + dot(weights, d_h, TN)
        near_ref[at, :] = mixed
        for i, part in enumerate((dq, dk, dv)):
            far_ref[i, at, :] = part
        copies += begin([(far_ref.at[:, at, :], far_hbm.at[:, at, :])], arrived, u)
    finish(copies)


def sum_half(ids, terms, owner, out_ref):
    half = out_ref.shape[0]
    chunk = min(256, half)
    for j, hot in enumerate(stacked_match(ids - owner * half, chunk, half // chunk)):
        out_ref[j * chunk : (j + 1) * chunk, :] = dot(hot, terms).astype(out_ref.dtype)


def gradient_kernel(
    at_ref,
    payload_ref,
    near_ref,
    far_hbm,
    dmixed_ref,
    wide_ref,
    rem_ref,
    quot_ref,
    slot_ref,
    ids_hbm,
    wq_hbm,
    wk_hbm,
    wv_hbm,
    w_out_hbm,
    out_hbm,
    rem_send_hbm,
    keep_ref,
    give_ref,
    far_ref,
    ids_ref,
    wq_ref,
    wk_ref,
    wv_ref,
    w_out_ref,
    out_ref,
    rem_send_ref,
    arrived,
    *,
    scale,
    heads,
):
    users, block = ids_ref.shape
    width = quot_ref.shape[1]
    copies = begin(
        (
            (wq_hbm, wq_ref),
            (wk_hbm, wk_ref),
            (wv_hbm, wv_ref),
            (w_out_hbm, w_out_ref),
            (ids_hbm, ids_ref),
        ),
        arrived,
    )
    waits = []
    for u in range(users):
        at = slice(u * block, (u + 1) * block)
        waits += begin([(far_hbm.at[:, at, :], far_ref.at[:, at, :])], arrived, 5 + u)
    peers = payload_ref.shape[0]
    size = width // heads
    slots = rem_send_ref.shape[0]
    me = at_ref[0]
    carried = []
    for u in range(users):
        ends = []
        for peer in range(peers):
            tail = payload_ref[peer, users * size :, :].astype(f32)
            ends.append(
                tail[u : u + 1, :]
                + tail[users + u : users + u + 1, :]
                + tail[2 * users + u : 2 * users + u + 1, :]
            )
        entering = jnp.zeros((size, width), f32)
        for peer in range(peers):
            part = payload_ref[peer, u * size : (u + 1) * size, :].astype(f32)
            linked = jnp.exp(ends[peer]) * entering + part
            entering = jnp.where(peer < me, linked, entering)
        leaving = jnp.zeros((size, width), f32)
        for peer in reversed(range(peers)):
            part = payload_ref[peer, u * size : (u + 1) * size, :].astype(f32)
            linked = jnp.exp(ends[peer]) * leaving + part
            leaving = jnp.where(peer > me, linked, leaving)
        carried.append((block_diagonal(entering, heads), block_diagonal(leaving, heads)))
    finish(copies)
    copies = []
    rem_terms, quot_terms = [], []
    for u in range(users):
        at = slice(u * block, (u + 1) * block)
        entering, leaving = carried[u]
        embedded = (quot_ref[at, :].astype(f32) * rem_ref[at, :].astype(f32)).astype(bf16)
        q = dot(embedded, wq_ref[...]).astype(bf16)
        k = dot(embedded, wk_ref[...]).astype(bf16)
        v = dot(embedded, wv_ref[...]).astype(bf16)
        dmixed = dmixed_ref[at, :]
        wide = wide_ref[at, :]
        growth = scale * jnp.exp(wide)
        falloff = scale * jnp.exp(wide[block - 1 : block, :] - wide)
        mixed = (near_ref[at, :] + growth * dot(q, entering)).astype(bf16)
        out_ref[u] = dot(mixed, w_out_ref[...]).astype(bf16)
        copies += begin([(out_ref.at[u], out_hbm.at[u])], arrived, 5 + users + u)
        finish(waits[u : u + 1])
        dq = (far_ref[0, at, :] + growth * dot(dmixed, entering, NT)).astype(bf16)
        dk = (far_ref[1, at, :] + falloff * dot(v, leaving, NT)).astype(bf16)
        dv = (far_ref[2, at, :] + falloff * dot(k, leaving)).astype(bf16)
        dembedded = dot(dq, wq_ref[...], NT) + dot(dk, wk_ref[...], NT) + dot(dv, wv_ref[...], NT)
        rem_terms.append((dembedded * quot_ref[at, :].astype(f32)).astype(bf16))
        quot_terms.append((dembedded * rem_ref[at, :].astype(f32)).astype(bf16))
    rem_terms = jnp.concatenate(rem_terms, axis=0)
    quot_terms = jnp.concatenate(quot_terms, axis=0)
    slot = jnp.concatenate([slot_ref[u : u + 1, :] for u in range(users)], axis=1)
    ids = jnp.concatenate([ids_ref[u : u + 1, :] for u in range(users)], axis=1)
    n = 5 + 2 * users
    for j, hot in enumerate(stacked_match(slot, block, slots // block)):
        at = slice(j * block, (j + 1) * block)
        rem_send_ref[at, :] = dot(hot, rem_terms).astype(bf16)
        copies += begin([(rem_send_ref.at[at, :], rem_send_hbm.at[at, :])], arrived, n + j)
    for ref, owner in ((give_ref, 1 - me % 2), (keep_ref, me % 2)):
        sum_half(ids, quot_terms, owner, ref)
    finish(copies)


def collect_kernel(at_ref, wanted_ref, back_ref, out_ref, *, per, other):
    shards, _, lanes = wanted_ref.shape
    slots = shards * per
    wanted = jnp.where(iota((shards, lanes), 1) < per, wanted_ref[:, 0, :], 0)
    high, low = halves(wanted)
    tile = where_bf16(remainder(iota((lanes, slots), 1), per) == iota((lanes, slots), 0), 1.0)
    own = quotient(iota((shards, slots), 1), per) == iota((shards, slots), 0)
    high = jnp.sum(jnp.where(own, dot(high.astype(bf16), tile), 0.0), axis=0, keepdims=True)
    low = jnp.sum(jnp.where(own, dot(low.astype(bf16), tile), 0.0), axis=0, keepdims=True)
    row = (16.0 * high + low).astype(i32) - 1
    core = at_ref[0] % 2
    sum_half(row, back_ref[...], 1 - core if other else core, out_ref)


def split_kernel(at_ref, keep_ref, got_ref, *out_refs):
    chips = len(out_refs)
    rows = out_refs[0].shape[0]
    bases = [
        pl.multiple_of(lax.rem(at_ref[0] // 2 + d, chips) * rows, rows) for d in range(chips)
    ]
    for base, out_ref in zip(bases, out_refs, strict=True):
        at = pl.ds(base, rows)
        out_ref[...] = (keep_ref[at, :].astype(f32) + got_ref[at, :].astype(f32)).astype(bf16)


def cut(chunk, shards):
    rows, width = chunk.shape
    lanes = width // 128
    part = rows * lanes // shards
    return [
        chunk[i // lanes * part : (i // lanes + 1) * part, i % lanes * 128 : (i % lanes + 1) * 128]
        for i in range(shards)
    ]


def total_kernel(*refs):
    total = sum((ref[...].astype(f32) for ref in refs[1:-1]), refs[0][...].astype(f32))
    for i, tile in enumerate(cut(total, refs[-1].shape[0])):
        refs[-1][i] = tile.astype(bf16)


def repeat_kernel(tiles_ref, out_ref):
    total = jnp.sum(tiles_ref[...].astype(f32), axis=0).astype(bf16)
    for i in range(out_ref.shape[0]):
        out_ref[i] = total


def place_kernel(at_ref, wanted_ref, *refs, jobs, chips, per, total):
    outs = refs[-2 * len(jobs) - 1 : -len(jobs) - 1]
    staged = refs[-len(jobs) - 1 : -1]
    arrived = refs[-1]
    copies = []
    shards, _, lanes = wanted_ref.shape
    counted = jnp.where(iota((shards, lanes), 1) == per, wanted_ref[:, 0, :], 0)
    ratio = total / jnp.sum(counted.astype(f32), axis=(0, 1), keepdims=True)
    chip, core = at_ref[0] // 2, at_ref[0] % 2
    for n, other in enumerate(jobs):
        out_hbm, out_ref = outs[n], staged[n]
        _, rows, width = out_ref.shape
        half = core + other - 2 * core * other
        for d in range(chips):
            chunk = refs[n * chips + d]
            spot = half * chips + lax.rem(chip + chips - d, chips)
            base = pl.multiple_of(spot * rows, rows)
            if len(chunk.shape) == 2:
                out_ref[d] = ratio * chunk[...].astype(f32)
            else:
                part = chunk.shape[1]
                for i in range(shards):
                    across = i % (width // 128) * 128
                    down = i // (width // 128) * part
                    tile = ratio * chunk[i].astype(f32)
                    out_ref[d, down : down + part, across : across + 128] = tile
            pair = (out_ref.at[d], out_hbm.at[pl.ds(base, rows), :])
            copies += begin([pair], arrived, n * chips + d)
    finish(copies)


def exchange(array, axis):
    return lax.all_to_all(array, axis, split_axis=0, concat_axis=0, tiled=True)


def to_core(array):
    peers = lax.axis_size("hist")
    return lax.ppermute(array, "hist", [(i, i ^ 1) for i in range(peers)])


def to_chip(array, steps):
    peers = lax.axis_size("hist")
    return lax.ppermute(array, "hist", [(i, (i + 2 * steps) % peers) for i in range(peers)])


def split(at, keep, give, spec=VM):
    chips = lax.axis_size("hist") // 2
    outs = [((keep.shape[0] // chips, keep.shape[1]), bf16)] * chips
    return call(split_kernel, outs, (at, keep, to_core(give)), [SM, spec, VM])


def shared(chunks):
    return [chunks[0]] + [to_chip(chunks[d], d) for d in range(1, len(chunks))]


def along_chips(chunk):
    chips = lax.axis_size("hist") // 2
    return [chunk] + [to_chip(chunk, d) for d in range(1, chips)]


def place(at, wanted, jobs, width, per, total):
    chips = len(jobs[0][0])
    args, specs, outs, scratch, others, aliases = (at, wanted), [SM, VM], [], [], [], {}
    for chunks, rows, out in jobs:
        args, specs = args + tuple(chunks), specs + [VM] * chips
        outs.append(((rows, width), f32))
        scratch.append(pltpu.VMEM((chips, rows // (2 * chips), width), f32))
        others.append(0 if out is None else 1)
    for n, (_, _, out) in enumerate(jobs):
        if out is not None:
            aliases[len(args)] = n
            args, specs = args + (out,), specs + [HB]
    kernel = functools.partial(
        place_kernel, jobs=tuple(others), chips=chips, per=per, total=total
    )
    scratch.append(dma(chips * len(jobs)))
    return call(kernel, outs, args, specs, scratch, [HB] * len(jobs), aliases=aliases)


def body(
    quot_ids,
    rem_ids,
    lengths,
    log_decay,
    quot_table,
    rem_table,
    w_query,
    w_key,
    w_value,
    w_out,
    cotangent,
):
    users, block = quot_ids.shape
    rows_all, width = quot_table.shape
    heads = log_decay.shape[1]
    size = width // heads
    shards = lax.axis_size("user")
    peers = lax.axis_size("hist")
    rows_own = rem_table.shape[0]
    cap = 2 * block // shards
    per = users * cap
    slots = shards * per
    scale = 1.0 / math.sqrt(size * block * peers)
    at = lax.axis_index("hist").astype(i32).reshape(1)
    lanes = (per // 128 + 1) * 128

    square = pltpu.VMEM((width, width), bf16)
    requests, slot, table = call(
        functools.partial(request_kernel, rows_own=rows_own, cap=cap),
        [((shards, 1, lanes), i32), ((8, block), i32), (rem_table.shape, bf16)],
        (in_hbm(lengths), rem_ids, rem_table),
        [SM, HB, HB],
        [pltpu.VMEM((users, block), i32), dma(2)],
        [VM, IN_VM, IN_VM],
        MOST,
    )
    wanted = exchange(requests, "user")
    quot_emb, dmixed, wide = call(
        quotient_kernel,
        [
            ((users * block, width), bf16),
            ((users * block, width), bf16),
            ((users * block, width), f32),
        ],
        (lengths, at)
        + tuple(in_hbm(a) for a in (quot_ids, quot_table, cotangent, log_decay, w_out)),
        [SM, SM] + [VM] * 5,
        (),
        [IN_VM] * 3,
        MOST,
    )
    (found,) = call(
        functools.partial(answer_kernel, per=per),
        [((slots, width), bf16)],
        (wanted, table),
        [VM, IN_VM],
        [pltpu.VMEM((slots, width), bf16), dma(4)],
        [HB],
        MOST,
    )
    answered = exchange(found.reshape(shards, per, width), "user").reshape(slots, width)
    rem_emb, payload = call(
        functools.partial(project_kernel, users=users, heads=heads),
        [((users * block, width), bf16), ((peers, users * size + 16, width), bf16)],
        (at, slot, answered, quot_emb, w_query, w_key, w_value, wide, dmixed),
        [SM, IN_VM, VM, IN_VM, HB, HB, HB, IN_VM, IN_VM],
        [square] * 3 + [pltpu.VMEM((2, users * size + 16, width), bf16), dma(3 + peers)],
        [IN_VM, HB],
        MOST,
    )
    states = exchange(payload, "hist")
    parts = (3, users * block, width)
    near, far = call(
        functools.partial(within_kernel, scale=scale),
        [(parts[1:], f32), (parts, f32)],
        (quot_emb, rem_emb, dmixed)
        + tuple(in_hbm(a) for a in (log_decay, w_query, w_key, w_value)),
        [IN_VM] * 3 + [VM] * 4,
        [pltpu.VMEM(parts, f32), dma(users)],
        [IN_VM, HB],
        MOST,
    )
    output, rem_send, keep, give = call(
        functools.partial(gradient_kernel, scale=scale, heads=heads),
        [
            ((users, block, width), bf16),
            ((slots, width), bf16),
            ((rows_all // 2, width), bf16),
            ((rows_all // 2, width), bf16),
        ],
        (at, states, near, far, dmixed, wide, rem_emb, quot_emb, slot, quot_ids)
        + (w_query, w_key, w_value, w_out),
        [SM, VM, IN_VM, HB] + [IN_VM] * 5 + [HB] * 5,
        [pltpu.VMEM(parts, f32), pltpu.VMEM((users, block), i32)]
        + [square] * 4
        + [pltpu.VMEM((users, block, width), bf16), pltpu.VMEM((slots, width), bf16)]
        + [dma(5 + 2 * users + slots // block)],
        [HB, HB, IN_VM, IN_VM],
        MOST,
    )
    rem_back = exchange(rem_send.reshape(shards, per, width), "user").reshape(slots, width)
    tiles = (shards, rows_all // peers * width // shards // 128, 128)
    (quot_tiles,) = call(total_kernel, [(tiles, bf16)], shared(split(at, keep, give, IN_VM)))
    rem_back, quot_tiles = lax.optimization_barrier((rem_back, quot_tiles))
    quot_back = exchange(quot_tiles, "user")
    keep, give = (
        call(
            functools.partial(collect_kernel, per=per, other=other),
            [((rows_own // 2, width), bf16 if other else f32)],
            (at, wanted, rem_back),
            [SM, VM, VM],
        )[0]
        for other in (False, True)
    )
    chunks = split(at, keep, give)
    (quot_tiles,) = call(repeat_kernel, [(tiles, bf16)], (quot_back,))
    quot_tiles, *_ = lax.optimization_barrier((quot_tiles, *chunks))
    quot_tiles = exchange(quot_tiles, "user")
    rem_sum = sum(c.astype(f32) for c in shared(chunks)).astype(bf16)
    rem_mine = along_chips(rem_sum)
    quot_tiles, _ = lax.optimization_barrier((quot_tiles, rem_sum))
    total = float(users * shards * block * peers)
    (rem_grad,) = place(at, wanted, [(rem_mine, rows_own, None)], width, per, total)
    quot_mine = along_chips(quot_tiles)
    rem_theirs = [to_core(c) for c in rem_mine]
    *quot_mine, rem_grad = lax.optimization_barrier((*quot_mine, rem_grad))
    quot_theirs = [to_core(c) for c in quot_mine]
    jobs = [(quot_mine, rows_all, None), (rem_theirs, rows_own, rem_grad)]
    quot_grad, rem_grad = place(at, wanted, jobs, width, per, total)
    (quot_grad,) = place(at, wanted, [(quot_theirs, rows_all, quot_grad)], width, per, total)
    return (output, quot_grad, rem_grad)


def solution(mesh):
    return jax.shard_map(
        body,
        mesh=mesh,
        in_specs=(
            P("user", "hist"),
            P("user", "hist"),
            P("user"),
            P("user", None, "hist"),
            P(),
            P("user", None),
            P(),
            P(),
            P(),
            P(),
            P("user", "hist", None),
        ),
        out_specs=(P("user", "hist", None), P(), P("user", None)),
        check_vma=False,
    )
```

```python
import functools
import math

import jax
import jax.numpy as jnp
from jax import lax
from jax.experimental import pallas as pl
from jax.experimental.pallas import tpu as pltpu
from jax.sharding import PartitionSpec as P

f32 = jnp.float32
bf16 = jnp.bfloat16
i32 = jnp.int32
FULL = 62
MOST = 24
EXACT = lax.Precision.HIGHEST
VM = pl.BlockSpec(memory_space=pltpu.VMEM)
SM = pl.BlockSpec(memory_space=pltpu.SMEM)
HB = pl.BlockSpec(memory_space=pltpu.HBM)
IN_VM = pl.BlockSpec(memory_space=pltpu.VMEM)

NN = (((1,), (0,)), ((), ()))
NT = (((1,), (1,)), ((), ()))
TN = (((0,), (0,)), ((), ()))


def dot(a, b, dims=NN, precision=None):
    return lax.dot_general(a, b, dims, preferred_element_type=f32, precision=precision)


def iota(shape, dim):
    return lax.broadcasted_iota(i32, shape, dim)


def quotient(a, n):
    return a >> (n.bit_length() - 1) if n & (n - 1) == 0 else a // n


def remainder(a, n):
    return a & (n - 1) if n & (n - 1) == 0 else a % n


def where_bf16(mask, a):
    return jnp.where(mask, a, 0.0).astype(bf16)


def halves(whole):
    return (whole >> 4).astype(f32), (whole & 15).astype(f32)


def spread_column(row):
    n = row.shape[1]
    diagonal = iota((n, n), 0) == iota((n, n), 1)
    high, low = halves(row)
    ones = jnp.ones((n, 128), bf16)
    column = 16.0 * dot(where_bf16(diagonal, high), ones) + dot(where_bf16(diagonal, low), ones)
    return column.astype(i32)


def tiled_match(column, width):
    near = where_bf16(iota(column.shape, 1) == (column & 127), 1.0)
    tile = (column >> 7).astype(f32).astype(bf16)
    zero = jnp.zeros_like(near)
    parts = [jnp.where(tile == jnp.asarray(j, bf16), near, zero) for j in range(width // 128)]
    return jnp.concatenate(parts, axis=1)


def stacked_match(row, chunk, count):
    row = jnp.broadcast_to(row, (chunk, row.shape[1]))
    near = where_bf16(iota(row.shape, 0) == (row & (chunk - 1)), 1.0)
    part = (row >> (chunk.bit_length() - 1)).astype(f32).astype(bf16)
    zero = jnp.zeros_like(near)
    return [jnp.where(part == jnp.asarray(j, bf16), near, zero) for j in range(count)]


def begin(pairs, arrived, at=0):
    copies = [
        pltpu.make_async_copy(source, target, arrived.at[at + i])
        for i, (source, target) in enumerate(pairs)
    ]
    for copy in copies:
        copy.start()
    return copies


def finish(copies):
    for copy in copies:
        copy.wait()


def dma(n):
    return pltpu.SemaphoreType.DMA((n,))


def held(spec):
    return pltpu.HBM if spec is HB else pltpu.VMEM if spec is IN_VM else None


def in_hbm(array):
    return pltpu.with_memory_space_constraint(array, pltpu.HBM)


def call(kernel, outs, args, specs=None, scratch=(), out_specs=None, limit=16, aliases={}):
    out_specs = out_specs if out_specs is not None else [VM] * len(outs)
    shapes = [
        held(spec)(s, d) if held(spec) else jax.ShapeDtypeStruct(s, d)
        for (s, d), spec in zip(outs, out_specs, strict=True)
    ]
    specs = specs if specs is not None else [VM] * len(args)
    args = [
        pltpu.with_memory_space_constraint(a, held(spec)) if held(spec) else a
        for a, spec in zip(args, specs, strict=True)
    ]
    return pl.pallas_call(
        kernel,
        out_shape=tuple(shapes),
        in_specs=specs,
        out_specs=tuple(out_specs),
        input_output_aliases=aliases,
        scratch_shapes=list(scratch),
        compiler_params=pltpu.CompilerParams(vmem_limit_bytes=limit * 1024 * 1024),
    )(*args)


def request_kernel(
    len_hbm, ids_hbm, table_hbm, out_ref, slot_ref, table_ref, len_ref, ids_ref, arrived,
    *, rows_own, cap,
):
    copies = begin(((ids_hbm, ids_ref), (len_hbm, len_ref), (table_hbm, table_ref)), arrived)
    users, block = ids_ref.shape
    shards, _, lanes = out_ref.shape
    shift = rows_own.bit_length() - 1
    earlier = where_bf16(iota((block, block), 0) < iota((block, block), 1), 1.0)
    place = iota((lanes, block), 0)
    finish(copies[:1])
    total = jnp.zeros((shards, lanes), f32)
    count = jnp.int32(0)
    finish(copies[1:2])
    slot_ref[...] = jnp.zeros_like(slot_ref)
    for u in range(users):
        ids = ids_ref[u : u + 1, :]
        owner = ids >> shift
        named = iota((shards, block), 0) == owner
        named_16 = where_bf16(named, 1.0)
        before = dot(named_16, earlier)
        rank = jnp.sum(jnp.where(named, before, 0.0), axis=0, keepdims=True).astype(i32)
        high, low = halves((ids & (rows_own - 1)) + 1)
        chosen = place == rank + u * cap
        total = total + 16.0 * dot(named_16, where_bf16(chosen, high), NT)
        total = total + dot(named_16, where_bf16(chosen, low), NT)
        slot_ref[u : u + 1, :] = (owner * users + u) * cap + rank
        count = count + len_ref[u]
    wanted = jnp.where(iota((shards, lanes), 1) == users * cap, count, total.astype(i32))
    out_ref[:, 0, :] = wanted
    finish(copies[2:])


def answer_kernel(
    wanted_ref, table_ref, out_hbm, out_ref, arrived, *, per
):
    shards, _, lanes = wanted_ref.shape
    parts = 4
    group = shards // parts
    slots = group * per
    rows = table_ref.shape[0]
    repeat = where_bf16(quotient(iota((slots, group), 0), per) == iota((slots, group), 1), 1.0)
    own = remainder(iota((slots, lanes), 0), per) == iota((slots, lanes), 1)
    ones = jnp.ones((lanes, 128), bf16)
    wanted = jnp.where(iota((shards, lanes), 1) < per, wanted_ref[:, 0, :], 0)
    stores = []
    for j in range(parts):
        high, low = halves(wanted[j * group : (j + 1) * group, :])
        high = dot(where_bf16(own, dot(repeat, high.astype(bf16))), ones)
        low = dot(where_bf16(own, dot(repeat, low.astype(bf16))), ones)
        column = (16.0 * high + low).astype(i32) - 1
        hot = tiled_match(column, rows)
        at = slice(j * slots, (j + 1) * slots)
        out_ref[at, :] = dot(hot, table_ref[...]).astype(bf16)
        stores += begin([(out_ref.at[at, :], out_hbm.at[at, :])], arrived, j)
    finish(stores)


def quotient_kernel(
    len_ref,
    at_ref,
    ids_ref,
    table_ref,
    cot_ref,
    decay_ref,
    w_out_ref,
    quot_ref,
    dmixed_ref,
    wide_ref,
):
    users, block = ids_ref.shape
    heads = decay_ref.shape[1]
    rows, width = table_ref.shape
    for u in range(users):
        at = slice(u * block, (u + 1) * block)
        hot = tiled_match(spread_column(ids_ref[u : u + 1, :]), rows)
        quot_ref[at, :] = dot(hot, table_ref[...]).astype(bf16)
        valid = at_ref[0] * block + iota((block, width), 0) < len_ref[u]
        masked = jnp.where(valid, cot_ref[u].astype(f32), 0.0).astype(bf16)
        dmixed_ref[at, :] = dot(masked, w_out_ref[...], NT).astype(bf16)
        _, columns = decays(decay_ref[u], width)
        wide_ref[at, :] = over_heads(columns, heads, width)


def decays(log_decay, width):
    heads, block = log_decay.shape
    upper = jnp.where(iota((block, block), 0) <= iota((block, block), 1), 1.0, 0.0)
    lower = jnp.where(iota((block, block), 0) >= iota((block, block), 1), 1.0, 0.0)
    padded = jnp.concatenate([log_decay, jnp.zeros((8 - heads, block), f32)], axis=0)
    rows = dot(padded, upper, precision=EXACT)
    columns = dot(lower, padded, NT, precision=EXACT)
    return rows, columns


def over_heads(columns, heads, width):
    n = columns.shape[0]
    head_of = quotient(iota((n, width), 1), width // heads)
    wide = jnp.broadcast_to(columns[:, 0:1], (n, width))
    for h in range(1, heads):
        wide = jnp.where(head_of == h, jnp.broadcast_to(columns[:, h : h + 1], (n, width)), wide)
    return wide


def diagonal_heads(square, heads):
    width = square.shape[1]
    size = width // heads
    head_of = quotient(iota((size, width), 1), size)
    out = square[0:size, :]
    for h in range(1, heads):
        out = jnp.where(head_of == h, square[h * size : (h + 1) * size, :], out)
    return out


def block_diagonal(state, heads):
    size, width = state.shape
    head_of = quotient(iota((size, width), 1), width // heads)
    return jnp.concatenate([where_bf16(head_of == h, state) for h in range(heads)], axis=0)


def project_kernel(
    at_ref,
    slot_ref,
    answered_ref,
    quot_ref,
    wq_hbm,
    wk_hbm,
    wv_hbm,
    wide_ref,
    dmixed_ref,
    rem_ref,
    payload_hbm,
    wq_ref,
    wk_ref,
    wv_ref,
    states_ref,
    arrived,
    *,
    users,
    heads,
):
    slots, width = answered_ref.shape
    block = quot_ref.shape[0] // users
    peers = payload_hbm.shape[0]
    size = width // heads
    me = at_ref[0]
    ends = []
    copies = begin(
        (
            (wq_hbm, wq_ref),
            (wk_hbm, wk_ref),
            (wv_hbm, wv_ref),
        ),
        arrived,
    )
    hot = [tiled_match(spread_column(slot_ref[u : u + 1, :]), slots) for u in range(users)]
    for u in range(users):
        at = slice(u * block, (u + 1) * block)
        rem_ref[at, :] = dot(hot[u], answered_ref[...]).astype(bf16)
    finish(copies)
    for u in range(users):
        at = slice(u * block, (u + 1) * block)
        embedded = (quot_ref[at, :].astype(f32) * rem_ref[at, :].astype(f32)).astype(bf16)
        q = dot(embedded, wq_ref[...]).astype(bf16)
        k = dot(embedded, wk_ref[...]).astype(bf16)
        v = dot(embedded, wv_ref[...]).astype(bf16)
        wide = wide_ref[at, :]
        end = wide[block - 1 : block, :]
        ends.append(end)
        falling = (k.astype(f32) * jnp.exp(end - wide)).astype(bf16)
        growing = (q.astype(f32) * jnp.exp(wide)).astype(bf16)
        state = diagonal_heads(dot(falling, v, TN), heads).astype(bf16)
        grad = diagonal_heads(dot(growing, dmixed_ref[at, :], TN), heads).astype(bf16)
        states_ref[0, u * size : (u + 1) * size, :] = state
        states_ref[1, u * size : (u + 1) * size, :] = grad
    rows = iota((16, width), 0)
    tail = jnp.zeros((16, width), f32)
    for u in range(users):
        left = ends[u]
        for part in range(3):
            piece = left.astype(bf16).astype(f32)
            left = left - piece
            tail = jnp.where(rows == part * users + u, piece, tail)
    tail = tail.astype(bf16)
    states_ref[0, users * size :, :] = tail
    states_ref[1, users * size :, :] = tail
    which = [jnp.where(peer > me, 0, 1) for peer in range(peers)]
    pairs = [(states_ref.at[which[peer]], payload_hbm.at[peer]) for peer in range(peers)]
    finish(begin(pairs, arrived, 3))


def within_kernel(
    quot_ref,
    rem_ref,
    dmixed_ref,
    decay_ref,
    wq_ref,
    wk_ref,
    wv_ref,
    near_ref,
    far_hbm,
    far_ref,
    arrived,
    *,
    scale,
):
    users, heads, block = decay_ref.shape
    width = quot_ref.shape[1]
    copies = []
    head_of = quotient(iota((block, width), 1), width // heads)
    lower_tri = iota((block, block), 0) >= iota((block, block), 1)
    for u in range(users):
        at = slice(u * block, (u + 1) * block)
        embedded = (quot_ref[at, :].astype(f32) * rem_ref[at, :].astype(f32)).astype(bf16)
        q = dot(embedded, wq_ref[...]).astype(bf16)
        k = dot(embedded, wk_ref[...]).astype(bf16)
        v = dot(embedded, wv_ref[...]).astype(bf16)
        dmixed = dmixed_ref[at, :]
        rows, columns = decays(decay_ref[u], width)
        mixed = jnp.zeros((block, width), f32)
        dq = jnp.zeros((block, width), f32)
        dk = jnp.zeros((block, width), f32)
        dv = jnp.zeros((block, width), f32)
        zero = jnp.zeros((), bf16)
        for h in range(heads):
            own = head_of == h
            q_h = jnp.where(own, q, zero)
            k_h = jnp.where(own, k, zero)
            v_h = jnp.where(own, v, zero)
            d_h = jnp.where(own, dmixed, zero)
            gap = columns[:, h : h + 1] - rows[h : h + 1, :]
            mask = jnp.where(lower_tri, scale * jnp.exp(jnp.minimum(gap, 0.0)), 0.0)
            weights = (dot(q_h, k, NT) * mask).astype(bf16)
            dweights = (dot(d_h, v, NT) * mask).astype(bf16)
            mixed = mixed + dot(weights, v_h)
            dq = dq + dot(dweights, k_h)
            dk = dk + dot(dweights, q_h, TN)
            dv = dv + dot(weights, d_h, TN)
        near_ref[at, :] = mixed
        for i, part in enumerate((dq, dk, dv)):
            far_ref[i, at, :] = part
        copies += begin([(far_ref.at[:, at, :], far_hbm.at[:, at, :])], arrived, u)
    finish(copies)


def sum_half(ids, terms, owner, out_ref):
    half = out_ref.shape[0]
    chunk = min(256, half)
    for j, hot in enumerate(stacked_match(ids - owner * half, chunk, half // chunk)):
        out_ref[j * chunk : (j + 1) * chunk, :] = dot(hot, terms).astype(out_ref.dtype)


def gradient_kernel(
    at_ref,
    payload_ref,
    near_ref,
    far_hbm,
    dmixed_ref,
    wide_ref,
    rem_ref,
    quot_ref,
    slot_ref,
    ids_hbm,
    wq_hbm,
    wk_hbm,
    wv_hbm,
    w_out_hbm,
    out_hbm,
    rem_send_hbm,
    keep_ref,
    give_ref,
    far_ref,
    ids_ref,
    wq_ref,
    wk_ref,
    wv_ref,
    w_out_ref,
    out_ref,
    rem_send_ref,
    arrived,
    *,
    scale,
    heads,
):
    users, block = ids_ref.shape
    width = quot_ref.shape[1]
    copies = begin(
        (
            (wq_hbm, wq_ref),
            (wk_hbm, wk_ref),
            (wv_hbm, wv_ref),
            (w_out_hbm, w_out_ref),
            (ids_hbm, ids_ref),
        ),
        arrived,
    )
    waits = []
    for u in range(users):
        at = slice(u * block, (u + 1) * block)
        waits += begin([(far_hbm.at[:, at, :], far_ref.at[:, at, :])], arrived, 5 + u)
    peers = payload_ref.shape[0]
    size = width // heads
    slots = rem_send_ref.shape[0]
    me = at_ref[0]
    carried = []
    for u in range(users):
        ends = []
        for peer in range(peers):
            tail = payload_ref[peer, users * size :, :].astype(f32)
            ends.append(
                tail[u : u + 1, :]
                + tail[users + u : users + u + 1, :]
                + tail[2 * users + u : 2 * users + u + 1, :]
            )
        entering = jnp.zeros((size, width), f32)
        for peer in range(peers):
            part = payload_ref[peer, u * size : (u + 1) * size, :].astype(f32)
            linked = jnp.exp(ends[peer]) * entering + part
            entering = jnp.where(peer < me, linked, entering)
        leaving = jnp.zeros((size, width), f32)
        for peer in reversed(range(peers)):
            part = payload_ref[peer, u * size : (u + 1) * size, :].astype(f32)
            linked = jnp.exp(ends[peer]) * leaving + part
            leaving = jnp.where(peer > me, linked, leaving)
        carried.append((block_diagonal(entering, heads), block_diagonal(leaving, heads)))
    finish(copies)
    copies = []
    rem_terms, quot_terms = [], []
    for u in range(users):
        at = slice(u * block, (u + 1) * block)
        entering, leaving = carried[u]
        embedded = (quot_ref[at, :].astype(f32) * rem_ref[at, :].astype(f32)).astype(bf16)
        q = dot(embedded, wq_ref[...]).astype(bf16)
        k = dot(embedded, wk_ref[...]).astype(bf16)
        v = dot(embedded, wv_ref[...]).astype(bf16)
        dmixed = dmixed_ref[at, :]
        wide = wide_ref[at, :]
        growth = scale * jnp.exp(wide)
        falloff = scale * jnp.exp(wide[block - 1 : block, :] - wide)
        mixed = (near_ref[at, :] + growth * dot(q, entering)).astype(bf16)
        out_ref[u] = dot(mixed, w_out_ref[...]).astype(bf16)
        copies += begin([(out_ref.at[u], out_hbm.at[u])], arrived, 5 + users + u)
        finish(waits[u : u + 1])
        dq = (far_ref[0, at, :] + growth * dot(dmixed, entering, NT)).astype(bf16)
        dk = (far_ref[1, at, :] + falloff * dot(v, leaving, NT)).astype(bf16)
        dv = (far_ref[2, at, :] + falloff * dot(k, leaving)).astype(bf16)
        dembedded = dot(dq, wq_ref[...], NT) + dot(dk, wk_ref[...], NT) + dot(dv, wv_ref[...], NT)
        rem_terms.append((dembedded * quot_ref[at, :].astype(f32)).astype(bf16))
        quot_terms.append((dembedded * rem_ref[at, :].astype(f32)).astype(bf16))
    rem_terms = jnp.concatenate(rem_terms, axis=0)
    quot_terms = jnp.concatenate(quot_terms, axis=0)
    slot = jnp.concatenate([slot_ref[u : u + 1, :] for u in range(users)], axis=1)
    ids = jnp.concatenate([ids_ref[u : u + 1, :] for u in range(users)], axis=1)
    n = 5 + 2 * users
    for j, hot in enumerate(stacked_match(slot, block, slots // block)):
        at = slice(j * block, (j + 1) * block)
        rem_send_ref[at, :] = dot(hot, rem_terms).astype(bf16)
        copies += begin([(rem_send_ref.at[at, :], rem_send_hbm.at[at, :])], arrived, n + j)
    for ref, owner in ((give_ref, 1 - me % 2), (keep_ref, me % 2)):
        sum_half(ids, quot_terms, owner, ref)
    finish(copies)


def collect_kernel(at_ref, wanted_ref, back_ref, out_ref, *, per, other):
    shards, _, lanes = wanted_ref.shape
    slots = shards * per
    wanted = jnp.where(iota((shards, lanes), 1) < per, wanted_ref[:, 0, :], 0)
    high, low = halves(wanted)
    tile = where_bf16(remainder(iota((lanes, slots), 1), per) == iota((lanes, slots), 0), 1.0)
    own = quotient(iota((shards, slots), 1), per) == iota((shards, slots), 0)
    high = jnp.sum(jnp.where(own, dot(high.astype(bf16), tile), 0.0), axis=0, keepdims=True)
    low = jnp.sum(jnp.where(own, dot(low.astype(bf16), tile), 0.0), axis=0, keepdims=True)
    row = (16.0 * high + low).astype(i32) - 1
    core = at_ref[0] % 2
    sum_half(row, back_ref[...], 1 - core if other else core, out_ref)


def split_kernel(at_ref, keep_ref, got_ref, *out_refs):
    chips = len(out_refs)
    rows = out_refs[0].shape[0]
    bases = [
        pl.multiple_of(lax.rem(at_ref[0] // 2 + d, chips) * rows, rows) for d in range(chips)
    ]
    for base, out_ref in zip(bases, out_refs, strict=True):
        at = pl.ds(base, rows)
        out_ref[...] = (keep_ref[at, :].astype(f32) + got_ref[at, :].astype(f32)).astype(bf16)


def cut(chunk, shards):
    rows, width = chunk.shape
    lanes = width // 128
    part = rows * lanes // shards
    return [
        chunk[i // lanes * part : (i // lanes + 1) * part, i % lanes * 128 : (i % lanes + 1) * 128]
        for i in range(shards)
    ]


def total_kernel(*refs):
    total = sum((ref[...].astype(f32) for ref in refs[1:-1]), refs[0][...].astype(f32))
    for i, tile in enumerate(cut(total, refs[-1].shape[0])):
        refs[-1][i] = tile.astype(bf16)


def repeat_kernel(tiles_ref, out_ref):
    total = jnp.sum(tiles_ref[...].astype(f32), axis=0).astype(bf16)
    for i in range(out_ref.shape[0]):
        out_ref[i] = total


def place_kernel(at_ref, wanted_ref, *refs, jobs, chips, per, total):
    outs = refs[-2 * len(jobs) - 1 : -len(jobs) - 1]
    staged = refs[-len(jobs) - 1 : -1]
    arrived = refs[-1]
    copies = []
    shards, _, lanes = wanted_ref.shape
    counted = jnp.where(iota((shards, lanes), 1) == per, wanted_ref[:, 0, :], 0)
    ratio = total / jnp.sum(counted.astype(f32), axis=(0, 1), keepdims=True)
    chip, core = at_ref[0] // 2, at_ref[0] % 2
    for n, other in enumerate(jobs):
        out_hbm, out_ref = outs[n], staged[n]
        _, rows, width = out_ref.shape
        half = core + other - 2 * core * other
        for d in range(chips):
            chunk = refs[n * chips + d]
            spot = half * chips + lax.rem(chip + chips - d, chips)
            base = pl.multiple_of(spot * rows, rows)
            if len(chunk.shape) == 2:
                out_ref[d] = ratio * chunk[...].astype(f32)
            else:
                part = chunk.shape[1]
                for i in range(shards):
                    across = i % (width // 128) * 128
                    down = i // (width // 128) * part
                    tile = ratio * chunk[i].astype(f32)
                    out_ref[d, down : down + part, across : across + 128] = tile
            pair = (out_ref.at[d], out_hbm.at[pl.ds(base, rows), :])
            copies += begin([pair], arrived, n * chips + d)
    finish(copies)


def exchange(array, axis):
    return lax.all_to_all(array, axis, split_axis=0, concat_axis=0, tiled=True)


def to_core(array):
    peers = lax.axis_size("hist")
    return lax.ppermute(array, "hist", [(i, i ^ 1) for i in range(peers)])


def to_chip(array, steps):
    peers = lax.axis_size("hist")
    return lax.ppermute(array, "hist", [(i, (i + 2 * steps) % peers) for i in range(peers)])


def split(at, keep, give, spec=VM):
    chips = lax.axis_size("hist") // 2
    outs = [((keep.shape[0] // chips, keep.shape[1]), bf16)] * chips
    return call(split_kernel, outs, (at, keep, to_core(give)), [SM, spec, VM])


def shared(chunks):
    return [chunks[0]] + [to_chip(chunks[d], d) for d in range(1, len(chunks))]


def along_chips(chunk):
    chips = lax.axis_size("hist") // 2
    return [chunk] + [to_chip(chunk, d) for d in range(1, chips)]


def place(at, wanted, jobs, width, per, total):
    chips = len(jobs[0][0])
    args, specs, outs, scratch, others, aliases = (at, wanted), [SM, VM], [], [], [], {}
    for chunks, rows, out in jobs:
        args, specs = args + tuple(chunks), specs + [VM] * chips
        outs.append(((rows, width), f32))
        scratch.append(pltpu.VMEM((chips, rows // (2 * chips), width), f32))
        others.append(0 if out is None else 1)
    for n, (_, _, out) in enumerate(jobs):
        if out is not None:
            aliases[len(args)] = n
            args, specs = args + (out,), specs + [HB]
    kernel = functools.partial(
        place_kernel, jobs=tuple(others), chips=chips, per=per, total=total
    )
    scratch.append(dma(chips * len(jobs)))
    return call(kernel, outs, args, specs, scratch, [HB] * len(jobs), aliases=aliases)


def body(
    quot_ids,
    rem_ids,
    lengths,
    log_decay,
    quot_table,
    rem_table,
    w_query,
    w_key,
    w_value,
    w_out,
    cotangent,
):
    users, block = quot_ids.shape
    rows_all, width = quot_table.shape
    heads = log_decay.shape[1]
    size = width // heads
    shards = lax.axis_size("user")
    peers = lax.axis_size("hist")
    rows_own = rem_table.shape[0]
    cap = 2 * block // shards
    per = users * cap
    slots = shards * per
    scale = 1.0 / math.sqrt(size * block * peers)
    at = lax.axis_index("hist").astype(i32).reshape(1)
    lanes = (per // 128 + 1) * 128

    square = pltpu.VMEM((width, width), bf16)
    requests, slot, table = call(
        functools.partial(request_kernel, rows_own=rows_own, cap=cap),
        [((shards, 1, lanes), i32), ((8, block), i32), (rem_table.shape, bf16)],
        (lengths, rem_ids, rem_table),
        [HB, HB, HB],
        [pltpu.SMEM((users,), i32), pltpu.VMEM((users, block), i32), dma(3)],
        [VM, IN_VM, IN_VM],
        MOST,
    )
    wanted = exchange(requests, "user")
    quot_emb, dmixed, wide = call(
        quotient_kernel,
        [
            ((users * block, width), bf16),
            ((users * block, width), bf16),
            ((users * block, width), f32),
        ],
        (lengths, at)
        + tuple(in_hbm(a) for a in (quot_ids, quot_table, cotangent, log_decay, w_out)),
        [SM, SM] + [VM] * 5,
        (),
        [IN_VM] * 3,
        MOST,
    )
    (found,) = call(
        functools.partial(answer_kernel, per=per),
        [((slots, width), bf16)],
        (wanted, table),
        [VM, IN_VM],
        [pltpu.VMEM((slots, width), bf16), dma(4)],
        [HB],
        MOST,
    )
    answered = exchange(found.reshape(shards, per, width), "user").reshape(slots, width)
    rem_emb, payload = call(
        functools.partial(project_kernel, users=users, heads=heads),
        [((users * block, width), bf16), ((peers, users * size + 16, width), bf16)],
        (at, slot, answered, quot_emb, w_query, w_key, w_value, wide, dmixed),
        [SM, IN_VM, VM, IN_VM, HB, HB, HB, IN_VM, IN_VM],
        [square] * 3 + [pltpu.VMEM((2, users * size + 16, width), bf16), dma(3 + peers)],
        [IN_VM, HB],
        MOST,
    )
    states = exchange(payload, "hist")
    parts = (3, users * block, width)
    near, far = call(
        functools.partial(within_kernel, scale=scale),
        [(parts[1:], f32), (parts, f32)],
        (quot_emb, rem_emb, dmixed)
        + tuple(in_hbm(a) for a in (log_decay, w_query, w_key, w_value)),
        [IN_VM] * 3 + [VM] * 4,
        [pltpu.VMEM(parts, f32), dma(users)],
        [IN_VM, HB],
        MOST,
    )
    output, rem_send, keep, give = call(
        functools.partial(gradient_kernel, scale=scale, heads=heads),
        [
            ((users, block, width), bf16),
            ((slots, width), bf16),
            ((rows_all // 2, width), bf16),
            ((rows_all // 2, width), bf16),
        ],
        (at, states, near, far, dmixed, wide, rem_emb, quot_emb, slot, quot_ids)
        + (w_query, w_key, w_value, w_out),
        [SM, VM, IN_VM, HB] + [IN_VM] * 5 + [HB] * 5,
        [pltpu.VMEM(parts, f32), pltpu.VMEM((users, block), i32)]
        + [square] * 4
        + [pltpu.VMEM((users, block, width), bf16), pltpu.VMEM((slots, width), bf16)]
        + [dma(5 + 2 * users + slots // block)],
        [HB, HB, IN_VM, IN_VM],
        MOST,
    )
    rem_back = exchange(rem_send.reshape(shards, per, width), "user").reshape(slots, width)
    tiles = (shards, rows_all // peers * width // shards // 128, 128)
    (quot_tiles,) = call(total_kernel, [(tiles, bf16)], shared(split(at, keep, give, IN_VM)))
    rem_back, quot_tiles = lax.optimization_barrier((rem_back, quot_tiles))
    quot_back = exchange(quot_tiles, "user")
    keep, give = (
        call(
            functools.partial(collect_kernel, per=per, other=other),
            [((rows_own // 2, width), bf16 if other else f32)],
            (at, wanted, rem_back),
            [SM, VM, VM],
        )[0]
        for other in (False, True)
    )
    chunks = split(at, keep, give)
    (quot_tiles,) = call(repeat_kernel, [(tiles, bf16)], (quot_back,))
    quot_tiles, *_ = lax.optimization_barrier((quot_tiles, *chunks))
    quot_tiles = exchange(quot_tiles, "user")
    rem_sum = sum(c.astype(f32) for c in shared(chunks)).astype(bf16)
    rem_mine = along_chips(rem_sum)
    quot_tiles, _ = lax.optimization_barrier((quot_tiles, rem_sum))
    total = float(users * shards * block * peers)
    (rem_grad,) = place(at, wanted, [(rem_mine, rows_own, None)], width, per, total)
    quot_mine = along_chips(quot_tiles)
    rem_theirs = [to_core(c) for c in rem_mine]
    *quot_mine, rem_grad = lax.optimization_barrier((*quot_mine, rem_grad))
    quot_theirs = [to_core(c) for c in quot_mine]
    jobs = [(quot_mine, rows_all, None), (rem_theirs, rows_own, rem_grad)]
    quot_grad, rem_grad = place(at, wanted, jobs, width, per, total)
    (quot_grad,) = place(at, wanted, [(quot_theirs, rows_all, quot_grad)], width, per, total)
    return (output, quot_grad, rem_grad)


def solution(mesh):
    return jax.shard_map(
        body,
        mesh=mesh,
        in_specs=(
            P("user", "hist"),
            P("user", "hist"),
            P("user"),
            P("user", None, "hist"),
            P(),
            P("user", None),
            P(),
            P(),
            P(),
            P(),
            P("user", "hist", None),
        ),
        out_specs=(P("user", "hist", None), P(), P("user", None)),
        check_vma=False,
    )
```

```python
import functools
import math

import jax
import jax.numpy as jnp
from jax import lax
from jax.experimental import pallas as pl
from jax.experimental.pallas import tpu as pltpu
from jax.sharding import PartitionSpec as P

f32 = jnp.float32
bf16 = jnp.bfloat16
i32 = jnp.int32
FULL = 62
MOST = 24
EXACT = lax.Precision.HIGHEST
VM = pl.BlockSpec(memory_space=pltpu.VMEM)
SM = pl.BlockSpec(memory_space=pltpu.SMEM)
HB = pl.BlockSpec(memory_space=pltpu.HBM)
IN_VM = pl.BlockSpec(memory_space=pltpu.VMEM)

NN = (((1,), (0,)), ((), ()))
NT = (((1,), (1,)), ((), ()))
TN = (((0,), (0,)), ((), ()))


def dot(a, b, dims=NN, precision=None):
    return lax.dot_general(a, b, dims, preferred_element_type=f32, precision=precision)


def iota(shape, dim):
    return lax.broadcasted_iota(i32, shape, dim)


def quotient(a, n):
    return a >> (n.bit_length() - 1) if n & (n - 1) == 0 else a // n


def remainder(a, n):
    return a & (n - 1) if n & (n - 1) == 0 else a % n


def where_bf16(mask, a):
    return jnp.where(mask, a, 0.0).astype(bf16)


def halves(whole):
    return (whole >> 4).astype(f32), (whole & 15).astype(f32)


def spread_column(row):
    n = row.shape[1]
    diagonal = iota((n, n), 0) == iota((n, n), 1)
    high, low = halves(row)
    ones = jnp.ones((n, 128), bf16)
    column = 16.0 * dot(where_bf16(diagonal, high), ones) + dot(where_bf16(diagonal, low), ones)
    return column.astype(i32)


def tiled_match(column, width):
    near = where_bf16(iota(column.shape, 1) == (column & 127), 1.0)
    tile = (column >> 7).astype(f32).astype(bf16)
    zero = jnp.zeros_like(near)
    parts = [jnp.where(tile == jnp.asarray(j, bf16), near, zero) for j in range(width // 128)]
    return jnp.concatenate(parts, axis=1)


def stacked_match(row, chunk, count):
    row = jnp.broadcast_to(row, (chunk, row.shape[1]))
    near = where_bf16(iota(row.shape, 0) == (row & (chunk - 1)), 1.0)
    part = (row >> (chunk.bit_length() - 1)).astype(f32).astype(bf16)
    zero = jnp.zeros_like(near)
    return [jnp.where(part == jnp.asarray(j, bf16), near, zero) for j in range(count)]


def begin(pairs, arrived, at=0):
    copies = [
        pltpu.make_async_copy(source, target, arrived.at[at + i])
        for i, (source, target) in enumerate(pairs)
    ]
    for copy in copies:
        copy.start()
    return copies


def finish(copies):
    for copy in copies:
        copy.wait()


def dma(n):
    return pltpu.SemaphoreType.DMA((n,))


def held(spec):
    return pltpu.HBM if spec is HB else pltpu.VMEM if spec is IN_VM else None


def in_hbm(array):
    return pltpu.with_memory_space_constraint(array, pltpu.HBM)


def call(kernel, outs, args, specs=None, scratch=(), out_specs=None, limit=16, aliases={}):
    out_specs = out_specs if out_specs is not None else [VM] * len(outs)
    shapes = [
        held(spec)(s, d) if held(spec) else jax.ShapeDtypeStruct(s, d)
        for (s, d), spec in zip(outs, out_specs, strict=True)
    ]
    specs = specs if specs is not None else [VM] * len(args)
    args = [
        pltpu.with_memory_space_constraint(a, held(spec)) if held(spec) else a
        for a, spec in zip(args, specs, strict=True)
    ]
    return pl.pallas_call(
        kernel,
        out_shape=tuple(shapes),
        in_specs=specs,
        out_specs=tuple(out_specs),
        input_output_aliases=aliases,
        scratch_shapes=list(scratch),
        compiler_params=pltpu.CompilerParams(vmem_limit_bytes=limit * 1024 * 1024),
    )(*args)


def request_kernel(
    len_hbm, ids_hbm, table_hbm, out_ref, slot_ref, table_ref, len_ref, ids_ref, arrived,
    *, rows_own, cap,
):
    copies = begin(((ids_hbm, ids_ref), (len_hbm, len_ref), (table_hbm, table_ref)), arrived)
    users, block = ids_ref.shape
    shards, _, lanes = out_ref.shape
    shift = rows_own.bit_length() - 1
    earlier = where_bf16(iota((block, block), 0) < iota((block, block), 1), 1.0)
    place = iota((lanes, block), 0)
    finish(copies[:1])
    total = jnp.zeros((shards, lanes), f32)
    count = jnp.int32(0)
    finish(copies[1:2])
    slot_ref[...] = jnp.zeros_like(slot_ref)
    for u in range(users):
        ids = ids_ref[u : u + 1, :]
        owner = ids >> shift
        named = iota((shards, block), 0) == owner
        named_16 = where_bf16(named, 1.0)
        before = dot(named_16, earlier)
        rank = jnp.sum(jnp.where(named, before, 0.0), axis=0, keepdims=True).astype(i32)
        high, low = halves((ids & (rows_own - 1)) + 1)
        chosen = place == rank + u * cap
        total = total + 16.0 * dot(named_16, where_bf16(chosen, high), NT)
        total = total + dot(named_16, where_bf16(chosen, low), NT)
        slot_ref[u : u + 1, :] = (owner * users + u) * cap + rank
        count = count + len_ref[u]
    wanted = jnp.where(iota((shards, lanes), 1) == users * cap, count, total.astype(i32))
    out_ref[:, 0, :] = wanted
    finish(copies[2:])


def answer_kernel(
    wanted_ref, table_ref, out_hbm, out_ref, arrived, *, per
):
    shards, _, lanes = wanted_ref.shape
    parts = 4
    group = shards // parts
    slots = group * per
    rows = table_ref.shape[0]
    repeat = where_bf16(quotient(iota((slots, group), 0), per) == iota((slots, group), 1), 1.0)
    own = remainder(iota((slots, lanes), 0), per) == iota((slots, lanes), 1)
    ones = jnp.ones((lanes, 128), bf16)
    wanted = jnp.where(iota((shards, lanes), 1) < per, wanted_ref[:, 0, :], 0)
    stores = []
    for j in range(parts):
        high, low = halves(wanted[j * group : (j + 1) * group, :])
        high = dot(where_bf16(own, dot(repeat, high.astype(bf16))), ones)
        low = dot(where_bf16(own, dot(repeat, low.astype(bf16))), ones)
        column = (16.0 * high + low).astype(i32) - 1
        hot = tiled_match(column, rows)
        at = slice(j * slots, (j + 1) * slots)
        out_ref[at, :] = dot(hot, table_ref[...]).astype(bf16)
        stores += begin([(out_ref.at[at, :], out_hbm.at[at, :])], arrived, j)
    finish(stores)


def quotient_kernel(
    len_ref,
    at_ref,
    ids_ref,
    table_ref,
    cot_ref,
    decay_ref,
    w_out_ref,
    quot_ref,
    dmixed_ref,
    wide_ref,
):
    users, block = ids_ref.shape
    heads = decay_ref.shape[1]
    rows, width = table_ref.shape
    for u in range(users):
        at = slice(u * block, (u + 1) * block)
        hot = tiled_match(spread_column(ids_ref[u : u + 1, :]), rows)
        quot_ref[at, :] = dot(hot, table_ref[...]).astype(bf16)
        valid = at_ref[0] * block + iota((block, width), 0) < len_ref[u]
        masked = jnp.where(valid, cot_ref[u].astype(f32), 0.0).astype(bf16)
        dmixed_ref[at, :] = dot(masked, w_out_ref[...], NT).astype(bf16)
        _, columns = decays(decay_ref[u], width)
        wide_ref[at, :] = over_heads(columns, heads, width)


def decays(log_decay, width):
    heads, block = log_decay.shape
    upper = jnp.where(iota((block, block), 0) <= iota((block, block), 1), 1.0, 0.0)
    lower = jnp.where(iota((block, block), 0) >= iota((block, block), 1), 1.0, 0.0)
    padded = jnp.concatenate([log_decay, jnp.zeros((8 - heads, block), f32)], axis=0)
    rows = dot(padded, upper, precision=EXACT)
    columns = dot(lower, padded, NT, precision=EXACT)
    return rows, columns


def over_heads(columns, heads, width):
    n = columns.shape[0]
    head_of = quotient(iota((n, width), 1), width // heads)
    wide = jnp.broadcast_to(columns[:, 0:1], (n, width))
    for h in range(1, heads):
        wide = jnp.where(head_of == h, jnp.broadcast_to(columns[:, h : h + 1], (n, width)), wide)
    return wide


def diagonal_heads(square, heads):
    width = square.shape[1]
    size = width // heads
    head_of = quotient(iota((size, width), 1), size)
    out = square[0:size, :]
    for h in range(1, heads):
        out = jnp.where(head_of == h, square[h * size : (h + 1) * size, :], out)
    return out


def block_diagonal(state, heads):
    size, width = state.shape
    head_of = quotient(iota((size, width), 1), width // heads)
    return jnp.concatenate([where_bf16(head_of == h, state) for h in range(heads)], axis=0)


def project_kernel(
    at_ref,
    slot_ref,
    answered_ref,
    quot_ref,
    wq_hbm,
    wk_hbm,
    wv_hbm,
    wide_ref,
    dmixed_ref,
    rem_ref,
    payload_hbm,
    wq_ref,
    wk_ref,
    wv_ref,
    states_ref,
    arrived,
    *,
    users,
    heads,
):
    slots, width = answered_ref.shape
    block = quot_ref.shape[0] // users
    peers = payload_hbm.shape[0]
    size = width // heads
    me = at_ref[0]
    ends = []
    copies = begin(
        (
            (wq_hbm, wq_ref),
            (wk_hbm, wk_ref),
            (wv_hbm, wv_ref),
        ),
        arrived,
    )
    hot = [tiled_match(spread_column(slot_ref[u : u + 1, :]), slots) for u in range(users)]
    for u in range(users):
        at = slice(u * block, (u + 1) * block)
        rem_ref[at, :] = dot(hot[u], answered_ref[...]).astype(bf16)
    finish(copies)
    for u in range(users):
        at = slice(u * block, (u + 1) * block)
        embedded = (quot_ref[at, :].astype(f32) * rem_ref[at, :].astype(f32)).astype(bf16)
        q = dot(embedded, wq_ref[...]).astype(bf16)
        k = dot(embedded, wk_ref[...]).astype(bf16)
        v = dot(embedded, wv_ref[...]).astype(bf16)
        wide = wide_ref[at, :]
        end = wide[block - 1 : block, :]
        ends.append(end)
        falling = (k.astype(f32) * jnp.exp(end - wide)).astype(bf16)
        growing = (q.astype(f32) * jnp.exp(wide)).astype(bf16)
        state = diagonal_heads(dot(falling, v, TN), heads).astype(bf16)
        grad = diagonal_heads(dot(growing, dmixed_ref[at, :], TN), heads).astype(bf16)
        states_ref[0, u * size : (u + 1) * size, :] = state
        states_ref[1, u * size : (u + 1) * size, :] = grad
    rows = iota((16, width), 0)
    tail = jnp.zeros((16, width), f32)
    for u in range(users):
        left = ends[u]
        for part in range(3):
            piece = left.astype(bf16).astype(f32)
            left = left - piece
            tail = jnp.where(rows == part * users + u, piece, tail)
    tail = tail.astype(bf16)
    states_ref[0, users * size :, :] = tail
    states_ref[1, users * size :, :] = tail
    which = [jnp.where(peer > me, 0, 1) for peer in range(peers)]
    pairs = [(states_ref.at[which[peer]], payload_hbm.at[peer]) for peer in range(peers)]
    finish(begin(pairs, arrived, 3))


def within_kernel(
    quot_ref,
    rem_ref,
    dmixed_ref,
    decay_ref,
    wq_ref,
    wk_ref,
    wv_ref,
    near_ref,
    far_hbm,
    far_ref,
    arrived,
    *,
    scale,
):
    users, heads, block = decay_ref.shape
    width = quot_ref.shape[1]
    copies = []
    head_of = quotient(iota((block, width), 1), width // heads)
    lower_tri = iota((block, block), 0) >= iota((block, block), 1)
    for u in range(users):
        at = slice(u * block, (u + 1) * block)
        embedded = (quot_ref[at, :].astype(f32) * rem_ref[at, :].astype(f32)).astype(bf16)
        q = dot(embedded, wq_ref[...]).astype(bf16)
        k = dot(embedded, wk_ref[...]).astype(bf16)
        v = dot(embedded, wv_ref[...]).astype(bf16)
        dmixed = dmixed_ref[at, :]
        rows, columns = decays(decay_ref[u], width)
        mixed = jnp.zeros((block, width), f32)
        dq = jnp.zeros((block, width), f32)
        dk = jnp.zeros((block, width), f32)
        dv = jnp.zeros((block, width), f32)
        zero = jnp.zeros((), bf16)
        for h in range(heads):
            own = head_of == h
            q_h = jnp.where(own, q, zero)
            k_h = jnp.where(own, k, zero)
            v_h = jnp.where(own, v, zero)
            d_h = jnp.where(own, dmixed, zero)
            gap = columns[:, h : h + 1] - rows[h : h + 1, :]
            mask = jnp.where(lower_tri, scale * jnp.exp(jnp.minimum(gap, 0.0)), 0.0)
            weights = (dot(q_h, k, NT) * mask).astype(bf16)
            dweights = (dot(d_h, v, NT) * mask).astype(bf16)
            mixed = mixed + dot(weights, v_h)
            dq = dq + dot(dweights, k_h)
            dk = dk + dot(dweights, q_h, TN)
            dv = dv + dot(weights, d_h, TN)
        near_ref[at, :] = mixed
        for i, part in enumerate((dq, dk, dv)):
            far_ref[i, at, :] = part
        copies += begin([(far_ref.at[:, at, :], far_hbm.at[:, at, :])], arrived, u)
    finish(copies)


def sum_half(ids, terms, owner, out_ref):
    half = out_ref.shape[0]
    chunk = min(256, half)
    for j, hot in enumerate(stacked_match(ids - owner * half, chunk, half // chunk)):
        out_ref[j * chunk : (j + 1) * chunk, :] = dot(hot, terms).astype(out_ref.dtype)


def gradient_kernel(
    at_ref,
    payload_ref,
    near_ref,
    far_hbm,
    dmixed_ref,
    wide_ref,
    rem_ref,
    quot_ref,
    slot_ref,
    ids_hbm,
    wq_hbm,
    wk_hbm,
    wv_hbm,
    w_out_hbm,
    out_hbm,
    rem_send_hbm,
    keep_ref,
    give_ref,
    far_ref,
    ids_ref,
    wq_ref,
    wk_ref,
    wv_ref,
    w_out_ref,
    out_ref,
    rem_send_ref,
    arrived,
    *,
    scale,
    heads,
):
    users, block = ids_ref.shape
    width = quot_ref.shape[1]
    copies = begin(
        (
            (wq_hbm, wq_ref),
            (wk_hbm, wk_ref),
            (wv_hbm, wv_ref),
            (w_out_hbm, w_out_ref),
            (ids_hbm, ids_ref),
        ),
        arrived,
    )
    waits = []
    for u in range(users):
        at = slice(u * block, (u + 1) * block)
        waits += begin([(far_hbm.at[:, at, :], far_ref.at[:, at, :])], arrived, 5 + u)
    peers = payload_ref.shape[0]
    size = width // heads
    slots = rem_send_ref.shape[0]
    me = at_ref[0]
    carried = []
    for u in range(users):
        ends = []
        for peer in range(peers):
            tail = payload_ref[peer, users * size :, :].astype(f32)
            ends.append(
                tail[u : u + 1, :]
                + tail[users + u : users + u + 1, :]
                + tail[2 * users + u : 2 * users + u + 1, :]
            )
        entering = jnp.zeros((size, width), f32)
        for peer in range(peers):
            part = payload_ref[peer, u * size : (u + 1) * size, :].astype(f32)
            linked = jnp.exp(ends[peer]) * entering + part
            entering = jnp.where(peer < me, linked, entering)
        leaving = jnp.zeros((size, width), f32)
        for peer in reversed(range(peers)):
            part = payload_ref[peer, u * size : (u + 1) * size, :].astype(f32)
            linked = jnp.exp(ends[peer]) * leaving + part
            leaving = jnp.where(peer > me, linked, leaving)
        carried.append((block_diagonal(entering, heads), block_diagonal(leaving, heads)))
    late, copies = copies, []
    rem_terms, quot_terms = [], []
    for u in range(users):
        at = slice(u * block, (u + 1) * block)
        entering, leaving = carried[u]
        dmixed = dmixed_ref[at, :]
        wide = wide_ref[at, :]
        growth = scale * jnp.exp(wide)
        falloff = scale * jnp.exp(wide[block - 1 : block, :] - wide)
        dq_carried = growth * dot(dmixed, entering, NT)
        if u == 0:
            finish(late)
        embedded = (quot_ref[at, :].astype(f32) * rem_ref[at, :].astype(f32)).astype(bf16)
        q = dot(embedded, wq_ref[...]).astype(bf16)
        k = dot(embedded, wk_ref[...]).astype(bf16)
        v = dot(embedded, wv_ref[...]).astype(bf16)
        mixed = (near_ref[at, :] + growth * dot(q, entering)).astype(bf16)
        out_ref[u] = dot(mixed, w_out_ref[...]).astype(bf16)
        copies += begin([(out_ref.at[u], out_hbm.at[u])], arrived, 5 + users + u)
        finish(waits[u : u + 1])
        dq = (far_ref[0, at, :] + dq_carried).astype(bf16)
        dk = (far_ref[1, at, :] + falloff * dot(v, leaving, NT)).astype(bf16)
        dv = (far_ref[2, at, :] + falloff * dot(k, leaving)).astype(bf16)
        dembedded = dot(dq, wq_ref[...], NT) + dot(dk, wk_ref[...], NT) + dot(dv, wv_ref[...], NT)
        rem_terms.append((dembedded * quot_ref[at, :].astype(f32)).astype(bf16))
        quot_terms.append((dembedded * rem_ref[at, :].astype(f32)).astype(bf16))
    rem_terms = jnp.concatenate(rem_terms, axis=0)
    quot_terms = jnp.concatenate(quot_terms, axis=0)
    slot = jnp.concatenate([slot_ref[u : u + 1, :] for u in range(users)], axis=1)
    ids = jnp.concatenate([ids_ref[u : u + 1, :] for u in range(users)], axis=1)
    n = 5 + 2 * users
    for j, hot in enumerate(stacked_match(slot, block, slots // block)):
        at = slice(j * block, (j + 1) * block)
        rem_send_ref[at, :] = dot(hot, rem_terms).astype(bf16)
        copies += begin([(rem_send_ref.at[at, :], rem_send_hbm.at[at, :])], arrived, n + j)
    for ref, owner in ((give_ref, 1 - me % 2), (keep_ref, me % 2)):
        sum_half(ids, quot_terms, owner, ref)
    finish(copies)


def collect_kernel(at_ref, wanted_ref, back_ref, out_ref, *, per, other):
    shards, _, lanes = wanted_ref.shape
    slots = shards * per
    wanted = jnp.where(iota((shards, lanes), 1) < per, wanted_ref[:, 0, :], 0)
    high, low = halves(wanted)
    tile = where_bf16(remainder(iota((lanes, slots), 1), per) == iota((lanes, slots), 0), 1.0)
    own = quotient(iota((shards, slots), 1), per) == iota((shards, slots), 0)
    high = jnp.sum(jnp.where(own, dot(high.astype(bf16), tile), 0.0), axis=0, keepdims=True)
    low = jnp.sum(jnp.where(own, dot(low.astype(bf16), tile), 0.0), axis=0, keepdims=True)
    row = (16.0 * high + low).astype(i32) - 1
    core = at_ref[0] % 2
    sum_half(row, back_ref[...], 1 - core if other else core, out_ref)


def split_kernel(at_ref, keep_ref, got_ref, *out_refs):
    chips = len(out_refs)
    rows = out_refs[0].shape[0]
    bases = [
        pl.multiple_of(lax.rem(at_ref[0] // 2 + d, chips) * rows, rows) for d in range(chips)
    ]
    for base, out_ref in zip(bases, out_refs, strict=True):
        at = pl.ds(base, rows)
        out_ref[...] = (keep_ref[at, :].astype(f32) + got_ref[at, :].astype(f32)).astype(bf16)


def cut(chunk, shards):
    rows, width = chunk.shape
    lanes = width // 128
    part = rows * lanes // shards
    return [
        chunk[i // lanes * part : (i // lanes + 1) * part, i % lanes * 128 : (i % lanes + 1) * 128]
        for i in range(shards)
    ]


def total_kernel(*refs):
    total = sum((ref[...].astype(f32) for ref in refs[1:-1]), refs[0][...].astype(f32))
    for i, tile in enumerate(cut(total, refs[-1].shape[0])):
        refs[-1][i] = tile.astype(bf16)


def repeat_kernel(tiles_ref, out_ref):
    total = jnp.sum(tiles_ref[...].astype(f32), axis=0).astype(bf16)
    for i in range(out_ref.shape[0]):
        out_ref[i] = total


def place_kernel(at_ref, wanted_ref, *refs, jobs, chips, per, total):
    outs = refs[-2 * len(jobs) - 1 : -len(jobs) - 1]
    staged = refs[-len(jobs) - 1 : -1]
    arrived = refs[-1]
    copies = []
    shards, _, lanes = wanted_ref.shape
    counted = jnp.where(iota((shards, lanes), 1) == per, wanted_ref[:, 0, :], 0)
    ratio = total / jnp.sum(counted.astype(f32), axis=(0, 1), keepdims=True)
    chip, core = at_ref[0] // 2, at_ref[0] % 2
    for n, other in enumerate(jobs):
        out_hbm, out_ref = outs[n], staged[n]
        _, rows, width = out_ref.shape
        half = core + other - 2 * core * other
        for d in range(chips):
            chunk = refs[n * chips + d]
            spot = half * chips + lax.rem(chip + chips - d, chips)
            base = pl.multiple_of(spot * rows, rows)
            if len(chunk.shape) == 2:
                out_ref[d] = ratio * chunk[...].astype(f32)
            else:
                part = chunk.shape[1]
                for i in range(shards):
                    across = i % (width // 128) * 128
                    down = i // (width // 128) * part
                    tile = ratio * chunk[i].astype(f32)
                    out_ref[d, down : down + part, across : across + 128] = tile
            pair = (out_ref.at[d], out_hbm.at[pl.ds(base, rows), :])
            copies += begin([pair], arrived, n * chips + d)
    finish(copies)


def exchange(array, axis):
    return lax.all_to_all(array, axis, split_axis=0, concat_axis=0, tiled=True)


def to_core(array):
    peers = lax.axis_size("hist")
    return lax.ppermute(array, "hist", [(i, i ^ 1) for i in range(peers)])


def to_chip(array, steps):
    peers = lax.axis_size("hist")
    return lax.ppermute(array, "hist", [(i, (i + 2 * steps) % peers) for i in range(peers)])


def split(at, keep, give, spec=VM):
    chips = lax.axis_size("hist") // 2
    outs = [((keep.shape[0] // chips, keep.shape[1]), bf16)] * chips
    return call(split_kernel, outs, (at, keep, to_core(give)), [SM, spec, VM])


def shared(chunks):
    return [chunks[0]] + [to_chip(chunks[d], d) for d in range(1, len(chunks))]


def along_chips(chunk):
    chips = lax.axis_size("hist") // 2
    return [chunk] + [to_chip(chunk, d) for d in range(1, chips)]


def place(at, wanted, jobs, width, per, total):
    chips = len(jobs[0][0])
    args, specs, outs, scratch, others, aliases = (at, wanted), [SM, VM], [], [], [], {}
    for chunks, rows, out in jobs:
        args, specs = args + tuple(chunks), specs + [VM] * chips
        outs.append(((rows, width), f32))
        scratch.append(pltpu.VMEM((chips, rows // (2 * chips), width), f32))
        others.append(0 if out is None else 1)
    for n, (_, _, out) in enumerate(jobs):
        if out is not None:
            aliases[len(args)] = n
            args, specs = args + (out,), specs + [HB]
    kernel = functools.partial(
        place_kernel, jobs=tuple(others), chips=chips, per=per, total=total
    )
    scratch.append(dma(chips * len(jobs)))
    return call(kernel, outs, args, specs, scratch, [HB] * len(jobs), aliases=aliases)


def body(
    quot_ids,
    rem_ids,
    lengths,
    log_decay,
    quot_table,
    rem_table,
    w_query,
    w_key,
    w_value,
    w_out,
    cotangent,
):
    users, block = quot_ids.shape
    rows_all, width = quot_table.shape
    heads = log_decay.shape[1]
    size = width // heads
    shards = lax.axis_size("user")
    peers = lax.axis_size("hist")
    rows_own = rem_table.shape[0]
    cap = 2 * block // shards
    per = users * cap
    slots = shards * per
    scale = 1.0 / math.sqrt(size * block * peers)
    at = lax.axis_index("hist").astype(i32).reshape(1)
    lanes = (per // 128 + 1) * 128

    square = pltpu.VMEM((width, width), bf16)
    requests, slot, table = call(
        functools.partial(request_kernel, rows_own=rows_own, cap=cap),
        [((shards, 1, lanes), i32), ((8, block), i32), (rem_table.shape, bf16)],
        (lengths, rem_ids, rem_table),
        [HB, HB, HB],
        [pltpu.SMEM((users,), i32), pltpu.VMEM((users, block), i32), dma(3)],
        [VM, IN_VM, IN_VM],
        MOST,
    )
    wanted = exchange(requests, "user")
    quot_emb, dmixed, wide = call(
        quotient_kernel,
        [
            ((users * block, width), bf16),
            ((users * block, width), bf16),
            ((users * block, width), f32),
        ],
        (lengths, at)
        + tuple(in_hbm(a) for a in (quot_ids, quot_table, cotangent, log_decay, w_out)),
        [SM, SM] + [VM] * 5,
        (),
        [IN_VM] * 3,
        MOST,
    )
    (found,) = call(
        functools.partial(answer_kernel, per=per),
        [((slots, width), bf16)],
        (wanted, table),
        [VM, IN_VM],
        [pltpu.VMEM((slots, width), bf16), dma(4)],
        [HB],
        MOST,
    )
    answered = exchange(found.reshape(shards, per, width), "user").reshape(slots, width)
    rem_emb, payload = call(
        functools.partial(project_kernel, users=users, heads=heads),
        [((users * block, width), bf16), ((peers, users * size + 16, width), bf16)],
        (at, slot, answered, quot_emb, w_query, w_key, w_value, wide, dmixed),
        [SM, IN_VM, VM, IN_VM, HB, HB, HB, IN_VM, IN_VM],
        [square] * 3 + [pltpu.VMEM((2, users * size + 16, width), bf16), dma(3 + peers)],
        [IN_VM, HB],
        MOST,
    )
    states = exchange(payload, "hist")
    parts = (3, users * block, width)
    near, far = call(
        functools.partial(within_kernel, scale=scale),
        [(parts[1:], f32), (parts, f32)],
        (quot_emb, rem_emb, dmixed)
        + tuple(in_hbm(a) for a in (log_decay, w_query, w_key, w_value)),
        [IN_VM] * 3 + [VM] * 4,
        [pltpu.VMEM(parts, f32), dma(users)],
        [IN_VM, HB],
        MOST,
    )
    output, rem_send, keep, give = call(
        functools.partial(gradient_kernel, scale=scale, heads=heads),
        [
            ((users, block, width), bf16),
            ((slots, width), bf16),
            ((rows_all // 2, width), bf16),
            ((rows_all // 2, width), bf16),
        ],
        (at, states, near, far, dmixed, wide, rem_emb, quot_emb, slot, quot_ids)
        + (w_query, w_key, w_value, w_out),
        [SM, VM, IN_VM, HB] + [IN_VM] * 5 + [HB] * 5,
        [pltpu.VMEM(parts, f32), pltpu.VMEM((users, block), i32)]
        + [square] * 4
        + [pltpu.VMEM((users, block, width), bf16), pltpu.VMEM((slots, width), bf16)]
        + [dma(5 + 2 * users + slots // block)],
        [HB, HB, IN_VM, IN_VM],
        MOST,
    )
    rem_back = exchange(rem_send.reshape(shards, per, width), "user").reshape(slots, width)
    tiles = (shards, rows_all // peers * width // shards // 128, 128)
    (quot_tiles,) = call(total_kernel, [(tiles, bf16)], shared(split(at, keep, give, IN_VM)))
    rem_back, quot_tiles = lax.optimization_barrier((rem_back, quot_tiles))
    quot_back = exchange(quot_tiles, "user")
    keep, give = (
        call(
            functools.partial(collect_kernel, per=per, other=other),
            [((rows_own // 2, width), bf16 if other else f32)],
            (at, wanted, rem_back),
            [SM, VM, VM],
        )[0]
        for other in (False, True)
    )
    chunks = split(at, keep, give)
    (quot_tiles,) = call(repeat_kernel, [(tiles, bf16)], (quot_back,))
    quot_tiles, *_ = lax.optimization_barrier((quot_tiles, *chunks))
    quot_tiles = exchange(quot_tiles, "user")
    rem_sum = sum(c.astype(f32) for c in shared(chunks)).astype(bf16)
    rem_mine = along_chips(rem_sum)
    quot_tiles, _ = lax.optimization_barrier((quot_tiles, rem_sum))
    total = float(users * shards * block * peers)
    (rem_grad,) = place(at, wanted, [(rem_mine, rows_own, None)], width, per, total)
    quot_mine = along_chips(quot_tiles)
    rem_theirs = [to_core(c) for c in rem_mine]
    *quot_mine, rem_grad = lax.optimization_barrier((*quot_mine, rem_grad))
    quot_theirs = [to_core(c) for c in quot_mine]
    jobs = [(quot_mine, rows_all, None), (rem_theirs, rows_own, rem_grad)]
    quot_grad, rem_grad = place(at, wanted, jobs, width, per, total)
    (quot_grad,) = place(at, wanted, [(quot_theirs, rows_all, quot_grad)], width, per, total)
    return (output, quot_grad, rem_grad)


def solution(mesh):
    return jax.shard_map(
        body,
        mesh=mesh,
        in_specs=(
            P("user", "hist"),
            P("user", "hist"),
            P("user"),
            P("user", None, "hist"),
            P(),
            P("user", None),
            P(),
            P(),
            P(),
            P(),
            P("user", "hist", None),
        ),
        out_specs=(P("user", "hist", None), P(), P("user", None)),
        check_vma=False,
    )
```
